32 devices in a mesh: blk: 16 (over z, x, core), pair: 2 (over y).
Axes of the slice: x: 2, y: 2, z: 4, core: 2. Of those that a mesh axis runs over, the one named last changes fastest.
Arguments:
- mps: float32 [64, 32, 2048], P('pair', None, 'blk'), may hold values from -0.75 to 0.75
Outputs:
- kernel: float32 [32, 26], P(('blk', 'pair'))
The draws below stay inside these ranges and needn't reach their ends.
All inputs are finite; a program needn't handle non-finite values.
Results may differ from the reference program's by a relative error of at most 0.0002.
Values sent between devices are 32-bit elements; how exact they have to be, the bound alone decides.
No kernel may reach another device: no remote copies, remote signals or barrier semaphores. Data moves between devices by JAX's collectives and lax.ppermute only.
A program may use at most 64 MiB of HBM per device.

```python
import math
import jax
import jax.numpy as jnp
from jax import lax

SITES = 64
CHI = 32
PHYS = 2
SAMP = 2
BAND = 6
SAMPLES = 32
N_BLK = 16


def draw_mps(key, part):
    key = jax.random.fold_in(key, 7)
    key_base, key_noise, key_level = jax.random.split(key, 3)
    scale = (2.0 * CHI) ** (-0.5)
    level = jnp.exp(jax.random.uniform(key_level, (1, 1, SAMPLES, 1), jnp.float32, math.log(0.06), math.log(1.2)))
    spread = jnp.sqrt(level / SITES)
    base = jax.random.truncated_normal(key_base, -4.0, 4.0, (SITES, CHI, 1, PHYS * CHI), jnp.float32)
    noise = jax.random.truncated_normal(key_noise, -4.0, 4.0, (SITES, CHI, SAMPLES, PHYS * CHI), jnp.float32)
    return (scale * (base + spread * noise)).reshape(SITES, CHI, SAMPLES * PHYS * CHI)


def setup_inputs(seed: int = 0) -> dict:
    key_of = jax.random.split(jax.random.key(seed), 2)
    mps = draw_mps(jax.random.fold_in(key_of[1], 71), 0)
    return {"mps": mps}


def contract_all(left, right):
    start = jnp.zeros((N_BLK, SAMP, SAMP, CHI, CHI), jnp.float32).at[:, :, :, 0, 0].set(1.0)

    def advance(state, pieces):
        own_site, far_site = pieces
        inner = jnp.einsum("bnmxy,ybmpq->bnmxpq", state, far_site, precision=lax.Precision.HIGHEST)
        return jnp.einsum("xbnpz,bnmxpq->bnmzq", own_site, inner, precision=lax.Precision.HIGHEST), None

    final, _ = lax.scan(advance, start, (left, right))
    return final[:, :, :, 0, 0]


def reference(mps):
    shaped = mps.reshape(SITES, CHI, N_BLK, SAMP, PHYS, CHI)
    correlations = [contract_all(shaped, jnp.roll(shaped, offset, axis=2)) for offset in range(BAND + 1)]
    own_norm = jnp.diagonal(correlations[0], axis1=1, axis2=2)
    lower = [correlations[offset] for offset in range(BAND, 0, -1)]
    upper = [jnp.swapaxes(jnp.roll(correlations[offset], -offset, axis=0), 1, 2) for offset in range(1, BAND + 1)]
    tiles = jnp.stack(lower + [correlations[0]] + upper, axis=1)
    remote = jnp.stack([jnp.roll(own_norm, -offset, axis=0) for offset in range(-BAND, BAND + 1)], axis=1)
    kernel = tiles * tiles / (own_norm[:, None, :, None] * remote[:, :, None, :])
    return jnp.transpose(kernel, (0, 2, 1, 3)).reshape(SAMPLES, (2 * BAND + 1) * SAMP)
```

```python
import jax
import jax.numpy as jnp
from jax import lax
from jax.experimental import pallas as pl
from jax.experimental.pallas import tpu as pltpu
from jax.sharding import PartitionSpec as P

REACH = 6
MARKS = (0, 1, 4, 6)
HOME = 1
BF16, F32 = jnp.bfloat16, jnp.float32


def shifted(array, axis, by):
    peers = lax.axis_size(axis)
    return lax.ppermute(array, axis, [(i, (i + by) % peers) for i in range(peers)])


def split(x):
    high = x.astype(BF16)
    return high, (x - high.astype(F32)).astype(BF16)


def product(left, right, across):
    dims = (((1,), (1 if across else 0,)), ((), ()))
    return lax.dot_general(left, right, dims, preferred_element_type=F32)


def lane_slot(shape):
    return lax.broadcasted_iota(jnp.int32, shape, 1) // 32


def interleave(first, second):
    even = lane_slot(first.shape) % 2 == 0
    return (
        jnp.where(even, first, pltpu.roll(second, 32, 1)),
        jnp.where(even, pltpu.roll(first, 96, 1), second),
    )


def far_weights(tiles, flip):
    parts = []
    for half in zip(*[split(t) for t in tiles]):
        slot = lane_slot(half[0].shape)
        zero = jnp.zeros_like(half[0])
        placed = [[jnp.where(slot == k, h, zero) for h in half] for k in range(4)]
        if flip:
            parts.append(jnp.concatenate([placed[k][p] for p in range(2) for k in range(4)], 0))
        else:
            parts.append(jnp.concatenate([jnp.concatenate(placed[k], 1) for k in range(4)], 0))
    high, low = parts
    return jnp.concatenate([high, high], 1 if flip else 0), low


def near_turned(tiles):
    stack = jnp.concatenate([tiles[0], tiles[1], tiles[0], tiles[1]], 0).T
    return [stack[32 * k : 32 * k + 32] for k in range(4)]


def near_plain(tile):
    twice = pltpu.roll(tile, 64, 1)
    lower = lane_slot(tile.shape) < 2
    return [jnp.where(lower, tile, twice), jnp.where(lower, twice, tile)]


def near_operand(tile):
    high, low = split(tile)
    return jnp.concatenate([high, low], 1)


def spread(states, weights, flip):
    double, low = weights
    high, rest = split(states)
    return product(jnp.concatenate([high, rest], 1), double, flip) + product(high, low, flip)


def stacked(inner):
    h0, l0 = split(inner[:, :128])
    h1, l1 = split(inner[:, 128:])
    return jnp.concatenate([h0, h1, l0, l1] * 2, 0)


def site_step(wide, narrow, tiles, flip):
    t0, t1, t4, t6 = tiles
    low_pair, high_pair = interleave(t0, t1), interleave(t4, t6)
    if flip:
        near = near_plain(t0) + near_plain(t1) + near_plain(t4)
    else:
        turned, other = near_turned(low_pair), near_turned(high_pair)
        near = [turned[0], turned[2], turned[1], turned[3], other[0], other[2]]
    wide_inner = spread(wide, far_weights(high_pair, flip), flip)
    narrow_inner = spread(narrow, far_weights(low_pair, flip), flip)
    wide_out, narrow_out = [], []
    for k, tile in enumerate(near):
        rows = slice(32 * k, 32 * k + 32)
        operand = near_operand(tile)
        if k < 2:
            both = jnp.concatenate([stacked(wide_inner[rows]), stacked(narrow_inner[rows])], 1)
            result = product(operand, both, False)
            wide_out.append(result[:, :128])
            narrow_out.append(result[:, 128:])
        else:
            wide_out.append(product(operand, stacked(wide_inner[rows]), False))
    return jnp.concatenate(wide_out, 0), jnp.concatenate(narrow_out, 0)


def chain_kernel(core_ref, b0, b1, b4, b6, out):
    sites = b0.shape[0]
    row = lax.broadcasted_iota(jnp.int32, out.shape, 0) % 32
    lane = lax.broadcasted_iota(jnp.int32, out.shape, 1) % 32
    out[...] = jnp.where((row == 0) & (lane == 0), 1.0, 0.0)

    def run(flip):
        def step(index, carry):
            site = sites - 1 - index if flip else index
            return site_step(*carry, [b[site] for b in (b0, b1, b4, b6)], flip)

        wide, narrow = lax.fori_loop(0, sites, step, (out[:192], out[192:]), unroll=2)
        out[:192] = wide
        out[192:] = narrow

    @pl.when(core_ref[0] == 0)
    def _():
        run(False)

    @pl.when(core_ref[0] == 1)
    def _():
        run(True)


def meet_kernel(mine, theirs, out):
    pairs = (mine[...] * theirs[...]).reshape(8, 32, 128).sum(1)
    row = lax.broadcasted_iota(jnp.int32, (128, 128), 0) // 32
    lane = lax.broadcasted_iota(jnp.int32, (128, 128), 1)
    chosen = jnp.where(row == lane, 1.0, 0.0)
    out[...] = jnp.dot(pairs, chosen, precision=lax.Precision.HIGHEST, preferred_element_type=F32)


def tables(samp, band):
    at = {m: k for k, m in enumerate(MARKS)}

    def tile(low, high, near, far):
        if (low, high) in ((0, 0), (0, 1)):
            return 6 + near, (0 if high == 0 else 1) + 2 * far
        return 2 * at[low] + near, (0 if high == 4 else 1) + 2 * far

    which = {}
    for low in MARKS:
        for high in MARKS:
            if low < high:
                which[high - low] = (low, high)
    which[0] = (0, 0)
    rows = []
    for n in range(samp):
        entries = []
        for o in range(-band, band + 1):
            low, high = which[abs(o)]
            for m in range(samp):
                if o >= 0:
                    entries.append((MARKS[HOME] - low, *tile(low, high, n, m)))
                else:
                    entries.append((MARKS[HOME] - high, *tile(low, high, m, n)))
        norms = [(o + MARKS[HOME], *tile(0, 0, m, m)) for o in range(-band, band + 1) for m in range(samp)]
        rows.append(entries + norms + [(MARKS[HOME], *tile(0, 0, n, n))])
    return rows


def body(mps):
    chi = mps.shape[1]
    samp = mps.shape[2] // (2 * chi)
    blocks = lax.axis_size("blk")
    band = min(REACH, (blocks - 1) // 2)
    core = lax.axis_index("pair")
    home = MARKS[HOME]
    held = [mps if m == home else shifted(mps, "blk", home - m) for m in MARKS]
    vmem = pl.BlockSpec(memory_space=pltpu.VMEM)
    states = pl.pallas_call(
        chain_kernel,
        out_shape=jax.ShapeDtypeStruct((256, 128), F32),
        in_specs=[pl.BlockSpec(memory_space=pltpu.SMEM)] + [vmem] * 4,
        out_specs=vmem,
        compiler_params=pltpu.CompilerParams(vmem_limit_bytes=32 * 2**20),
        name="half_chains",
    )(core[None].astype(jnp.int32), *held)
    partner = lax.ppermute(states, "pair", [(0, 1), (1, 0)])
    correlations = pl.pallas_call(
        meet_kernel,
        out_shape=jax.ShapeDtypeStruct((8, 128), F32),
        in_specs=[vmem] * 2,
        out_specs=vmem,
        name="meet",
    )(states, partner)[:, :4]
    everywhere = lax.all_gather(correlations.reshape(32), "blk")
    spots = jnp.asarray(tables(samp, band), jnp.int32)[core]
    source = (lax.axis_index("blk") + spots[:, 0]) % blocks
    values = everywhere.reshape(-1)[source * 32 + spots[:, 1] * 4 + spots[:, 2]]
    width = (2 * band + 1) * samp
    tile, remote, own = values[:width], values[width : 2 * width], values[2 * width]
    return (tile * tile / (own * remote))[None]


def solution(mesh):
    in_specs = (P("pair", None, "blk"),)
    out_specs = P(("blk", "pair"), None)
    return jax.shard_map(body, mesh=mesh, in_specs=in_specs, out_specs=out_specs, check_vma=False)
```

```python
import functools

import jax
import jax.numpy as jnp
from jax import lax
from jax.experimental import pallas as pl
from jax.experimental.pallas import tpu as pltpu
from jax.sharding import PartitionSpec as P

REACH = 6
CHUNKS = (12, 12, 8)
BF16, F32 = jnp.bfloat16, jnp.float32
VMEM = pl.BlockSpec(memory_space=pltpu.VMEM)
SMEM = pl.BlockSpec(memory_space=pltpu.SMEM)


def move(array, source):
    peers = lax.axis_size("blk")
    chips = peers // 2
    pairs = []
    for d in range(peers):
        chip, core = source(d // 2, d % 2)
        pairs.append(((chip % chips) * 2 + core, d))
    return lax.ppermute(array, "blk", pairs)


def split(x):
    high = x.astype(BF16)
    return high, (x - high.astype(F32)).astype(BF16)


def product(left, right, across=False):
    dims = (((1,), (1 if across else 0,)), ((), ()))
    return lax.dot_general(left, right, dims, preferred_element_type=F32)


def lane_slot(shape):
    return lax.broadcasted_iota(jnp.int32, shape, 1) // 32


def interleave(first, second):
    even = lane_slot(first.shape) % 2 == 0
    return (
        jnp.where(even, first, pltpu.roll(second, 32, 1)),
        jnp.where(even, pltpu.roll(first, 96, 1), second),
    )


def far_weights(tiles, flip):
    parts = []
    for half in zip(*[split(t) for t in tiles]):
        slot = lane_slot(half[0].shape)
        zero = jnp.zeros_like(half[0])
        placed = [[jnp.where(slot == k, h, zero) for h in half] for k in range(4)]
        if flip:
            parts.append(jnp.concatenate([placed[k][p] for p in range(2) for k in range(4)], 0))
        else:
            parts.append(jnp.concatenate([jnp.concatenate(placed[k], 1) for k in range(4)], 0))
    high, low = parts
    return jnp.concatenate([high, high], 1 if flip else 0), low


def near_turned(tiles):
    stack = jnp.concatenate([tiles[0], tiles[1], tiles[0], tiles[1]], 0).T
    return [stack[32 * k : 32 * k + 32] for k in (0, 2, 1, 3)]


def near_plain(tile):
    twice = pltpu.roll(tile, 64, 1)
    lower = lane_slot(tile.shape) < 2
    return [jnp.where(lower, tile, twice), jnp.where(lower, twice, tile)]


def advance(state, near, far, flip):
    double, low = far_weights(far, flip)
    high, rest = split(state)
    inner = product(jnp.concatenate([high, rest], 1), double, flip) + product(high, low, flip)
    h0, l0 = split(inner[:, :128])
    h1, l1 = split(inner[:, 128:])
    results = []
    for k, tile in enumerate(near):
        rows = slice(32 * k, 32 * k + 32)
        weights = jnp.concatenate([h0[rows], h1[rows], l0[rows], l1[rows]], 0)
        both = product(jnp.concatenate(split(tile), 0), weights)
        results.append(both[:32] + both[32:])
    return jnp.concatenate(results, 0)


def corner(shape):
    row = lax.broadcasted_iota(jnp.int32, shape, 0) % 32
    lane = lax.broadcasted_iota(jnp.int32, shape, 1) % 32
    return jnp.where((row == 0) & (lane == 0), 1.0, 0.0)


def on_each_side(side_ref, run):
    for side in range(2):
        pl.when(side_ref[0] == side)(functools.partial(run, side == 1))


def wide_kernel(start, side_ref, own, sibling, first, second, other, *rest):
    out = rest[-1]
    sites, count = own.shape[0], first.shape[0]

    def run(flip):
        def step(index, state):
            whole = sites - 1 - start - index if flip else start + index
            part = count - 1 - index if flip else index
            far = interleave(first[part], second[part])
            if flip:
                near = [n for t in (own[whole], sibling[whole], other[part], first[part], second[part])
                        for n in near_plain(t)]
            else:
                extra = other[part]
                near = (
                    near_turned(interleave(own[whole], sibling[whole]))
                    + near_turned(interleave(extra, extra))[:2]
                    + near_turned(far)
                )
            return advance(state, near, far, flip)

        begin = corner(out.shape) if start == 0 else rest[0][...]
        out[...] = lax.fori_loop(0, count, step, begin, unroll=2)

    on_each_side(side_ref, run)


def narrow_kernel(side_ref, own, sibling, out):
    sites = own.shape[0]

    def run(flip):
        def step(index, state):
            site = sites - 1 - index if flip else index
            far = interleave(own[site], sibling[site])
            near = near_plain(own[site]) if flip else near_turned(far)[:2]
            return advance(state, near, far, flip)

        out[...] = lax.fori_loop(0, sites, step, corner(out.shape), unroll=4)

    on_each_side(side_ref, run)


def meet_kernel(wide, narrow, far_wide, far_narrow, out):
    units = [
        jnp.sum((a[...] * b[...]).reshape(-1, 32, 128), 1)
        for a, b in ((wide, far_wide), (narrow, far_narrow))
    ]
    units = jnp.concatenate(units + [jnp.zeros((4, 128), F32)], 0)
    row = lax.broadcasted_iota(jnp.int32, (8, 128), 0)
    chosen = jnp.where(row == lane_slot((8, 128)), 1.0, 0.0)
    found = lax.dot_general(
        chosen, units, (((1,), (1,)), ((), ())), precision=lax.Precision.HIGHEST, preferred_element_type=F32
    )
    out[...] = jnp.concatenate([found, jnp.zeros((8, 112), F32)], 1)


def pick_kernel(spot_ref, *refs):
    *tiles, out = refs
    joined = tiles[0][...]
    for k, tile in enumerate(tiles[1:], 1):
        joined += pltpu.roll(tile[...], 16 * k, 1)
    unit = lax.broadcasted_iota(jnp.int32, (128, 128), 0)
    slot = lax.broadcasted_iota(jnp.int32, (8, 128), 0)
    values = []
    for k in range(3):
        spot = spot_ref[pl.ds(k, 1), :]
        chosen = jnp.where(unit == spot // 8, 1.0, 0.0)
        found = jnp.dot(joined, chosen, precision=lax.Precision.HIGHEST, preferred_element_type=F32)
        values.append(jnp.sum(jnp.where(slot == spot % 8, found, 0.0), 0, keepdims=True))
    tile, remote, own = values
    width = out.shape[1]
    out[...] = (tile * tile / (own * remote))[:, :width]


def rosters(core):
    mine, theirs = ("A0", "A1"), ("Z1", "Z0")
    if core == 1:
        mine, theirs = theirs, mine
    own, sibling = f"O{core}", f"O{1 - core}"
    wide = [own, sibling, theirs[1], mine[0], mine[1]]
    return (wide, mine), ([own], (own, sibling))


def find(core, near, far):
    base = 0
    for rows, lanes in rosters(core):
        for a in range(2):
            for left, right in ((near, far), (far, near)):
                if left in rows and right in lanes:
                    unit, slot = base + 2 * rows.index(left), lanes.index(right)
                    if left == near:
                        return lambda n, m: (unit + n, slot + 2 * m)
                    return lambda n, m: (unit + m, slot + 2 * n)
        base += 2 * len(rows)
    return None


def spot_table(core, samp, band):
    views = [(role, (k, k + 1) if core == 0 else (k + 1, k)) for k, role in ((0, "O"), (2, "A"), (4, "Z"))]
    shift = {"O": 0, "A": -1, "Z": 2}

    def place(offset):
        goal = core + offset
        chip, lane = goal // 2, goal % 2
        for role, messages in views:
            for name, gap in shift.items():
                if gap - shift[role] == chip:
                    for k, message in enumerate(messages):
                        got = find(k, f"{role}{core}", f"{name}{lane}")
                        if got:
                            return message, got
        raise ValueError(offset)

    def norm(offset):
        goal = core + offset
        chip, lane = goal // 2, goal % 2
        for role, messages in views:
            for name, gap in shift.items():
                if gap - shift[role] == chip:
                    for k, message in enumerate(messages):
                        got = find(k, f"{name}{lane}", f"{name}{lane}")
                        if got:
                            return message, got
        raise ValueError(offset)

    def code(where, n, m):
        message, got = where
        unit, slot = got(n, m)
        return 8 * (16 * message + unit) + slot

    offsets = range(-band, band + 1)
    table = []
    for n in range(samp):
        tile = [code(place(o), n, m) for o in offsets for m in range(samp)]
        remote = [code(norm(o), m, m) for o in offsets for m in range(samp)]
        own = [code(norm(0), n, n)] * len(tile)
        rows = [r + r[:1] * (128 - len(r)) for r in (tile, remote, own)]
        table.append(rows + rows[:1] * 5)
    return table


def call(kernel, shape, *args, name):
    return pl.pallas_call(
        kernel,
        out_shape=jax.ShapeDtypeStruct(shape, F32),
        in_specs=[SMEM if a.ndim == 1 else VMEM for a in args],
        out_specs=VMEM,
        compiler_params=pltpu.CompilerParams(vmem_limit_bytes=40 * 2**20),
        name=name,
    )(*args)


def body(mps):
    sites, chi = mps.shape[:2]
    samp = mps.shape[2] // (2 * chi)
    blocks = lax.axis_size("blk")
    band = min(REACH, (blocks - 1) // 2)
    side = lax.axis_index("pair")
    flag = side[None].astype(jnp.int32)

    starts = [sum(CHUNKS[:k]) for k in range(len(CHUNKS))]
    firsts, seconds = [], []
    for start, count in zip(starts, CHUNKS):
        piece = lax.dynamic_slice_in_dim(mps, jnp.where(side == 0, start, sites - start - count), count, 0)
        seconds.append(move(piece, lambda chip, core: (chip - 1, 1) if core == 0 else (chip + 2, 0)))
        firsts.append(move(piece, lambda chip, core: (chip - 1, 0) if core == 0 else (chip + 2, 1)))
    across = lambda chip, core: (chip, 1 - core)
    sibling = move(mps, across)
    narrow = call(narrow_kernel, (64, 128), flag, mps, sibling, name="own_chains")
    swap = [(0, 1), (1, 0)]
    far_narrow = lax.ppermute(narrow, "pair", swap)
    wide = ()
    for start, first, second in zip(starts, firsts, seconds):
        other = move(second, across)
        wide = (
            call(functools.partial(wide_kernel, start), (320, 128), flag, mps, sibling, first, second, other,
                 *wide, name="half_chains"),
        )
    (wide,) = wide
    far_wide = lax.ppermute(wide, "pair", swap)
    tile = call(meet_kernel, (8, 128), wide, narrow, far_wide, far_narrow, name="meet")
    tiles = [tile, move(tile, across)]
    for gap in (1, -2):
        straight = move(tile, lambda chip, core: (chip + gap, core))
        crossed = move(tile, lambda chip, core: (chip + gap, 1 - core))
        tiles += [straight, crossed]
    spots = jnp.asarray([spot_table(core, samp, band) for core in range(2)], jnp.int32)
    spot = spots[lax.axis_index("blk") % 2, side]
    return call(pick_kernel, (1, (2 * band + 1) * samp), spot, *tiles, name="pick")


def solution(mesh):
    in_specs = (P("pair", None, "blk"),)
    out_specs = P(("blk", "pair"), None)
    return jax.shard_map(body, mesh=mesh, in_specs=in_specs, out_specs=out_specs, check_vma=False)
```

```python
import functools

import jax
import jax.numpy as jnp
from jax import lax
from jax.experimental import pallas as pl
from jax.experimental.pallas import tpu as pltpu
from jax.sharding import PartitionSpec as P

REACH = 6
CHUNKS = (12, 12, 8)
BF16, F32 = jnp.bfloat16, jnp.float32
VMEM = pl.BlockSpec(memory_space=pltpu.VMEM)
SMEM = pl.BlockSpec(memory_space=pltpu.SMEM)


def move(array, source):
    peers = lax.axis_size("blk")
    chips = peers // 2
    pairs = []
    for d in range(peers):
        chip, core = source(d // 2, d % 2)
        pairs.append(((chip % chips) * 2 + core, d))
    return lax.ppermute(array, "blk", pairs)


def split(x):
    high = x.astype(BF16)
    return high, (x - high.astype(F32)).astype(BF16)


def product(left, right, across=False):
    dims = (((1,), (1 if across else 0,)), ((), ()))
    return lax.dot_general(left, right, dims, preferred_element_type=F32)


def lane_slot(shape):
    return lax.broadcasted_iota(jnp.int32, shape, 1) // 32


def interleave(first, second):
    even = lane_slot(first.shape) % 2 == 0
    return (
        jnp.where(even, first, pltpu.roll(second, 32, 1)),
        jnp.where(even, pltpu.roll(first, 96, 1), second),
    )


def far_weights(tiles, flip):
    parts = []
    for half in zip(*[split(t) for t in tiles]):
        slot = lane_slot(half[0].shape)
        zero = jnp.zeros_like(half[0])
        placed = [[jnp.where(slot == k, h, zero) for h in half] for k in range(4)]
        if flip:
            parts.append(jnp.concatenate([placed[k][p] for p in range(2) for k in range(4)], 0))
        else:
            parts.append(jnp.concatenate([jnp.concatenate(placed[k], 1) for k in range(4)], 0))
    high, low = parts
    return jnp.concatenate([high, high], 1 if flip else 0), low


def near_turned(tiles):
    stack = jnp.concatenate([tiles[0], tiles[1], tiles[0], tiles[1]], 0).T
    return [stack[32 * k : 32 * k + 32] for k in (0, 2, 1, 3)]


def near_plain(tile):
    twice = pltpu.roll(tile, 64, 1)
    lower = lane_slot(tile.shape) < 2
    return [jnp.where(lower, tile, twice), jnp.where(lower, twice, tile)]


def advance(state, near, far, flip):
    double, low = far
    high, rest = split(state)
    inner = product(jnp.concatenate([high, rest], 1), double, flip) + product(high, low, flip)
    h0, l0 = split(inner[:, :128])
    h1, l1 = split(inner[:, 128:])
    results = []
    for k, tile in enumerate(near):
        rows = slice(32 * k, 32 * k + 32)
        weights = jnp.concatenate([h0[rows], h1[rows], l0[rows], l1[rows]], 0)
        both = product(jnp.concatenate(split(tile), 0), weights)
        results.append(both[:32] + both[32:])
    return jnp.concatenate(results, 0)


def corner(shape):
    row = lax.broadcasted_iota(jnp.int32, shape, 0) % 32
    lane = lax.broadcasted_iota(jnp.int32, shape, 1) % 32
    return jnp.where((row == 0) & (lane == 0), 1.0, 0.0)


def on_each_side(side_ref, run):
    for side in range(2):
        pl.when(side_ref[0] == side)(functools.partial(run, side == 1))


def norms_only(state):
    slot = lane_slot((32, 128))
    first = jnp.where(slot == 0, state[192:224], state[224:256])
    second = jnp.where(slot == 1, state[256:288], state[288:320])
    kept = jnp.where(slot % 2 == 0, first, second)
    return jnp.concatenate([state[:192], kept, state[320:]], 0)


def chain_kernel(start, side_ref, own, sibling, first, second, other, *rest):
    out = rest[-1]
    sites, count = own.shape[0], first.shape[0]

    def run(flip):
        state = corner((384, 128)) if start == 0 else rest[0][...]
        for index in range(count):
            whole = sites - 1 - start - index if flip else start + index
            part = count - 1 - index if flip else index
            home = interleave(own[whole], sibling[whole])
            far = interleave(first[part], second[part])
            if flip:
                near = [n for t in (own[whole], sibling[whole], other[part], first[part], second[part])
                        for n in near_plain(t)]
            else:
                extra = other[part]
                near = near_turned(home) + near_turned(interleave(extra, extra))[:2] + near_turned(far)
            weights = far_weights(far, flip)
            parts = [
                advance(state[:192], near[:6], weights, flip),
                advance(state[192:320], near[6:], weights, flip),
                advance(state[320:], near[:2], far_weights(home, flip), flip),
            ]
            state = jnp.concatenate(parts, 0)
        out[...] = norms_only(state) if start + count == sites else state

    on_each_side(side_ref, run)


def meet_kernel(mine, theirs, out):
    units = jnp.sum((mine[...] * theirs[...]).reshape(-1, 32, 128), 1)
    units = jnp.concatenate([units, jnp.zeros((16 - units.shape[0], 128), F32)], 0)
    row = lax.broadcasted_iota(jnp.int32, (8, 128), 0)
    chosen = jnp.where(row == lane_slot((8, 128)), 1.0, 0.0)
    found = lax.dot_general(
        chosen, units, (((1,), (1,)), ((), ())), precision=lax.Precision.HIGHEST, preferred_element_type=F32
    )
    out[...] = jnp.concatenate([found, jnp.zeros((8, 112), F32)], 1)


def pick_kernel(spot_ref, *refs):
    *tiles, out = refs
    joined = tiles[0][...]
    for k, tile in enumerate(tiles[1:], 1):
        joined += pltpu.roll(tile[...], 16 * k, 1)
    unit = lax.broadcasted_iota(jnp.int32, (128, 128), 0)
    slot = lax.broadcasted_iota(jnp.int32, (8, 128), 0)
    values = []
    for k in range(3):
        spot = spot_ref[pl.ds(k, 1), :]
        chosen = jnp.where(unit == spot // 8, 1.0, 0.0)
        found = jnp.dot(joined, chosen, precision=lax.Precision.HIGHEST, preferred_element_type=F32)
        values.append(jnp.sum(jnp.where(slot == spot % 8, found, 0.0), 0, keepdims=True))
    tile, remote, own = values
    width = out.shape[1]
    out[...] = (tile * tile / (own * remote))[:, :width]


def find(core, near, far):
    mine, theirs = ("A0", "A1"), ("Z1", "Z0")
    if core == 1:
        mine, theirs = theirs, mine
    own, sibling = f"O{core}", f"O{1 - core}"
    if near == far and near in mine:
        return lambda n, m: (6, mine.index(near) + 2 * m)
    for base, rows, lanes in ((0, (own, sibling, theirs[1]), mine), (7, (own,), (own, sibling))):
        if near in rows and far in lanes:
            return lambda n, m: (base + 2 * rows.index(near) + n, lanes.index(far) + 2 * m)
        if far in rows and near in lanes:
            return lambda n, m: (base + 2 * rows.index(far) + m, lanes.index(near) + 2 * n)
    return None


def spot_table(core, samp, band):
    views = [(role, (k, k + 1) if core == 0 else (k + 1, k)) for k, role in ((0, "O"), (2, "A"), (4, "Z"))]
    shift = {"O": 0, "A": -1, "Z": 2}

    def place(offset, alone=False):
        chip, lane = (core + offset) // 2, (core + offset) % 2
        for role, messages in views:
            for name, gap in shift.items():
                if gap - shift[role] == chip:
                    goal = f"{name}{lane}"
                    for k, message in enumerate(messages):
                        got = find(k, goal if alone else f"{role}{core}", goal)
                        if got:
                            return message, got
        raise ValueError(offset)

    def code(where, n, m):
        message, got = where
        unit, slot = got(n, m)
        return 8 * (16 * message + unit) + slot

    offsets = range(-band, band + 1)
    table = []
    for n in range(samp):
        tile = [code(place(o), n, m) for o in offsets for m in range(samp)]
        remote = [code(place(o, True), m, m) for o in offsets for m in range(samp)]
        own = [code(place(0, True), n, n)] * len(tile)
        rows = [r + r[:1] * (128 - len(r)) for r in (tile, remote, own)]
        table.append(rows + rows[:1] * 5)
    return table


def call(kernel, shape, *args, name):
    return pl.pallas_call(
        kernel,
        out_shape=jax.ShapeDtypeStruct(shape, F32),
        in_specs=[SMEM if a.ndim == 1 else VMEM for a in args],
        out_specs=VMEM,
        compiler_params=pltpu.CompilerParams(vmem_limit_bytes=40 * 2**20),
        name=name,
    )(*args)


def body(mps):
    sites, chi = mps.shape[:2]
    samp = mps.shape[2] // (2 * chi)
    blocks = lax.axis_size("blk")
    band = min(REACH, (blocks - 1) // 2)
    side = lax.axis_index("pair")
    flag = side[None].astype(jnp.int32)

    starts = [sum(CHUNKS[:k]) for k in range(len(CHUNKS))]
    firsts, seconds = [], []
    for start, count in zip(starts, CHUNKS):
        piece = lax.dynamic_slice_in_dim(mps, jnp.where(side == 0, start, sites - start - count), count, 0)
        seconds.append(move(piece, lambda chip, core: (chip - 1, 1) if core == 0 else (chip + 2, 0)))
        firsts.append(move(piece, lambda chip, core: (chip - 1, 0) if core == 0 else (chip + 2, 1)))
    across = lambda chip, core: (chip, 1 - core)
    sibling = move(mps, across)
    state = ()
    for start, first, second in zip(starts, firsts, seconds):
        if state:
            second, *state = lax.optimization_barrier((second, *state))
        other = move(second, across)
        last = start == starts[-1]
        state = (
            call(functools.partial(chain_kernel, start), (288 if last else 384, 128), flag, mps, sibling, first,
                 second, other, *state, name="half_chains"),
        )
    (state,) = state
    partner = lax.ppermute(state, "pair", [(0, 1), (1, 0)])
    tile = call(meet_kernel, (8, 128), state, partner, name="meet")
    tiles = [tile, move(tile, across)]
    for gap in (1, -2):
        straight = move(tile, lambda chip, core: (chip + gap, core))
        crossed = move(tile, lambda chip, core: (chip + gap, 1 - core))
        tiles += [straight, crossed]
    spots = jnp.asarray([spot_table(core, samp, band) for core in range(2)], jnp.int32)
    spot = spots[lax.axis_index("blk") % 2, side]
    return call(pick_kernel, (1, (2 * band + 1) * samp), spot, *tiles, name="pick")


def solution(mesh):
    in_specs = (P("pair", None, "blk"),)
    out_specs = P(("blk", "pair"), None)
    return jax.shard_map(body, mesh=mesh, in_specs=in_specs, out_specs=out_specs, check_vma=False)
```

```python
import functools

import jax
import jax.numpy as jnp
from jax import lax
from jax.experimental import pallas as pl
from jax.experimental.pallas import tpu as pltpu
from jax.sharding import PartitionSpec as P

REACH = 6
CHUNKS = (18, 14)
BF16, F32 = jnp.bfloat16, jnp.float32
VMEM = pl.BlockSpec(memory_space=pltpu.VMEM)
SMEM = pl.BlockSpec(memory_space=pltpu.SMEM)


def move(array, source):
    peers = lax.axis_size("blk")
    chips = peers // 2
    pairs = []
    for d in range(peers):
        chip, core = source(d // 2, d % 2)
        pairs.append(((chip % chips) * 2 + core, d))
    return lax.ppermute(array, "blk", pairs)


def split(x):
    high = x.astype(BF16)
    return high, (x - high.astype(F32)).astype(BF16)


def product(left, right):
    return jnp.dot(left, right, preferred_element_type=F32)


def lane_slot(shape):
    return lax.broadcasted_iota(jnp.int32, shape, 1) // 32


def interleave(first, second):
    even = lane_slot(first.shape) % 2 == 0
    return (
        jnp.where(even, first, pltpu.roll(second, 32, 1)),
        jnp.where(even, pltpu.roll(first, 96, 1), second),
    )


def far_weights(tiles, flip):
    if flip:
        tiles = [jnp.concatenate([t] * 4, 0).T for t in tiles]
        blocks = [[t[32 * k : 32 * k + 32] for t in tiles] for k in range(4)]
    else:
        blocks = [tiles] * 4
    slot = lane_slot((32, 128))
    rows = [jnp.concatenate([jnp.where(slot == k, t, 0.0) for t in blocks[k]], 1) for k in range(4)]
    high, low = split(jnp.concatenate(rows, 0))
    return jnp.concatenate([high, high], 0), low


def near_turned(tiles):
    stack = jnp.concatenate([tiles[0], tiles[1], tiles[0], tiles[1]], 0).T
    return [stack[32 * k : 32 * k + 32] for k in (0, 2, 1, 3)]


def near_plain(tile):
    twice = pltpu.roll(tile, 64, 1)
    lower = lane_slot(tile.shape) < 2
    return [jnp.where(lower, tile, twice), jnp.where(lower, twice, tile)]


def advance(state, near, far):
    double, low = far
    high, rest = split(state)
    inner = product(jnp.concatenate([high, rest], 1), double) + product(high, low)
    h0, l0 = split(inner[:, :128])
    h1, l1 = split(inner[:, 128:])
    results = []
    for k, tile in enumerate(near):
        rows = slice(32 * k, 32 * k + 32)
        weights = jnp.concatenate([h0[rows], h1[rows], l0[rows], l1[rows]], 0)
        both = product(jnp.concatenate(split(tile), 0), weights)
        results.append(both[:32] + both[32:])
    return jnp.concatenate(results, 0)


def corner(shape):
    row = lax.broadcasted_iota(jnp.int32, shape, 0) % 32
    lane = lax.broadcasted_iota(jnp.int32, shape, 1) % 32
    return jnp.where((row == 0) & (lane == 0), 1.0, 0.0)


def on_each_side(side_ref, run):
    for side in range(2):
        pl.when(side_ref[0] == side)(functools.partial(run, side == 1))


def norms_only(state):
    slot = lane_slot((32, 128))
    first = jnp.where(slot == 0, state[192:224], state[224:256])
    second = jnp.where(slot == 1, state[256:288], state[288:320])
    kept = jnp.where(slot % 2 == 0, first, second)
    return jnp.concatenate([state[:192], kept], 0)


def home_step(state, home, near, flip):
    return advance(state, near[:2], far_weights(home, flip))


def home_kernel(count, side_ref, own, sibling, out):
    sites = own.shape[0]

    def run(flip):
        state = corner((64, 128))
        for index in range(count):
            site = sites - 1 - index if flip else index
            home = interleave(own[site], sibling[site])
            state = home_step(state, home, near_plain(own[site]) if flip else near_turned(home), flip)
        out[...] = state

    on_each_side(side_ref, run)


def chain_kernel(start, side_ref, own, sibling, first, second, other, *rest):
    out = rest[-1]
    sites, count = own.shape[0], first.shape[0]
    last = start + count == sites

    def run(flip):
        state = rest[1][...] if start else corner((320, 128))
        inner = rest[0][...] if last else None
        for index in range(count):
            whole = sites - 1 - start - index if flip else start + index
            part = count - 1 - index if flip else index
            home = interleave(own[whole], sibling[whole])
            far = interleave(first[part], second[part])
            if flip:
                near = [n for t in (own[whole], sibling[whole], other[part], first[part], second[part])
                        for n in near_plain(t)]
            else:
                extra = other[part]
                near = near_turned(home) + near_turned(interleave(extra, extra))[:2] + near_turned(far)
            weights = far_weights(far, flip)
            parts = [advance(state[:192], near[:6], weights), advance(state[192:], near[6:], weights)]
            state = jnp.concatenate(parts, 0)
            if last:
                inner = home_step(inner, home, near, flip)
        out[...] = jnp.concatenate([norms_only(state), inner], 0) if last else state

    on_each_side(side_ref, run)


def meet_kernel(mine, theirs, out):
    units = jnp.sum((mine[...] * theirs[...]).reshape(-1, 32, 128), 1)
    units = jnp.concatenate([units, jnp.zeros((16 - units.shape[0], 128), F32)], 0)
    row = lax.broadcasted_iota(jnp.int32, (8, 128), 0)
    chosen = jnp.where(row == lane_slot((8, 128)), 1.0, 0.0)
    found = lax.dot_general(
        chosen, units, (((1,), (1,)), ((), ())), precision=lax.Precision.HIGHEST, preferred_element_type=F32
    )
    out[...] = jnp.concatenate([found, jnp.zeros((8, 112), F32)], 1)


def pick_kernel(spot_ref, *refs):
    *tiles, out = refs
    joined = tiles[0][...]
    for k, tile in enumerate(tiles[1:], 1):
        joined += pltpu.roll(tile[...], 16 * k, 1)
    unit = lax.broadcasted_iota(jnp.int32, (128, 128), 0)
    slot = lax.broadcasted_iota(jnp.int32, (8, 128), 0)
    values = []
    for k in range(3):
        spot = spot_ref[pl.ds(k, 1), :]
        chosen = jnp.where(unit == spot // 8, 1.0, 0.0)
        found = jnp.dot(joined, chosen, precision=lax.Precision.HIGHEST, preferred_element_type=F32)
        values.append(jnp.sum(jnp.where(slot == spot % 8, found, 0.0), 0, keepdims=True))
    tile, remote, own = values
    width = out.shape[1]
    out[...] = (tile * tile / (own * remote))[:, :width]


def find(core, near, far):
    mine, theirs = ("A0", "A1"), ("Z1", "Z0")
    if core == 1:
        mine, theirs = theirs, mine
    own, sibling = f"O{core}", f"O{1 - core}"
    if near == far and near in mine:
        return lambda n, m: (6, mine.index(near) + 2 * m)
    for base, rows, lanes in ((0, (own, sibling, theirs[1]), mine), (7, (own,), (own, sibling))):
        if near in rows and far in lanes:
            return lambda n, m: (base + 2 * rows.index(near) + n, lanes.index(far) + 2 * m)
        if far in rows and near in lanes:
            return lambda n, m: (base + 2 * rows.index(far) + m, lanes.index(near) + 2 * n)
    return None


def spot_table(core, samp, band):
    views = [(role, (k, k + 1) if core == 0 else (k + 1, k)) for k, role in ((0, "O"), (2, "A"), (4, "Z"))]
    shift = {"O": 0, "A": -1, "Z": 2}

    def place(offset, alone=False):
        chip, lane = (core + offset) // 2, (core + offset) % 2
        for role, messages in views:
            for name, gap in shift.items():
                if gap - shift[role] == chip:
                    goal = f"{name}{lane}"
                    for k, message in enumerate(messages):
                        got = find(k, goal if alone else f"{role}{core}", goal)
                        if got:
                            return message, got
        raise ValueError(offset)

    def code(where, n, m):
        message, got = where
        unit, slot = got(n, m)
        return 8 * (16 * message + unit) + slot

    offsets = range(-band, band + 1)
    table = []
    for n in range(samp):
        tile = [code(place(o), n, m) for o in offsets for m in range(samp)]
        remote = [code(place(o, True), m, m) for o in offsets for m in range(samp)]
        own = [code(place(0, True), n, n)] * len(tile)
        rows = [r + r[:1] * (128 - len(r)) for r in (tile, remote, own)]
        table.append(rows + rows[:1] * 5)
    return table


def call(kernel, shape, *args, name):
    return pl.pallas_call(
        kernel,
        out_shape=jax.ShapeDtypeStruct(shape, F32),
        in_specs=[SMEM if a.ndim == 1 else VMEM for a in args],
        out_specs=VMEM,
        compiler_params=pltpu.CompilerParams(vmem_limit_bytes=40 * 2**20),
        name=name,
    )(*args)


def body(mps):
    sites, chi = mps.shape[:2]
    samp = mps.shape[2] // (2 * chi)
    blocks = lax.axis_size("blk")
    band = min(REACH, (blocks - 1) // 2)
    side = lax.axis_index("pair")
    flag = side[None].astype(jnp.int32)

    starts = [sum(CHUNKS[:k]) for k in range(len(CHUNKS))]
    pieces = [
        lax.dynamic_slice_in_dim(mps, jnp.where(side == 0, start, sites - start - count), count, 0)
        for start, count in zip(starts, CHUNKS)
    ]
    pieces = lax.optimization_barrier(pieces)
    seconds = [move(p, lambda chip, core: (chip - 1, 1) if core == 0 else (chip + 2, 0)) for p in pieces]
    firsts = [move(p, lambda chip, core: (chip - 1, 0) if core == 0 else (chip + 2, 1)) for p in pieces]
    across = lambda chip, core: (chip, 1 - core)
    sibling = move(mps, across)
    inner = call(functools.partial(home_kernel, starts[-1]), (64, 128), flag, mps, sibling, name="own_chains")
    carried = (inner,)
    for start, first, second in zip(starts, firsts, seconds):
        second, *carried = lax.optimization_barrier((second, *carried))
        other = move(second, across)
        rows = 288 if start == starts[-1] else 320
        state = call(functools.partial(chain_kernel, start), (rows, 128), flag, mps, sibling, first, second, other,
                     *carried, name="half_chains")
        carried = (carried[0], state)
    partner = lax.ppermute(state, "pair", [(0, 1), (1, 0)])
    tile = call(meet_kernel, (8, 128), state, partner, name="meet")
    tiles = [tile, move(tile, across)]
    for gap in (1, -2):
        straight = move(tile, lambda chip, core: (chip + gap, core))
        crossed = move(tile, lambda chip, core: (chip + gap, 1 - core))
        tiles += [straight, crossed]
    spots = jnp.asarray([spot_table(core, samp, band) for core in range(2)], jnp.int32)
    spot = spots[lax.axis_index("blk") % 2, side]
    return call(pick_kernel, (1, (2 * band + 1) * samp), spot, *tiles, name="pick")


def solution(mesh):
    in_specs = (P("pair", None, "blk"),)
    out_specs = P(("blk", "pair"), None)
    return jax.shard_map(body, mesh=mesh, in_specs=in_specs, out_specs=out_specs, check_vma=False)
```

```python
import functools

import jax
import jax.numpy as jnp
from jax import lax
from jax.experimental import pallas as pl
from jax.experimental.pallas import tpu as pltpu
from jax.sharding import PartitionSpec as P

REACH = 6
EDGE = 6
SHARE = 0.63
BF16, F32 = jnp.bfloat16, jnp.float32
VMEM = pl.BlockSpec(memory_space=pltpu.VMEM)
SMEM = pl.BlockSpec(memory_space=pltpu.SMEM)


def move(array, source):
    peers = lax.axis_size("blk")
    chips = peers // 2
    pairs = []
    for d in range(peers):
        chip, core = source(d // 2, d % 2)
        pairs.append(((chip % chips) * 2 + core, d))
    return lax.ppermute(array, "blk", pairs)


def split(x):
    high = x.astype(BF16)
    return high, (x - high.astype(F32)).astype(BF16)


def product(left, right):
    return jnp.dot(left, right, preferred_element_type=F32)


def lane_slot(shape):
    return lax.broadcasted_iota(jnp.int32, shape, 1) // 32


def interleave(first, second):
    even = lane_slot(first.shape) % 2 == 0
    return (
        jnp.where(even, first, pltpu.roll(second, 32, 1)),
        jnp.where(even, pltpu.roll(first, 96, 1), second),
    )


def far_weights(tiles, flip):
    if flip:
        tiles = [jnp.concatenate([t] * 4, 0).T for t in tiles]
        blocks = [[t[32 * k : 32 * k + 32] for t in tiles] for k in range(4)]
    else:
        blocks = [tiles] * 4
    slot = lane_slot((32, 128))
    rows = [jnp.concatenate([jnp.where(slot == k, t, 0.0) for t in blocks[k]], 1) for k in range(4)]
    high, low = split(jnp.concatenate(rows, 0))
    return jnp.concatenate([high, high], 0), low


def near_turned(tiles):
    stack = jnp.concatenate([tiles[0], tiles[1], tiles[0], tiles[1]], 0).T
    return [stack[32 * k : 32 * k + 32] for k in (0, 2, 1, 3)]


def near_plain(tile):
    twice = pltpu.roll(tile, 64, 1)
    lower = lane_slot(tile.shape) < 2
    return [jnp.where(lower, tile, twice), jnp.where(lower, twice, tile)]


def advance(state, near, far):
    double, low = far
    high, rest = split(state)
    inner = product(jnp.concatenate([high, rest], 1), double) + product(high, low)
    h0, l0 = split(inner[:, :128])
    h1, l1 = split(inner[:, 128:])
    results = []
    for k, tile in enumerate(near):
        rows = slice(32 * k, 32 * k + 32)
        weights = jnp.concatenate([h0[rows], h1[rows], l0[rows], l1[rows]], 0)
        both = product(jnp.concatenate(split(tile), 0), weights)
        results.append(both[:32] + both[32:])
    return jnp.concatenate(results, 0)


def identities(rows):
    row = lax.broadcasted_iota(jnp.int32, (rows, 128), 0) % 32
    lane = lax.broadcasted_iota(jnp.int32, (rows, 128), 1) % 32
    return jnp.where(row == lane, 1.0, 0.0)


def on_each_side(side_ref, run):
    for side in range(2):
        pl.when(side_ref[0] == side)(functools.partial(run, side == 1))


def turned(tile):
    stack = jnp.concatenate([tile] * 4, 0).T
    slot = lane_slot(tile.shape)
    result = stack[:32]
    for k in range(1, 4):
        result = jnp.where(slot == k, stack[32 * k : 32 * k + 32], result)
    return result


def edge_tile(tiles):
    slot = lane_slot((32, 128))
    row = lax.broadcasted_iota(jnp.int32, (32, 128), 0)
    current = jnp.broadcast_to(tiles[0][:1], (32, 128))
    for k, tile in enumerate(tiles[1:]):
        chosen = jnp.where(slot % 2 == (row >> k) % 2, current, 0.0)
        weights = [jnp.where(slot // 2 == n, tile, 0.0) for n in (0, 0, 1, 1)]
        current = jnp.dot(
            chosen,
            jnp.concatenate(weights, 0),
            precision=lax.Precision.HIGHEST,
            preferred_element_type=F32,
        )
    return current


def order_kernel(side_ref, sites_ref, whole, *pieces):
    sites = sites_ref.shape[0]

    def run(flip):
        def tile(k):
            return sites_ref[sites - 1 - k if flip else k]

        edge = edge_tile([turned(tile(k)) if flip else tile(k) for k in range(EDGE)])
        if flip:
            edge = turned(edge)
        at = 0
        for piece in pieces:
            for k in range(piece.shape[0]):
                value = edge if at == 0 else tile(at + EDGE - 1)
                piece[k] = value
                whole[at] = value
                at += 1

    on_each_side(side_ref, run)


def norms_only(state):
    slot = lane_slot((32, 128))
    first = jnp.where(slot == 0, state[192:224], state[224:256])
    second = jnp.where(slot == 1, state[256:288], state[288:320])
    kept = jnp.where(slot % 2 == 0, first, second)
    return jnp.concatenate([state[:192], kept], 0)


def home_step(state, home, near, flip):
    return advance(state, near[:2], far_weights(home, flip))


def home_kernel(count, side_ref, own, sibling, out):
    def run(flip):
        state = identities(64)
        for site in range(count):
            home = interleave(own[site], sibling[site])
            state = home_step(state, home, near_plain(own[site]) if flip else near_turned(home), flip)
        out[...] = state

    on_each_side(side_ref, run)


def chain_kernel(start, side_ref, own, sibling, first, second, other, *rest):
    out = rest[-1]
    count = first.shape[0]
    last = start + count == own.shape[0]

    def run(flip):
        state = rest[1][...] if start else identities(320)
        inner = rest[0][...] if last else None
        for index in range(count):
            whole = start + index
            home = interleave(own[whole], sibling[whole])
            far = interleave(first[index], second[index])
            if flip:
                near = [n for t in (own[whole], sibling[whole], other[index], first[index], second[index])
                        for n in near_plain(t)]
            else:
                extra = other[index]
                near = near_turned(home) + near_turned(interleave(extra, extra))[:2] + near_turned(far)
            weights = far_weights(far, flip)
            parts = [advance(state[:192], near[:6], weights), advance(state[192:], near[6:], weights)]
            state = jnp.concatenate(parts, 0)
            if last:
                inner = home_step(inner, home, near, flip)
        out[...] = jnp.concatenate([norms_only(state), inner], 0) if last else state

    on_each_side(side_ref, run)


def meet_kernel(mine, theirs, out):
    units = jnp.sum((mine[...] * theirs[...]).reshape(-1, 32, 128), 1)
    units = jnp.concatenate([units, jnp.zeros((16 - units.shape[0], 128), F32)], 0)
    row = lax.broadcasted_iota(jnp.int32, (8, 128), 0)
    chosen = jnp.where(row == lane_slot((8, 128)), 1.0, 0.0)
    found = lax.dot_general(
        chosen, units, (((1,), (1,)), ((), ())), precision=lax.Precision.HIGHEST, preferred_element_type=F32
    )
    out[...] = jnp.concatenate([found, jnp.zeros((8, 112), F32)], 1)


def join_kernel(mine, theirs, out):
    out[...] = mine[...] + pltpu.roll(theirs[...], 16, 1)


def pick_kernel(spot_ref, here, after, before, out):
    joined = here[...] + pltpu.roll(after[...], 32, 1) + pltpu.roll(before[...], 64, 1)
    unit = lax.broadcasted_iota(jnp.int32, (128, 128), 0)
    slot = lax.broadcasted_iota(jnp.int32, (8, 128), 0)
    values = []
    for k in range(3):
        spot = spot_ref[pl.ds(k, 1), :]
        chosen = jnp.where(unit == spot // 8, 1.0, 0.0)
        found = jnp.dot(joined, chosen, precision=lax.Precision.HIGHEST, preferred_element_type=F32)
        values.append(jnp.sum(jnp.where(slot == spot % 8, found, 0.0), 0, keepdims=True))
    tile, remote, own = values
    width = out.shape[1]
    out[...] = (tile * tile / (own * remote))[:, :width]


def find(core, near, far):
    mine, theirs = ("A0", "A1"), ("Z1", "Z0")
    if core == 1:
        mine, theirs = theirs, mine
    own, sibling = f"O{core}", f"O{1 - core}"
    if near == far and near in mine:
        return lambda n, m: (6, mine.index(near) + 2 * m)
    for base, rows, lanes in ((0, (own, sibling, theirs[1]), mine), (7, (own,), (own, sibling))):
        if near in rows and far in lanes:
            return lambda n, m: (base + 2 * rows.index(near) + n, lanes.index(far) + 2 * m)
        if far in rows and near in lanes:
            return lambda n, m: (base + 2 * rows.index(far) + m, lanes.index(near) + 2 * n)
    return None


def spot_table(core, samp, band):
    views = [(role, (k, k + 1) if core == 0 else (k + 1, k)) for k, role in ((0, "O"), (2, "A"), (4, "Z"))]
    shift = {"O": 0, "A": -1, "Z": 2}

    def place(offset, alone=False):
        chip, lane = (core + offset) // 2, (core + offset) % 2
        for role, messages in views:
            for name, gap in shift.items():
                if gap - shift[role] == chip:
                    goal = f"{name}{lane}"
                    for k, message in enumerate(messages):
                        got = find(k, goal if alone else f"{role}{core}", goal)
                        if got:
                            return message, got
        raise ValueError(offset)

    def code(where, n, m):
        message, got = where
        unit, slot = got(n, m)
        return 8 * (16 * message + unit) + slot

    offsets = range(-band, band + 1)
    table = []
    for n in range(samp):
        tile = [code(place(o), n, m) for o in offsets for m in range(samp)]
        remote = [code(place(o, True), m, m) for o in offsets for m in range(samp)]
        own = [code(place(0, True), n, n)] * len(tile)
        rows = [r + r[:1] * (128 - len(r)) for r in (tile, remote, own)]
        table.append(rows + rows[:1] * 5)
    return table


def call(kernel, shapes, *args, name):
    many = isinstance(shapes, list)
    shapes = [jax.ShapeDtypeStruct(shape, F32) for shape in (shapes if many else [shapes])]
    return pl.pallas_call(
        kernel,
        out_shape=shapes if many else shapes[0],
        in_specs=[SMEM if a.ndim == 1 else VMEM for a in args],
        out_specs=[VMEM] * len(shapes) if many else VMEM,
        compiler_params=pltpu.CompilerParams(vmem_limit_bytes=40 * 2**20),
        name=name,
    )(*args)


def body(mps):
    sites, chi = mps.shape[:2]
    samp = mps.shape[2] // (2 * chi)
    blocks = lax.axis_size("blk")
    band = min(REACH, (blocks - 1) // 2)
    side = lax.axis_index("pair")
    flag = side[None].astype(jnp.int32)

    steps = sites - EDGE + 1
    starts = [0, round(SHARE * steps)]
    counts = [starts[1], steps - starts[1]]
    tile = mps.shape[1:]
    mps, *pieces = call(order_kernel, [(n, *tile) for n in (steps, *counts)], flag, mps, name="order")
    seconds = [move(p, lambda chip, core: (chip - 1, 1) if core == 0 else (chip + 2, 0)) for p in pieces]
    firsts = [move(p, lambda chip, core: (chip - 1, 0) if core == 0 else (chip + 2, 1)) for p in pieces]
    across = lambda chip, core: (chip, 1 - core)
    sibling = move(mps, across)
    inner = call(functools.partial(home_kernel, starts[-1]), (64, 128), flag, mps, sibling, name="own_chains")
    carried = (inner,)
    for start, first, second in zip(starts, firsts, seconds):
        second, *carried = lax.optimization_barrier((second, *carried))
        other = move(second, across)
        rows = 288 if start == starts[-1] else 320
        state = call(functools.partial(chain_kernel, start), (rows, 128), flag, mps, sibling, first, second, other,
                     *carried, name="half_chains")
        carried = (carried[0], state)
    partner = lax.ppermute(state, "pair", [(0, 1), (1, 0)])
    tile = call(meet_kernel, (8, 128), state, partner, name="meet")
    tile = call(join_kernel, (8, 128), tile, move(tile, across), name="join")
    tiles = [tile] + [move(tile, lambda chip, core: (chip + gap, core)) for gap in (1, -2)]
    spots = jnp.asarray([spot_table(core, samp, band) for core in range(2)], jnp.int32)
    spot = spots[lax.axis_index("blk") % 2, side]
    return call(pick_kernel, (1, (2 * band + 1) * samp), spot, *tiles, name="pick")


def solution(mesh):
    in_specs = (P("pair", None, "blk"),)
    out_specs = P(("blk", "pair"), None)
    return jax.shard_map(body, mesh=mesh, in_specs=in_specs, out_specs=out_specs, check_vma=False)
```

```python
import functools

import jax
import jax.numpy as jnp
from jax import lax
from jax.experimental import pallas as pl
from jax.experimental.pallas import tpu as pltpu
from jax.sharding import PartitionSpec as P

REACH = 6
EDGE = 6
SHARE = 0.63
BF16, F32 = jnp.bfloat16, jnp.float32
VMEM = pl.BlockSpec(memory_space=pltpu.VMEM)
SMEM = pl.BlockSpec(memory_space=pltpu.SMEM)


def move(array, source):
    peers = lax.axis_size("blk")
    chips = peers // 2
    pairs = []
    for d in range(peers):
        chip, core = source(d // 2, d % 2)
        pairs.append(((chip % chips) * 2 + core, d))
    return lax.ppermute(array, "blk", pairs)


def split(x):
    high = x.astype(BF16)
    return high, (x - high.astype(F32)).astype(BF16)


def product(left, right):
    return jnp.dot(left, right, preferred_element_type=F32)


def lane_slot(shape):
    return lax.broadcasted_iota(jnp.int32, shape, 1) // 32


def interleave(first, second):
    even = lane_slot(first.shape) % 2 == 0
    return (
        jnp.where(even, first, pltpu.roll(second, 32, 1)),
        jnp.where(even, pltpu.roll(first, 96, 1), second),
    )


def far_weights(tiles, flip):
    if flip:
        tiles = [jnp.concatenate([t] * 4, 0).T for t in tiles]
        blocks = [[t[32 * k : 32 * k + 32] for t in tiles] for k in range(4)]
    else:
        blocks = [tiles] * 4
    slot = lane_slot((32, 128))
    rows = [jnp.concatenate([jnp.where(slot == k, t, 0.0) for t in blocks[k]], 1) for k in range(4)]
    high, low = split(jnp.concatenate(rows, 0))
    return jnp.concatenate([high, high], 0), low


def near_turned(tiles):
    stack = jnp.concatenate([tiles[0], tiles[1], tiles[0], tiles[1]], 0).T
    return [stack[32 * k : 32 * k + 32] for k in (0, 2, 1, 3)]


def near_plain(tile):
    twice = pltpu.roll(tile, 64, 1)
    lower = lane_slot(tile.shape) < 2
    return [jnp.where(lower, tile, twice), jnp.where(lower, twice, tile)]


def advance(state, near, far):
    double, low = far
    high, rest = split(state)
    inner = product(jnp.concatenate([high, rest], 1), double) + product(high, low)
    h0, l0 = split(inner[:, :128])
    h1, l1 = split(inner[:, 128:])
    results = []
    for k, tile in enumerate(near):
        rows = slice(32 * k, 32 * k + 32)
        weights = jnp.concatenate([h0[rows], h1[rows], l0[rows], l1[rows]], 0)
        both = product(jnp.concatenate(split(tile), 0), weights)
        results.append(both[:32] + both[32:])
    return jnp.concatenate(results, 0)


def identities(rows):
    row = lax.broadcasted_iota(jnp.int32, (rows, 128), 0) % 32
    lane = lax.broadcasted_iota(jnp.int32, (rows, 128), 1) % 32
    return jnp.where(row == lane, 1.0, 0.0)


def on_each_side(side_ref, run):
    for side in range(2):
        pl.when(side_ref[0] == side)(functools.partial(run, side == 1))


def turned(tile):
    stack = jnp.concatenate([tile] * 4, 0).T
    slot = lane_slot(tile.shape)
    result = stack[:32]
    for k in range(1, 4):
        result = jnp.where(slot == k, stack[32 * k : 32 * k + 32], result)
    return result


def edge_tile(tiles):
    slot = lane_slot((32, 128))
    row = lax.broadcasted_iota(jnp.int32, (32, 128), 0)
    current = jnp.broadcast_to(tiles[0][:1], (32, 128))
    for k, tile in enumerate(tiles[1:]):
        chosen = jnp.where(slot % 2 == (row >> k) % 2, current, 0.0)
        weights = [jnp.where(slot // 2 == n, tile, 0.0) for n in (0, 0, 1, 1)]
        current = jnp.dot(
            chosen,
            jnp.concatenate(weights, 0),
            precision=lax.Precision.HIGHEST,
            preferred_element_type=F32,
        )
    return current


def order_kernel(side_ref, sites_ref, whole, *rest):
    *pieces, edges, semaphores = rest
    sites, steps = sites_ref.shape[0], whole.shape[0]

    def run(flip):
        outer = sites_ref.at[pl.ds(sites - EDGE if flip else 0, EDGE)]
        copies = [pltpu.make_async_copy(outer, edges, semaphores.at[0])]
        begin = 0
        spots = []
        for k, (array, start) in enumerate([(whole, 0)] + [(p, None) for p in pieces]):
            start = begin if start is None else start
            count = array.shape[0]
            begin = 0 if k == 0 else begin + count
            spare = 1 if start == 0 else 0
            low = steps - start - count if flip else start
            kept = count - spare
            source = sites_ref.at[pl.ds(low if flip else low + spare + EDGE - 1, kept)]
            target = array.at[pl.ds(0 if flip else spare, kept)]
            copies.append(pltpu.make_async_copy(source, target, semaphores.at[k + 1]))
            if spare:
                spots.append((array, count - 1 if flip else 0))
        for copy in copies:
            copy.start()
        copies[0].wait()
        tiles = [edges[EDGE - 1 - k if flip else k] for k in range(EDGE)]
        edge = edge_tile([turned(t) for t in tiles] if flip else tiles)
        if flip:
            edge = turned(edge)
        for array, at in spots:
            array[at] = edge
        for copy in copies[1:]:
            copy.wait()

    on_each_side(side_ref, run)


def norms_only(state):
    slot = lane_slot((32, 128))
    first = jnp.where(slot == 0, state[192:224], state[224:256])
    second = jnp.where(slot == 1, state[256:288], state[288:320])
    kept = jnp.where(slot % 2 == 0, first, second)
    return jnp.concatenate([state[:192], kept], 0)


def home_kernel(start, count, side_ref, own, sibling, *rest):
    out = rest[-1]

    def run(flip):
        state = rest[0][...] if start else identities(64)
        for step in range(start, start + count):
            site = own.shape[0] - 1 - step if flip else step
            home = interleave(own[site], sibling[site])
            near = near_plain(own[site]) if flip else near_turned(home)[:2]
            state = advance(state, near, far_weights(home, flip))
        out[...] = state

    on_each_side(side_ref, run)


def chain_kernel(start, side_ref, own, sibling, first, second, other, *rest):
    out = rest[-1]
    count, steps = first.shape[0], own.shape[0]

    def run(flip):
        state = rest[-2][...] if start else identities(320)
        for index in range(count):
            whole = steps - 1 - start - index if flip else start + index
            part = count - 1 - index if flip else index
            far = interleave(first[part], second[part])
            if flip:
                near = [n for t in (own[whole], sibling[whole], other[part], first[part], second[part])
                        for n in near_plain(t)]
            else:
                extra = other[part]
                near = (
                    near_turned(interleave(own[whole], sibling[whole]))
                    + near_turned(interleave(extra, extra))[:2]
                    + near_turned(far)
                )
            weights = far_weights(far, flip)
            parts = [advance(state[:192], near[:6], weights), advance(state[192:], near[6:], weights)]
            state = jnp.concatenate(parts, 0)
        out[...] = norms_only(state) if start + count == steps else state

    on_each_side(side_ref, run)


def meet_kernel(*refs):
    *states, out = refs
    units = [
        jnp.sum((mine[...] * theirs[...]).reshape(-1, 32, 128), 1)
        for mine, theirs in zip(states[::2], states[1::2])
    ]
    units = jnp.concatenate(units, 0)
    units = jnp.concatenate([units, jnp.zeros((16 - units.shape[0], 128), F32)], 0)
    row = lax.broadcasted_iota(jnp.int32, (8, 128), 0)
    chosen = jnp.where(row == lane_slot((8, 128)), 1.0, 0.0)
    found = lax.dot_general(
        chosen, units, (((1,), (1,)), ((), ())), precision=lax.Precision.HIGHEST, preferred_element_type=F32
    )
    out[...] = jnp.concatenate([found, jnp.zeros((8, 112), F32)], 1)


def join_kernel(mine, theirs, out):
    out[...] = mine[...] + pltpu.roll(theirs[...], 16, 1)


def pick_kernel(which_ref, spots_ref, here, after, before, out):
    joined = here[...] + pltpu.roll(after[...], 32, 1) + pltpu.roll(before[...], 64, 1)
    spots = spots_ref[which_ref[0]]
    unit = lax.broadcasted_iota(jnp.int32, (128, 128), 0)
    slot = lax.broadcasted_iota(jnp.int32, (8, 128), 0)
    chosen = [jnp.where(unit == spots[k : k + 1] // 8, 1.0, 0.0) for k in range(3)]
    found = jnp.dot(
        joined, jnp.concatenate(chosen, 1), precision=lax.Precision.HIGHEST, preferred_element_type=F32
    )
    tile, remote, own = [
        jnp.sum(jnp.where(slot == spots[k : k + 1] % 8, found[:, 128 * k : 128 * k + 128], 0.0), 0, keepdims=True)
        for k in range(3)
    ]
    out[...] = (tile * tile / (own * remote))[:, : out.shape[1]]


def find(core, near, far):
    mine, theirs = ("A0", "A1"), ("Z1", "Z0")
    if core == 1:
        mine, theirs = theirs, mine
    own, sibling = f"O{core}", f"O{1 - core}"
    if near == far and near in mine:
        return lambda n, m: (6, mine.index(near) + 2 * m)
    for base, rows, lanes in ((0, (own, sibling, theirs[1]), mine), (7, (own,), (own, sibling))):
        if near in rows and far in lanes:
            return lambda n, m: (base + 2 * rows.index(near) + n, lanes.index(far) + 2 * m)
        if far in rows and near in lanes:
            return lambda n, m: (base + 2 * rows.index(far) + m, lanes.index(near) + 2 * n)
    return None


def spot_table(core, samp, band):
    views = [(role, (k, k + 1) if core == 0 else (k + 1, k)) for k, role in ((0, "O"), (2, "A"), (4, "Z"))]
    shift = {"O": 0, "A": -1, "Z": 2}

    def place(offset, alone=False):
        chip, lane = (core + offset) // 2, (core + offset) % 2
        for role, messages in views:
            for name, gap in shift.items():
                if gap - shift[role] == chip:
                    goal = f"{name}{lane}"
                    for k, message in enumerate(messages):
                        got = find(k, goal if alone else f"{role}{core}", goal)
                        if got:
                            return message, got
        raise ValueError(offset)

    def code(where, n, m):
        message, got = where
        unit, slot = got(n, m)
        return 8 * (16 * message + unit) + slot

    offsets = range(-band, band + 1)
    table = []
    for n in range(samp):
        tile = [code(place(o), n, m) for o in offsets for m in range(samp)]
        remote = [code(place(o, True), m, m) for o in offsets for m in range(samp)]
        own = [code(place(0, True), n, n)] * len(tile)
        rows = [r + r[:1] * (128 - len(r)) for r in (tile, remote, own)]
        table.append(rows + rows[:1] * 5)
    return table


def call(kernel, shapes, *args, name, spaces=None, scratch=()):
    many = isinstance(shapes, list)
    shapes = [jax.ShapeDtypeStruct(shape, F32) for shape in (shapes if many else [shapes])]
    return pl.pallas_call(
        kernel,
        out_shape=shapes if many else shapes[0],
        in_specs=spaces or [SMEM if a.ndim == 1 else VMEM for a in args],
        out_specs=[VMEM] * len(shapes) if many else VMEM,
        scratch_shapes=scratch,
        compiler_params=pltpu.CompilerParams(vmem_limit_bytes=40 * 2**20),
        name=name,
    )(*args)


def body(mps):
    sites, chi = mps.shape[:2]
    samp = mps.shape[2] // (2 * chi)
    blocks = lax.axis_size("blk")
    band = min(REACH, (blocks - 1) // 2)
    side = lax.axis_index("pair")
    flag = side[None].astype(jnp.int32)
    core = lax.axis_index("blk") % 2

    steps = sites - EDGE + 1
    starts = [0, round(SHARE * steps)]
    counts = [starts[1], steps - starts[1]]
    tile = mps.shape[1:]
    own, *pieces = call(
        order_kernel,
        [(n, *tile) for n in (steps, *counts)],
        flag,
        mps,
        name="order",
        spaces=[SMEM, pl.BlockSpec(memory_space=pltpu.HBM)],
        scratch=[pltpu.VMEM((EDGE, *tile), F32), pltpu.SemaphoreType.DMA((2 + len(counts),))],
    )
    seconds = [move(p, lambda chip, core: (chip - 1, 1) if core == 0 else (chip + 2, 0)) for p in pieces]
    firsts = [move(p, lambda chip, core: (chip - 1, 0) if core == 0 else (chip + 2, 1)) for p in pieces]
    across = lambda chip, core: (chip, 1 - core)
    swap = [(0, 1), (1, 0)]
    sibling = move(own, across)

    early = steps // 2
    home = functools.partial(home_kernel, 0, early)
    home = call(home, (64, 128), flag, own, sibling, name="own_chains")
    carried = (home,)
    for k, (start, first, second) in enumerate(zip(starts, firsts, seconds)):
        second, behind = lax.optimization_barrier((second, carried[-1]))
        carried = (*carried[:-1], behind)
        other = move(second, across)
        if k == 0:
            home = functools.partial(home_kernel, early, steps - early)
            home = call(home, (64, 128), flag, own, sibling, *carried, name="own_chains")
            far_home = lax.ppermute(home, "pair", swap)
            carried = (home,)
        rows = 224 if k == len(starts) - 1 else 320
        state = call(functools.partial(chain_kernel, start), (rows, 128), flag, own, sibling, first, second, other,
                     *carried, name="half_chains")
        carried = (far_home, state)
    partner = lax.ppermute(state, "pair", swap)
    tile = call(meet_kernel, (8, 128), state, partner, home, far_home, name="meet")
    tile = call(join_kernel, (8, 128), tile, move(tile, across), name="join")
    tiles = [tile] + [move(tile, lambda chip, core: (chip + gap, core)) for gap in (1, -2)]
    spots = jnp.asarray([t for k in range(2) for t in spot_table(k, samp, band)], jnp.int32)
    which = (core * samp + side)[None].astype(jnp.int32)
    return call(pick_kernel, (1, (2 * band + 1) * samp), which, spots, *tiles, name="pick")


def solution(mesh):
    in_specs = (P("pair", None, "blk"),)
    out_specs = P(("blk", "pair"), None)
    return jax.shard_map(body, mesh=mesh, in_specs=in_specs, out_specs=out_specs, check_vma=False)
```

```python
import functools

import jax
import jax.numpy as jnp
from jax import lax
from jax.experimental import pallas as pl
from jax.experimental.pallas import tpu as pltpu
from jax.sharding import PartitionSpec as P

REACH = 6
EDGE = 6
SHARES = (1.0,)
BF16, F32 = jnp.bfloat16, jnp.float32
VMEM = pl.BlockSpec(memory_space=pltpu.VMEM)
SMEM = pl.BlockSpec(memory_space=pltpu.SMEM)


def move(array, source, takes=lambda chip, core: True):
    peers = lax.axis_size("blk")
    chips = peers // 2
    pairs = []
    for d in range(peers):
        if takes(d // 2, d % 2):
            chip, core = source(d // 2, d % 2)
            pairs.append(((chip % chips) * 2 + core, d))
    return lax.ppermute(array, "blk", pairs)


def split(x):
    high = x.astype(BF16)
    return high, (x - high.astype(F32)).astype(BF16)


def product(left, right):
    return jnp.dot(left, right, preferred_element_type=F32)


def lane_slot(shape):
    return lax.broadcasted_iota(jnp.int32, shape, 1) // 32


def interleave(first, second):
    even = lane_slot(first.shape) % 2 == 0
    return (
        jnp.where(even, first, pltpu.roll(second, 32, 1)),
        jnp.where(even, pltpu.roll(first, 96, 1), second),
    )


def far_weights(tiles, flip):
    if flip:
        tiles = [jnp.concatenate([t] * 4, 0).T for t in tiles]
        blocks = [[t[32 * k : 32 * k + 32] for t in tiles] for k in range(4)]
    else:
        blocks = [tiles] * 4
    slot = lane_slot((32, 128))
    rows = [jnp.concatenate([jnp.where(slot == k, t, 0.0) for t in blocks[k]], 1) for k in range(4)]
    high, low = split(jnp.concatenate(rows, 0))
    return jnp.concatenate([high, high], 0), low


def near_turned(tiles):
    stack = jnp.concatenate([tiles[0], tiles[1], tiles[0], tiles[1]], 0).T
    return [stack[32 * k : 32 * k + 32] for k in (0, 2, 1, 3)]


def near_plain(tile):
    twice = pltpu.roll(tile, 64, 1)
    lower = lane_slot(tile.shape) < 2
    return [jnp.where(lower, tile, twice), jnp.where(lower, twice, tile)]


def advance(state, near, far):
    double, low = far
    high, rest = split(state)
    inner = product(jnp.concatenate([high, rest], 1), double) + product(high, low)
    h0, l0 = split(inner[:, :128])
    h1, l1 = split(inner[:, 128:])
    results = []
    for k, tile in enumerate(near):
        rows = slice(32 * k, 32 * k + 32)
        weights = jnp.concatenate([h0[rows], h1[rows], l0[rows], l1[rows]], 0)
        both = product(jnp.concatenate(split(tile), 0), weights)
        results.append(both[:32] + both[32:])
    return jnp.concatenate(results, 0)


def identities(rows):
    row = lax.broadcasted_iota(jnp.int32, (rows, 128), 0) % 32
    lane = lax.broadcasted_iota(jnp.int32, (rows, 128), 1) % 32
    return jnp.where(row == lane, 1.0, 0.0)


def on_each_side(side_ref, run):
    for side in range(2):
        pl.when(side_ref[0] == side)(functools.partial(run, side == 1))


def turned(tile):
    stack = jnp.concatenate([tile] * 4, 0).T
    slot = lane_slot(tile.shape)
    result = stack[:32]
    for k in range(1, 4):
        result = jnp.where(slot == k, stack[32 * k : 32 * k + 32], result)
    return result


def edge_tile(tiles):
    slot = lane_slot((32, 128))
    row = lax.broadcasted_iota(jnp.int32, (32, 128), 0)
    current = jnp.broadcast_to(tiles[0][:1], (32, 128))
    for k, tile in enumerate(tiles[1:]):
        chosen = jnp.where(slot % 2 == (row >> k) % 2, current, 0.0)
        weights = [jnp.where(slot // 2 == n, tile, 0.0) for n in (0, 0, 1, 1)]
        current = jnp.dot(
            chosen,
            jnp.concatenate(weights, 0),
            precision=lax.Precision.HIGHEST,
            preferred_element_type=F32,
        )
    return current


def order_kernel(side_ref, sites_ref, whole, *pieces):
    sites = sites_ref.shape[0]

    def run(flip):
        def tile(k):
            return sites_ref[sites - 1 - k if flip else k]

        edge = edge_tile([turned(tile(k)) if flip else tile(k) for k in range(EDGE)])
        if flip:
            edge = turned(edge)
        tiles = [edge] + [tile(k) for k in range(EDGE, sites)]
        for k, value in enumerate(tiles):
            whole[k] = value
        begin = 0
        for piece in pieces:
            for k in range(piece.shape[0]):
                piece[k] = tiles[begin + k]
            begin += piece.shape[0]

    on_each_side(side_ref, run)


def norms_only(state):
    slot = lane_slot((32, 128))
    first = jnp.where(slot == 0, state[192:224], state[224:256])
    second = jnp.where(slot == 1, state[256:288], state[288:320])
    kept = jnp.where(slot % 2 == 0, first, second)
    return jnp.concatenate([state[:192], kept], 0)


def home_kernel(start, count, side_ref, own, sibling, *rest):
    out = rest[-1]

    def run(flip):
        state = rest[0][...] if start else identities(64)
        for step in range(start, start + count):
            home = interleave(own[step], sibling[step])
            near = near_plain(own[step]) if flip else near_turned(home)[:2]
            state = advance(state, near, far_weights(home, flip))
        out[...] = state

    on_each_side(side_ref, run)


def chain_kernel(start, side_ref, own, sibling, first, second, other, *rest):
    out = rest[-1]
    count, steps = first.shape[0], own.shape[0]

    def run(flip):
        state = rest[-2][...] if start else identities(320)
        for index in range(count):
            whole, part = start + index, index
            far = interleave(first[part], second[part])
            if flip:
                near = [n for t in (own[whole], sibling[whole], other[part], first[part], second[part])
                        for n in near_plain(t)]
            else:
                extra = other[part]
                near = (
                    near_turned(interleave(own[whole], sibling[whole]))
                    + near_turned(interleave(extra, extra))[:2]
                    + near_turned(far)
                )
            weights = far_weights(far, flip)
            parts = [advance(state[:192], near[:6], weights), advance(state[192:], near[6:], weights)]
            state = jnp.concatenate(parts, 0)
        out[...] = norms_only(state) if start + count == steps else state

    on_each_side(side_ref, run)


def meet_kernel(*refs):
    *states, out = refs
    units = [
        jnp.sum((mine[...] * theirs[...]).reshape(-1, 32, 128), 1)
        for mine, theirs in zip(states[::2], states[1::2])
    ]
    units = jnp.concatenate(units, 0)
    units = jnp.concatenate([units, jnp.zeros((16 - units.shape[0], 128), F32)], 0)
    row = lax.broadcasted_iota(jnp.int32, (8, 128), 0)
    chosen = jnp.where(row == lane_slot((8, 128)), 1.0, 0.0)
    found = lax.dot_general(
        chosen, units, (((1,), (1,)), ((), ())), precision=lax.Precision.HIGHEST, preferred_element_type=F32
    )
    out[...] = jnp.concatenate([found, jnp.zeros((8, 112), F32)], 1)


def join_kernel(mine, theirs, out):
    out[...] = mine[...] + pltpu.roll(theirs[...], 16, 1)


def pick_kernel(which_ref, spots_ref, here, after, before, out):
    joined = here[...] + pltpu.roll(after[...], 32, 1) + pltpu.roll(before[...], 64, 1)
    spots = spots_ref[which_ref[0]]
    unit = lax.broadcasted_iota(jnp.int32, (128, 128), 0)
    slot = lax.broadcasted_iota(jnp.int32, (8, 128), 0)
    chosen = [jnp.where(unit == spots[k : k + 1] // 8, 1.0, 0.0) for k in range(3)]
    found = jnp.dot(
        joined, jnp.concatenate(chosen, 1), precision=lax.Precision.HIGHEST, preferred_element_type=F32
    )
    tile, remote, own = [
        jnp.sum(jnp.where(slot == spots[k : k + 1] % 8, found[:, 128 * k : 128 * k + 128], 0.0), 0, keepdims=True)
        for k in range(3)
    ]
    out[...] = (tile * tile / (own * remote))[:, : out.shape[1]]


def find(core, near, far):
    mine, theirs = ("A0", "A1"), ("Z1", "Z0")
    if core == 1:
        mine, theirs = theirs, mine
    own, sibling = f"O{core}", f"O{1 - core}"
    if near == far and near in mine:
        return lambda n, m: (6, mine.index(near) + 2 * m)
    for base, rows, lanes in ((0, (own, sibling, theirs[1]), mine), (7, (own,), (own, sibling))):
        if near in rows and far in lanes:
            return lambda n, m: (base + 2 * rows.index(near) + n, lanes.index(far) + 2 * m)
        if far in rows and near in lanes:
            return lambda n, m: (base + 2 * rows.index(far) + m, lanes.index(near) + 2 * n)
    return None


def spot_table(core, samp, band):
    views = [(role, (k, k + 1) if core == 0 else (k + 1, k)) for k, role in ((0, "O"), (2, "A"), (4, "Z"))]
    shift = {"O": 0, "A": -1, "Z": 2}

    def place(offset, alone=False):
        chip, lane = (core + offset) // 2, (core + offset) % 2
        for role, messages in views:
            for name, gap in shift.items():
                if gap - shift[role] == chip:
                    goal = f"{name}{lane}"
                    for k, message in enumerate(messages):
                        got = find(k, goal if alone else f"{role}{core}", goal)
                        if got:
                            return message, got
        raise ValueError(offset)

    def code(where, n, m):
        message, got = where
        unit, slot = got(n, m)
        return 8 * (16 * message + unit) + slot

    offsets = range(-band, band + 1)
    table = []
    for n in range(samp):
        tile = [code(place(o), n, m) for o in offsets for m in range(samp)]
        remote = [code(place(o, True), m, m) for o in offsets for m in range(samp)]
        own = [code(place(0, True), n, n)] * len(tile)
        rows = [r + r[:1] * (128 - len(r)) for r in (tile, remote, own)]
        table.append(rows + rows[:1] * 5)
    return table


def call(kernel, shapes, *args, name):
    many = isinstance(shapes, list)
    shapes = [jax.ShapeDtypeStruct(shape, F32) for shape in (shapes if many else [shapes])]
    return pl.pallas_call(
        kernel,
        out_shape=shapes if many else shapes[0],
        in_specs=[SMEM if a.ndim == 1 else VMEM for a in args],
        out_specs=[VMEM] * len(shapes) if many else VMEM,
        compiler_params=pltpu.CompilerParams(vmem_limit_bytes=40 * 2**20),
        name=name,
    )(*args)


def body(mps):
    sites, chi = mps.shape[:2]
    samp = mps.shape[2] // (2 * chi)
    blocks = lax.axis_size("blk")
    band = min(REACH, (blocks - 1) // 2)
    side = lax.axis_index("pair")
    flag = side[None].astype(jnp.int32)

    place = lax.axis_index("blk")
    core, chip = place % 2, place // 2

    steps = sites - EDGE + 1
    counts = [round(share * steps) for share in SHARES[:-1]]
    counts.append(steps - sum(counts))
    starts = [sum(counts[:k]) for k in range(len(counts))]
    tile = mps.shape[1:]
    chunks = counts if len(counts) > 1 else []
    own, *pieces = call(order_kernel, [(n, *tile) for n in (steps, *chunks)], flag, mps, name="order")
    pieces = pieces or [own]

    relayed = move(own, lambda chip, core: (chip - 2, core), lambda chip, core: chip % 2 == 1 and core == 0)
    seconds = [move(p, lambda chip, core: (chip - 1, 1) if core == 0 else (chip + 2, 0)) for p in pieces]
    across = lambda chip, core: (chip, 1 - core)
    swap = [(0, 1), (1, 0)]
    sibling = move(own, across)
    early = steps * 5 // 8
    home = call(functools.partial(home_kernel, 0, early), (64, 128), flag, own, sibling, name="own_chains")
    relayed, home = lax.optimization_barrier((relayed, home))
    passes = (chip % 2 == 1) & (core == 0)
    firsts = [
        move(jnp.where(passes, relayed[start : start + count], piece),
             lambda chip, core: (chip ^ 1, 0) if core == 0 else (chip + 2, 1))
        for start, count, piece in zip(starts, counts, pieces)
    ]
    behind = home
    for k, (start, first, second) in enumerate(zip(starts, firsts, seconds)):
        second, behind = lax.optimization_barrier((second, behind))
        other = move(second, across)
        if k == 0:
            home = functools.partial(home_kernel, early, steps - early)
            home = call(home, (64, 128), flag, own, sibling, behind, name="own_chains")
            behind = far_home = lax.ppermute(home, "pair", swap)
        rows = 224 if k == len(starts) - 1 else 320
        behind = call(functools.partial(chain_kernel, start), (rows, 128), flag, own, sibling, first, second, other,
                      behind, name="half_chains")
    partner = lax.ppermute(behind, "pair", swap)
    tile = call(meet_kernel, (8, 128), behind, partner, home, far_home, name="meet")
    tile = call(join_kernel, (8, 128), tile, move(tile, across), name="join")
    after, before = [move(tile, lambda chip, core: (chip + gap, core)) for gap in (1, -2)]
    spots = jnp.asarray([t for k in range(2) for t in spot_table(k, samp, band)], jnp.int32)
    which = (core * samp + side)[None].astype(jnp.int32)
    return call(pick_kernel, (1, (2 * band + 1) * samp), which, spots, tile, after, before, name="pick")


def solution(mesh):
    in_specs = (P("pair", None, "blk"),)
    out_specs = P(("blk", "pair"), None)
    return jax.shard_map(body, mesh=mesh, in_specs=in_specs, out_specs=out_specs, check_vma=False)
```

```python
import functools

import jax
import jax.numpy as jnp
from jax import lax
from jax.experimental import pallas as pl
from jax.experimental.pallas import tpu as pltpu
from jax.sharding import PartitionSpec as P

REACH = 6
EDGE = 6
SHARE = 0.63
BF16, F32 = jnp.bfloat16, jnp.float32
VMEM = pl.BlockSpec(memory_space=pltpu.VMEM)
SMEM = pl.BlockSpec(memory_space=pltpu.SMEM)


def move(array, source, takes=lambda chip, core: True):
    peers = lax.axis_size("blk")
    chips = peers // 2
    pairs = []
    for d in range(peers):
        if takes(d // 2, d % 2):
            chip, core = source(d // 2, d % 2)
            pairs.append(((chip % chips) * 2 + core, d))
    return lax.ppermute(array, "blk", pairs)


def split(x):
    high = x.astype(BF16)
    return high, (x - high.astype(F32)).astype(BF16)


def product(left, right):
    return jnp.dot(left, right, preferred_element_type=F32)


def lane_slot(shape):
    return lax.broadcasted_iota(jnp.int32, shape, 1) // 32


def interleave(first, second):
    even = lane_slot(first.shape) % 2 == 0
    return (
        jnp.where(even, first, pltpu.roll(second, 32, 1)),
        jnp.where(even, pltpu.roll(first, 96, 1), second),
    )


def far_weights(tiles, flip):
    if flip:
        tiles = [jnp.concatenate([t] * 4, 0).T for t in tiles]
        blocks = [[t[32 * k : 32 * k + 32] for t in tiles] for k in range(4)]
    else:
        blocks = [tiles] * 4
    slot = lane_slot((32, 128))
    rows = [jnp.concatenate([jnp.where(slot == k, t, 0.0) for t in blocks[k]], 1) for k in range(4)]
    high, low = split(jnp.concatenate(rows, 0))
    return jnp.concatenate([high, high], 0), low


def near_turned(tiles):
    stack = jnp.concatenate([tiles[0], tiles[1], tiles[0], tiles[1]], 0).T
    return [stack[32 * k : 32 * k + 32] for k in (0, 2, 1, 3)]


def near_plain(tile):
    twice = pltpu.roll(tile, 64, 1)
    lower = lane_slot(tile.shape) < 2
    return [jnp.where(lower, tile, twice), jnp.where(lower, twice, tile)]


def advance(state, near, far):
    double, low = far
    high, rest = split(state)
    inner = product(jnp.concatenate([high, rest], 1), double) + product(high, low)
    h0, l0 = split(inner[:, :128])
    h1, l1 = split(inner[:, 128:])
    results = []
    for k, tile in enumerate(near):
        rows = slice(32 * k, 32 * k + 32)
        weights = jnp.concatenate([h0[rows], h1[rows], l0[rows], l1[rows]], 0)
        both = product(jnp.concatenate(split(tile), 0), weights)
        results.append(both[:32] + both[32:])
    return jnp.concatenate(results, 0)


def identities(rows):
    row = lax.broadcasted_iota(jnp.int32, (rows, 128), 0) % 32
    lane = lax.broadcasted_iota(jnp.int32, (rows, 128), 1) % 32
    return jnp.where(row == lane, 1.0, 0.0)


def on_each_side(side_ref, run):
    for side in range(2):
        pl.when(side_ref[0] == side)(functools.partial(run, side == 1))


def turned(tile):
    stack = jnp.concatenate([tile] * 4, 0).T
    slot = lane_slot(tile.shape)
    result = stack[:32]
    for k in range(1, 4):
        result = jnp.where(slot == k, stack[32 * k : 32 * k + 32], result)
    return result


def edge_tile(tiles):
    slot = lane_slot((32, 128))
    row = lax.broadcasted_iota(jnp.int32, (32, 128), 0)
    current = jnp.broadcast_to(tiles[0][:1], (32, 128))
    for k, tile in enumerate(tiles[1:]):
        chosen = jnp.where(slot % 2 == (row >> k) % 2, current, 0.0)
        weights = [jnp.where(slot // 2 == n, tile, 0.0) for n in (0, 0, 1, 1)]
        current = jnp.dot(
            chosen,
            jnp.concatenate(weights, 0),
            precision=lax.Precision.HIGHEST,
            preferred_element_type=F32,
        )
    return current


def order_kernel(side_ref, sites_ref, whole, *pieces):
    sites = sites_ref.shape[0]

    def run(flip):
        def tile(k):
            return sites_ref[sites - 1 - k if flip else k]

        edge = edge_tile([turned(tile(k)) if flip else tile(k) for k in range(EDGE)])
        if flip:
            edge = turned(edge)
        at = 0
        for piece in pieces:
            for k in range(piece.shape[0]):
                value = edge if at == 0 else tile(at + EDGE - 1)
                piece[k] = value
                whole[at] = value
                at += 1

    on_each_side(side_ref, run)


def norms_only(state):
    slot = lane_slot((32, 128))
    first = jnp.where(slot == 0, state[192:224], state[224:256])
    second = jnp.where(slot == 1, state[256:288], state[288:320])
    kept = jnp.where(slot % 2 == 0, first, second)
    return jnp.concatenate([state[:192], kept], 0)


def home_step(state, home, near, flip):
    return advance(state, near[:2], far_weights(home, flip))


def home_kernel(count, side_ref, own, sibling, out):
    def run(flip):
        state = identities(64)
        for site in range(count):
            home = interleave(own[site], sibling[site])
            state = home_step(state, home, near_plain(own[site]) if flip else near_turned(home), flip)
        out[...] = state

    on_each_side(side_ref, run)


def chain_kernel(start, side_ref, own, sibling, crossed, first, second, other, *rest):
    out = rest[-1]
    count = first.shape[0]
    last = start + count == own.shape[0]

    def run(flip):
        state = rest[1][...] if start else identities(320)
        inner = rest[0][...] if last else None
        for index in range(count):
            whole = start + index
            home = interleave(own[whole], sibling[whole])
            one = jnp.where(side_ref[1] == 1, crossed[whole], first[index])
            far = interleave(one, second[index])
            if flip:
                near = [n for t in (own[whole], sibling[whole], other[index], one, second[index])
                        for n in near_plain(t)]
            else:
                extra = other[index]
                near = near_turned(home) + near_turned(interleave(extra, extra))[:2] + near_turned(far)
            weights = far_weights(far, flip)
            parts = [advance(state[:192], near[:6], weights), advance(state[192:], near[6:], weights)]
            state = jnp.concatenate(parts, 0)
            if last:
                inner = home_step(inner, home, near, flip)
        out[...] = jnp.concatenate([norms_only(state), inner], 0) if last else state

    on_each_side(side_ref, run)


def meet_kernel(mine, theirs, out):
    units = jnp.sum((mine[...] * theirs[...]).reshape(-1, 32, 128), 1)
    units = jnp.concatenate([units, jnp.zeros((16 - units.shape[0], 128), F32)], 0)
    row = lax.broadcasted_iota(jnp.int32, (8, 128), 0)
    chosen = jnp.where(row == lane_slot((8, 128)), 1.0, 0.0)
    found = lax.dot_general(
        chosen, units, (((1,), (1,)), ((), ())), precision=lax.Precision.HIGHEST, preferred_element_type=F32
    )
    out[...] = jnp.concatenate([found, jnp.zeros((8, 112), F32)], 1)


def join_kernel(mine, theirs, out):
    out[...] = mine[...] + pltpu.roll(theirs[...], 16, 1)


def pick_kernel(spot_ref, here, after, before, out):
    joined = here[...] + pltpu.roll(after[...], 32, 1) + pltpu.roll(before[...], 64, 1)
    unit = lax.broadcasted_iota(jnp.int32, (128, 128), 0)
    slot = lax.broadcasted_iota(jnp.int32, (8, 128), 0)
    values = []
    for k in range(3):
        spot = spot_ref[pl.ds(k, 1), :]
        chosen = jnp.where(unit == spot // 8, 1.0, 0.0)
        found = jnp.dot(joined, chosen, precision=lax.Precision.HIGHEST, preferred_element_type=F32)
        values.append(jnp.sum(jnp.where(slot == spot % 8, found, 0.0), 0, keepdims=True))
    tile, remote, own = values
    width = out.shape[1]
    out[...] = (tile * tile / (own * remote))[:, :width]


def find(core, near, far):
    mine, theirs = ("A0", "A1"), ("Z1", "Z0")
    if core == 1:
        mine, theirs = theirs, mine
    own, sibling = f"O{core}", f"O{1 - core}"
    if near == far and near in mine:
        return lambda n, m: (6, mine.index(near) + 2 * m)
    for base, rows, lanes in ((0, (own, sibling, theirs[1]), mine), (7, (own,), (own, sibling))):
        if near in rows and far in lanes:
            return lambda n, m: (base + 2 * rows.index(near) + n, lanes.index(far) + 2 * m)
        if far in rows and near in lanes:
            return lambda n, m: (base + 2 * rows.index(far) + m, lanes.index(near) + 2 * n)
    return None


def spot_table(core, samp, band):
    views = [(role, (k, k + 1) if core == 0 else (k + 1, k)) for k, role in ((0, "O"), (2, "A"), (4, "Z"))]
    shift = {"O": 0, "A": -1, "Z": 2}

    def place(offset, alone=False):
        chip, lane = (core + offset) // 2, (core + offset) % 2
        for role, messages in views:
            for name, gap in shift.items():
                if gap - shift[role] == chip:
                    goal = f"{name}{lane}"
                    for k, message in enumerate(messages):
                        got = find(k, goal if alone else f"{role}{core}", goal)
                        if got:
                            return message, got
        raise ValueError(offset)

    def code(where, n, m):
        message, got = where
        unit, slot = got(n, m)
        return 8 * (16 * message + unit) + slot

    offsets = range(-band, band + 1)
    table = []
    for n in range(samp):
        tile = [code(place(o), n, m) for o in offsets for m in range(samp)]
        remote = [code(place(o, True), m, m) for o in offsets for m in range(samp)]
        own = [code(place(0, True), n, n)] * len(tile)
        rows = [r + r[:1] * (128 - len(r)) for r in (tile, remote, own)]
        table.append(rows + rows[:1] * 5)
    return table


def call(kernel, shapes, *args, name):
    many = isinstance(shapes, list)
    shapes = [jax.ShapeDtypeStruct(shape, F32) for shape in (shapes if many else [shapes])]
    return pl.pallas_call(
        kernel,
        out_shape=shapes if many else shapes[0],
        in_specs=[SMEM if a.ndim == 1 else VMEM for a in args],
        out_specs=[VMEM] * len(shapes) if many else VMEM,
        compiler_params=pltpu.CompilerParams(vmem_limit_bytes=40 * 2**20),
        name=name,
    )(*args)


def body(mps):
    sites, chi = mps.shape[:2]
    samp = mps.shape[2] // (2 * chi)
    blocks = lax.axis_size("blk")
    band = min(REACH, (blocks - 1) // 2)
    side = lax.axis_index("pair")
    place = lax.axis_index("blk")
    chip, core = place // 2, place % 2
    flag = jnp.stack([side, (chip % 2 == 1) & (core == 0)]).astype(jnp.int32)

    steps = sites - EDGE + 1
    starts = [0, round(SHARE * steps)]
    counts = [starts[1], steps - starts[1]]
    tile = mps.shape[1:]
    own, *pieces = call(order_kernel, [(n, *tile) for n in (steps, *counts)], flag, mps, name="order")

    crossed = move(own, lambda chip, core: (chip ^ 1, core), lambda chip, core: core == 0)
    seconds = [move(p, lambda chip, core: (chip - 1, 1) if core == 0 else (chip + 2, 0)) for p in pieces]
    across = lambda chip, core: (chip, 1 - core)
    sibling = move(own, across)
    inner = functools.partial(home_kernel, starts[-1])
    inner = call(inner, (64, 128), flag, own, sibling, name="own_chains")
    crossed, inner = lax.optimization_barrier((crossed, inner))
    firsts = [
        move(jnp.where(core == 0, crossed[start : start + count], piece),
             lambda chip, core: (chip - 2, 0) if core == 0 else (chip + 2, 1),
             lambda chip, core: core == 1 or chip % 2 == 0)
        for start, count, piece in zip(starts, counts, pieces)
    ]
    carried = (inner,)
    for start, first, second in zip(starts, firsts, seconds):
        second, *carried = lax.optimization_barrier((second, *carried))
        other = move(second, across)
        rows = 288 if start == starts[-1] else 320
        state = call(functools.partial(chain_kernel, start), (rows, 128), flag, own, sibling, crossed, first, second,
                     other, *carried, name="half_chains")
        carried = (carried[0], state)
    partner = lax.ppermute(state, "pair", [(0, 1), (1, 0)])
    tile = call(meet_kernel, (8, 128), state, partner, name="meet")
    tile = call(join_kernel, (8, 128), tile, move(tile, across), name="join")
    tiles = [tile] + [move(tile, lambda chip, core: (chip + gap, core)) for gap in (1, -2)]
    spots = jnp.asarray([spot_table(core, samp, band) for core in range(2)], jnp.int32)
    spot = spots[lax.axis_index("blk") % 2, side]
    return call(pick_kernel, (1, (2 * band + 1) * samp), spot, *tiles, name="pick")


def solution(mesh):
    in_specs = (P("pair", None, "blk"),)
    out_specs = P(("blk", "pair"), None)
    return jax.shard_map(body, mesh=mesh, in_specs=in_specs, out_specs=out_specs, check_vma=False)
```

```python
import functools

import jax
import jax.numpy as jnp
from jax import lax
from jax.experimental import pallas as pl
from jax.experimental.pallas import tpu as pltpu
from jax.sharding import PartitionSpec as P

REACH = 6
EDGE = 6
SHARE = 0.63
BF16, F32 = jnp.bfloat16, jnp.float32
VMEM = pl.BlockSpec(memory_space=pltpu.VMEM)
SMEM = pl.BlockSpec(memory_space=pltpu.SMEM)


def move(array, source):
    peers = lax.axis_size("blk")
    chips = peers // 2
    pairs = []
    for d in range(peers):
        chip, core = source(d // 2, d % 2)
        pairs.append(((chip % chips) * 2 + core, d))
    return lax.ppermute(array, "blk", pairs)


def split(x):
    high = x.astype(BF16)
    return high, (x - high.astype(F32)).astype(BF16)


def product(left, right):
    return jnp.dot(left, right, preferred_element_type=F32)


def lane_slot(shape):
    return lax.broadcasted_iota(jnp.int32, shape, 1) // 32


def interleave(first, second):
    even = lane_slot(first.shape) % 2 == 0
    return (
        jnp.where(even, first, pltpu.roll(second, 32, 1)),
        jnp.where(even, pltpu.roll(first, 96, 1), second),
    )


def far_weights(tiles, flip):
    if flip:
        tiles = [jnp.concatenate([t] * 4, 0).T for t in tiles]
        blocks = [[t[32 * k : 32 * k + 32] for t in tiles] for k in range(4)]
    else:
        blocks = [tiles] * 4
    slot = lane_slot((32, 128))
    rows = [jnp.concatenate([jnp.where(slot == k, t, 0.0) for t in blocks[k]], 1) for k in range(4)]
    high, low = split(jnp.concatenate(rows, 0))
    return jnp.concatenate([high, high], 0), low


def near_turned(tiles):
    stack = jnp.concatenate([tiles[0], tiles[1], tiles[0], tiles[1]], 0).T
    return [stack[32 * k : 32 * k + 32] for k in (0, 2, 1, 3)]


def near_plain(tile):
    twice = pltpu.roll(tile, 64, 1)
    lower = lane_slot(tile.shape) < 2
    return [jnp.where(lower, tile, twice), jnp.where(lower, twice, tile)]


def spread(state, far):
    double, low = far
    high, rest = split(state)
    inner = product(jnp.concatenate([high, rest], 1), double) + product(high, low)
    return (*split(inner[:, :128]), *split(inner[:, 128:]))


def gather(inner, near):
    h0, l0, h1, l1 = inner
    results = []
    for k, tile in enumerate(near):
        rows = slice(32 * k, 32 * k + 32)
        weights = jnp.concatenate([h0[rows], h1[rows], l0[rows], l1[rows]], 0)
        both = product(jnp.concatenate(split(tile), 0), weights)
        results.append(both[:32] + both[32:])
    return jnp.concatenate(results, 0)


def identities(rows):
    row = lax.broadcasted_iota(jnp.int32, (rows, 128), 0) % 32
    lane = lax.broadcasted_iota(jnp.int32, (rows, 128), 1) % 32
    return jnp.where(row == lane, 1.0, 0.0)


def on_each_side(side_ref, run):
    for side in range(2):
        pl.when(side_ref[0] == side)(functools.partial(run, side == 1))


def turned(tile):
    stack = jnp.concatenate([tile] * 4, 0).T
    slot = lane_slot(tile.shape)
    result = stack[:32]
    for k in range(1, 4):
        result = jnp.where(slot == k, stack[32 * k : 32 * k + 32], result)
    return result


def edge_tile(tiles):
    slot = lane_slot((32, 128))
    row = lax.broadcasted_iota(jnp.int32, (32, 128), 0)
    current = jnp.broadcast_to(tiles[0][:1], (32, 128))
    for k, tile in enumerate(tiles[1:]):
        chosen = jnp.where(slot % 2 == (row >> k) % 2, current, 0.0)
        weights = [jnp.where(slot // 2 == n, tile, 0.0) for n in (0, 0, 1, 1)]
        current = jnp.dot(
            chosen,
            jnp.concatenate(weights, 0),
            precision=lax.Precision.HIGHEST,
            preferred_element_type=F32,
        )
    return current


def order_kernel(side_ref, sites_ref, whole, *pieces):
    sites = sites_ref.shape[0]

    def run(flip):
        def tile(k):
            return sites_ref[sites - 1 - k if flip else k]

        edge = edge_tile([turned(tile(k)) if flip else tile(k) for k in range(EDGE)])
        if flip:
            edge = turned(edge)
        at = 0
        for piece in pieces:
            for k in range(piece.shape[0]):
                value = edge if at == 0 else tile(at + EDGE - 1)
                piece[k] = value
                whole[at] = value
                at += 1

    on_each_side(side_ref, run)


def norms_only(state):
    slot = lane_slot((32, 128))
    first = jnp.where(slot == 0, state[192:224], state[224:256])
    second = jnp.where(slot == 1, state[256:288], state[288:320])
    kept = jnp.where(slot % 2 == 0, first, second)
    return jnp.concatenate([state[:192], kept], 0)


def home_kernel(side_ref, own, sibling, out):
    def run(flip):
        state = identities(64)
        for site in range(own.shape[0]):
            home = interleave(own[site], sibling[site])
            near = near_plain(own[site]) if flip else near_turned(home)[:2]
            state = gather(spread(state, far_weights(home, flip)), near)
        out[...] = state

    on_each_side(side_ref, run)


def chain_kernel(start, side_ref, own, sibling, first, second, other, home, *rest):
    out = rest[-1]
    count = first.shape[0]

    def run(flip):
        state = rest[0][...] if start else identities(320)
        groups = [state[:160], state[160:]]
        for index in range(count):
            whole = start + index
            far = interleave(first[index], second[index])
            if flip:
                near = [n for t in (own[whole], sibling[whole], other[index], first[index], second[index])
                        for n in near_plain(t)]
            else:
                extra = other[index]
                near = (
                    near_turned(interleave(own[whole], sibling[whole]))
                    + near_turned(interleave(extra, extra))[:2]
                    + near_turned(far)
                )
            weights = far_weights(far, flip)
            inner = [spread(g, weights) for g in groups]
            groups = [gather(i, near[5 * k : 5 * k + 5]) for k, i in enumerate(inner)]
        state = jnp.concatenate(groups, 0)
        last = start + count == own.shape[0]
        out[...] = jnp.concatenate([norms_only(state), home[...]], 0) if last else state

    on_each_side(side_ref, run)


def meet_kernel(mine, theirs, out):
    units = jnp.sum((mine[...] * theirs[...]).reshape(-1, 32, 128), 1)
    units = jnp.concatenate([units, jnp.zeros((16 - units.shape[0], 128), F32)], 0)
    row = lax.broadcasted_iota(jnp.int32, (8, 128), 0)
    chosen = jnp.where(row == lane_slot((8, 128)), 1.0, 0.0)
    found = lax.dot_general(
        chosen, units, (((1,), (1,)), ((), ())), precision=lax.Precision.HIGHEST, preferred_element_type=F32
    )
    out[...] = jnp.concatenate([found, jnp.zeros((8, 112), F32)], 1)


def join_kernel(mine, theirs, out):
    out[...] = mine[...] + pltpu.roll(theirs[...], 16, 1)


def pick_kernel(spot_ref, here, after, before, out):
    joined = here[...] + pltpu.roll(after[...], 32, 1) + pltpu.roll(before[...], 64, 1)
    unit = lax.broadcasted_iota(jnp.int32, (128, 128), 0)
    slot = lax.broadcasted_iota(jnp.int32, (8, 128), 0)
    values = []
    for k in range(3):
        spot = spot_ref[pl.ds(k, 1), :]
        chosen = jnp.where(unit == spot // 8, 1.0, 0.0)
        found = jnp.dot(joined, chosen, precision=lax.Precision.HIGHEST, preferred_element_type=F32)
        values.append(jnp.sum(jnp.where(slot == spot % 8, found, 0.0), 0, keepdims=True))
    tile, remote, own = values
    width = out.shape[1]
    out[...] = (tile * tile / (own * remote))[:, :width]


def find(core, near, far):
    mine, theirs = ("A0", "A1"), ("Z1", "Z0")
    if core == 1:
        mine, theirs = theirs, mine
    own, sibling = f"O{core}", f"O{1 - core}"
    if near == far and near in mine:
        return lambda n, m: (6, mine.index(near) + 2 * m)
    for base, rows, lanes in ((0, (own, sibling, theirs[1]), mine), (7, (own,), (own, sibling))):
        if near in rows and far in lanes:
            return lambda n, m: (base + 2 * rows.index(near) + n, lanes.index(far) + 2 * m)
        if far in rows and near in lanes:
            return lambda n, m: (base + 2 * rows.index(far) + m, lanes.index(near) + 2 * n)
    return None


def spot_table(core, samp, band):
    views = [(role, (k, k + 1) if core == 0 else (k + 1, k)) for k, role in ((0, "O"), (2, "A"), (4, "Z"))]
    shift = {"O": 0, "A": -1, "Z": 2}

    def place(offset, alone=False):
        chip, lane = (core + offset) // 2, (core + offset) % 2
        for role, messages in views:
            for name, gap in shift.items():
                if gap - shift[role] == chip:
                    goal = f"{name}{lane}"
                    for k, message in enumerate(messages):
                        got = find(k, goal if alone else f"{role}{core}", goal)
                        if got:
                            return message, got
        raise ValueError(offset)

    def code(where, n, m):
        message, got = where
        unit, slot = got(n, m)
        return 8 * (16 * message + unit) + slot

    offsets = range(-band, band + 1)
    table = []
    for n in range(samp):
        tile = [code(place(o), n, m) for o in offsets for m in range(samp)]
        remote = [code(place(o, True), m, m) for o in offsets for m in range(samp)]
        own = [code(place(0, True), n, n)] * len(tile)
        rows = [r + r[:1] * (128 - len(r)) for r in (tile, remote, own)]
        table.append(rows + rows[:1] * 5)
    return table


def call(kernel, shapes, *args, name):
    many = isinstance(shapes, list)
    shapes = [jax.ShapeDtypeStruct(shape, F32) for shape in (shapes if many else [shapes])]
    return pl.pallas_call(
        kernel,
        out_shape=shapes if many else shapes[0],
        in_specs=[SMEM if a.ndim == 1 else VMEM for a in args],
        out_specs=[VMEM] * len(shapes) if many else VMEM,
        compiler_params=pltpu.CompilerParams(vmem_limit_bytes=40 * 2**20),
        name=name,
    )(*args)


def body(mps):
    sites, chi = mps.shape[:2]
    samp = mps.shape[2] // (2 * chi)
    blocks = lax.axis_size("blk")
    band = min(REACH, (blocks - 1) // 2)
    side = lax.axis_index("pair")
    flag = side[None].astype(jnp.int32)

    steps = sites - EDGE + 1
    starts = [0, round(SHARE * steps)]
    counts = [starts[1], steps - starts[1]]
    tile = mps.shape[1:]
    mps, *pieces = call(order_kernel, [(n, *tile) for n in (steps, *counts)], flag, mps, name="order")
    seconds = [move(p, lambda chip, core: (chip - 1, 1) if core == 0 else (chip + 2, 0)) for p in pieces]
    firsts = [move(p, lambda chip, core: (chip - 1, 0) if core == 0 else (chip + 2, 1)) for p in pieces]
    across = lambda chip, core: (chip, 1 - core)
    sibling = move(mps, across)
    inner = call(home_kernel, (64, 128), flag, mps, sibling, name="own_chains")
    carried = (inner,)
    for start, first, second in zip(starts, firsts, seconds):
        second, *carried = lax.optimization_barrier((second, *carried))
        other = move(second, across)
        rows = 288 if start == starts[-1] else 320
        state = call(functools.partial(chain_kernel, start), (rows, 128), flag, mps, sibling, first, second, other,
                     *carried, name="half_chains")
        carried = (carried[0], state)
    partner = lax.ppermute(state, "pair", [(0, 1), (1, 0)])
    tile = call(meet_kernel, (8, 128), state, partner, name="meet")
    tile = call(join_kernel, (8, 128), tile, move(tile, across), name="join")
    tiles = [tile] + [move(tile, lambda chip, core: (chip + gap, core)) for gap in (1, -2)]
    spots = jnp.asarray([spot_table(core, samp, band) for core in range(2)], jnp.int32)
    spot = spots[lax.axis_index("blk") % 2, side]
    return call(pick_kernel, (1, (2 * band + 1) * samp), spot, *tiles, name="pick")


def solution(mesh):
    in_specs = (P("pair", None, "blk"),)
    out_specs = P(("blk", "pair"), None)
    return jax.shard_map(body, mesh=mesh, in_specs=in_specs, out_specs=out_specs, check_vma=False)
```

```python
import functools

import jax
import jax.numpy as jnp
from jax import lax
from jax.experimental import pallas as pl
from jax.experimental.pallas import tpu as pltpu
from jax.sharding import PartitionSpec as P

REACH = 6
EDGE = 6
SHARE = 0.7
BF16, F32 = jnp.bfloat16, jnp.float32
VMEM = pl.BlockSpec(memory_space=pltpu.VMEM)
SMEM = pl.BlockSpec(memory_space=pltpu.SMEM)


def move(array, source):
    peers = lax.axis_size("blk")
    chips = peers // 2
    pairs = []
    for d in range(peers):
        chip, core = source(d // 2, d % 2)
        pairs.append(((chip % chips) * 2 + core, d))
    return lax.ppermute(array, "blk", pairs)


def split(x):
    high = x.astype(BF16)
    return high, (x - high.astype(F32)).astype(BF16)


def product(left, right):
    return jnp.dot(left, right, preferred_element_type=F32)


def lane_slot(shape):
    return lax.broadcasted_iota(jnp.int32, shape, 1) // 32


def interleave(first, second):
    even = lane_slot(first.shape) % 2 == 0
    return (
        jnp.where(even, first, pltpu.roll(second, 32, 1)),
        jnp.where(even, pltpu.roll(first, 96, 1), second),
    )


def far_weights(tiles, flip):
    if flip:
        tiles = [jnp.concatenate([t] * 4, 0).T for t in tiles]
        blocks = [[t[32 * k : 32 * k + 32] for t in tiles] for k in range(4)]
    else:
        blocks = [tiles] * 4
    slot = lane_slot((32, 128))
    rows = [jnp.concatenate([jnp.where(slot == k, t, 0.0) for t in blocks[k]], 1) for k in range(4)]
    high, low = split(jnp.concatenate(rows, 0))
    return jnp.concatenate([high, high], 0), low


def near_turned(tiles):
    stack = jnp.concatenate([tiles[0], tiles[1], tiles[0], tiles[1]], 0).T
    return [stack[32 * k : 32 * k + 32] for k in (0, 2, 1, 3)]


def near_plain(tile):
    twice = pltpu.roll(tile, 64, 1)
    lower = lane_slot(tile.shape) < 2
    return [jnp.where(lower, tile, twice), jnp.where(lower, twice, tile)]


def spread(state, far):
    double, low = far
    high, rest = split(state)
    inner = product(jnp.concatenate([high, rest], 1), double) + product(high, low)
    return (*split(inner[:, :128]), *split(inner[:, 128:]))


def gather(inner, near):
    h0, l0, h1, l1 = inner
    results = []
    for k, tile in enumerate(near):
        rows = slice(32 * k, 32 * k + 32)
        weights = jnp.concatenate([h0[rows], h1[rows], l0[rows], l1[rows]], 0)
        both = product(jnp.concatenate(split(tile), 0), weights)
        results.append(both[:32] + both[32:])
    return jnp.concatenate(results, 0)


def identities(rows):
    row = lax.broadcasted_iota(jnp.int32, (rows, 128), 0) % 32
    lane = lax.broadcasted_iota(jnp.int32, (rows, 128), 1) % 32
    return jnp.where(row == lane, 1.0, 0.0)


def on_each_side(side_ref, run):
    for side in range(2):
        pl.when(side_ref[0] == side)(functools.partial(run, side == 1))


def turned(tile):
    stack = jnp.concatenate([tile] * 4, 0).T
    slot = lane_slot(tile.shape)
    result = stack[:32]
    for k in range(1, 4):
        result = jnp.where(slot == k, stack[32 * k : 32 * k + 32], result)
    return result


def edge_tile(tiles):
    slot = lane_slot((32, 128))
    row = lax.broadcasted_iota(jnp.int32, (32, 128), 0)
    current = jnp.broadcast_to(tiles[0][:1], (32, 128))
    for k, tile in enumerate(tiles[1:]):
        chosen = jnp.where(slot % 2 == (row >> k) % 2, current, 0.0)
        weights = [jnp.where(slot // 2 == n, tile, 0.0) for n in (0, 0, 1, 1)]
        current = jnp.dot(
            chosen,
            jnp.concatenate(weights, 0),
            precision=lax.Precision.HIGHEST,
            preferred_element_type=F32,
        )
    return current


def order_kernel(side_ref, sites_ref, whole, *pieces):
    sites = sites_ref.shape[0]

    def run(flip):
        def tile(k):
            return sites_ref[sites - 1 - k if flip else k]

        edge = edge_tile([turned(tile(k)) if flip else tile(k) for k in range(EDGE)])
        if flip:
            edge = turned(edge)
        at = 0
        for piece in pieces:
            for k in range(piece.shape[0]):
                value = edge if at == 0 else tile(at + EDGE - 1)
                piece[k] = value
                whole[at] = value
                at += 1

    on_each_side(side_ref, run)


def norms_only(state):
    slot = lane_slot((32, 128))
    first = jnp.where(slot == 0, state[192:224], state[224:256])
    second = jnp.where(slot == 1, state[256:288], state[288:320])
    kept = jnp.where(slot % 2 == 0, first, second)
    return jnp.concatenate([state[:192], kept], 0)


def home_kernel(side_ref, own, sibling, out):
    def run(flip):
        state = identities(64)
        for site in range(own.shape[0]):
            home = interleave(own[site], sibling[site])
            near = near_plain(own[site]) if flip else near_turned(home)[:2]
            state = gather(spread(state, far_weights(home, flip)), near)
        out[...] = state

    on_each_side(side_ref, run)


def chain_kernel(start, side_ref, own, sibling, first, second, other, home, *rest):
    out = rest[-1]
    count = first.shape[0]

    def run(flip):
        state = rest[0][...] if start else identities(320)
        groups = [state[:160], state[160:]]
        for index in range(count):
            whole = start + index
            far = interleave(first[index], second[index])
            if flip:
                near = [n for t in (own[whole], sibling[whole], other[index], first[index], second[index])
                        for n in near_plain(t)]
            else:
                extra = other[index]
                near = (
                    near_turned(interleave(own[whole], sibling[whole]))
                    + near_turned(interleave(extra, extra))[:2]
                    + near_turned(far)
                )
            weights = far_weights(far, flip)
            inner = [spread(g, weights) for g in groups]
            groups = [gather(i, near[5 * k : 5 * k + 5]) for k, i in enumerate(inner)]
        state = jnp.concatenate(groups, 0)
        last = start + count == own.shape[0]
        out[...] = jnp.concatenate([norms_only(state), home[...]], 0) if last else state

    on_each_side(side_ref, run)


def meet_kernel(mine, theirs, out):
    units = jnp.sum((mine[...] * theirs[...]).reshape(-1, 32, 128), 1)
    units = jnp.concatenate([units, jnp.zeros((16 - units.shape[0], 128), F32)], 0)
    row = lax.broadcasted_iota(jnp.int32, (8, 128), 0)
    chosen = jnp.where(row == lane_slot((8, 128)), 1.0, 0.0)
    found = lax.dot_general(
        chosen, units, (((1,), (1,)), ((), ())), precision=lax.Precision.HIGHEST, preferred_element_type=F32
    )
    out[...] = jnp.concatenate([found, jnp.zeros((8, 112), F32)], 1)


def join_kernel(mine, theirs, out):
    out[...] = mine[...] + pltpu.roll(theirs[...], 16, 1)


def pick_kernel(spot_ref, here, after, before, out):
    joined = here[...] + pltpu.roll(after[...], 32, 1) + pltpu.roll(before[...], 64, 1)
    unit = lax.broadcasted_iota(jnp.int32, (128, 128), 0)
    slot = lax.broadcasted_iota(jnp.int32, (8, 128), 0)
    values = []
    for k in range(3):
        spot = spot_ref[pl.ds(k, 1), :]
        chosen = jnp.where(unit == spot // 8, 1.0, 0.0)
        found = jnp.dot(joined, chosen, precision=lax.Precision.HIGHEST, preferred_element_type=F32)
        values.append(jnp.sum(jnp.where(slot == spot % 8, found, 0.0), 0, keepdims=True))
    tile, remote, own = values
    width = out.shape[1]
    out[...] = (tile * tile / (own * remote))[:, :width]


def find(core, near, far):
    mine, theirs = ("A0", "A1"), ("Z1", "Z0")
    if core == 1:
        mine, theirs = theirs, mine
    own, sibling = f"O{core}", f"O{1 - core}"
    if near == far and near in mine:
        return lambda n, m: (6, mine.index(near) + 2 * m)
    for base, rows, lanes in ((0, (own, sibling, theirs[1]), mine), (7, (own,), (own, sibling))):
        if near in rows and far in lanes:
            return lambda n, m: (base + 2 * rows.index(near) + n, lanes.index(far) + 2 * m)
        if far in rows and near in lanes:
            return lambda n, m: (base + 2 * rows.index(far) + m, lanes.index(near) + 2 * n)
    return None


def spot_table(core, samp, band):
    views = [(role, (k, k + 1) if core == 0 else (k + 1, k)) for k, role in ((0, "O"), (2, "A"), (4, "Z"))]
    shift = {"O": 0, "A": -1, "Z": 2}

    def place(offset, alone=False):
        chip, lane = (core + offset) // 2, (core + offset) % 2
        for role, messages in views:
            for name, gap in shift.items():
                if gap - shift[role] == chip:
                    goal = f"{name}{lane}"
                    for k, message in enumerate(messages):
                        got = find(k, goal if alone else f"{role}{core}", goal)
                        if got:
                            return message, got
        raise ValueError(offset)

    def code(where, n, m):
        message, got = where
        unit, slot = got(n, m)
        return 8 * (16 * message + unit) + slot

    offsets = range(-band, band + 1)
    table = []
    for n in range(samp):
        tile = [code(place(o), n, m) for o in offsets for m in range(samp)]
        remote = [code(place(o, True), m, m) for o in offsets for m in range(samp)]
        own = [code(place(0, True), n, n)] * len(tile)
        rows = [r + r[:1] * (128 - len(r)) for r in (tile, remote, own)]
        table.append(rows + rows[:1] * 5)
    return table


def call(kernel, shapes, *args, name):
    many = isinstance(shapes, list)
    shapes = [jax.ShapeDtypeStruct(shape, F32) for shape in (shapes if many else [shapes])]
    return pl.pallas_call(
        kernel,
        out_shape=shapes if many else shapes[0],
        in_specs=[SMEM if a.ndim == 1 else VMEM for a in args],
        out_specs=[VMEM] * len(shapes) if many else VMEM,
        compiler_params=pltpu.CompilerParams(vmem_limit_bytes=40 * 2**20),
        name=name,
    )(*args)


def body(mps):
    sites, chi = mps.shape[:2]
    samp = mps.shape[2] // (2 * chi)
    blocks = lax.axis_size("blk")
    band = min(REACH, (blocks - 1) // 2)
    side = lax.axis_index("pair")
    flag = side[None].astype(jnp.int32)

    steps = sites - EDGE + 1
    starts = [0, round(SHARE * steps)]
    counts = [starts[1], steps - starts[1]]
    tile = mps.shape[1:]
    mps, *pieces = call(order_kernel, [(n, *tile) for n in (steps, *counts)], flag, mps, name="order")
    seconds = [move(p, lambda chip, core: (chip - 1, 1) if core == 0 else (chip + 2, 0)) for p in pieces]
    firsts = [move(p, lambda chip, core: (chip - 1, 0) if core == 0 else (chip + 2, 1)) for p in pieces]
    across = lambda chip, core: (chip, 1 - core)
    sibling = move(mps, across)
    inner = call(home_kernel, (64, 128), flag, mps, sibling, name="own_chains")
    spots = jnp.asarray([spot_table(core, samp, band) for core in range(2)], jnp.int32)
    spot = spots[lax.axis_index("blk") % 2, side]
    inner, spot = lax.optimization_barrier((inner, spot))
    carried = (inner,)
    for start, first, second in zip(starts, firsts, seconds):
        second, *carried = lax.optimization_barrier((second, *carried))
        other = move(second, across)
        rows = 288 if start == starts[-1] else 320
        state = call(functools.partial(chain_kernel, start), (rows, 128), flag, mps, sibling, first, second, other,
                     *carried, name="half_chains")
        carried = (carried[0], state)
    partner = lax.ppermute(state, "pair", [(0, 1), (1, 0)])
    tile = call(meet_kernel, (8, 128), state, partner, name="meet")
    tile = call(join_kernel, (8, 128), tile, move(tile, across), name="join")
    tiles = [tile] + [move(tile, lambda chip, core: (chip + gap, core)) for gap in (1, -2)]
    return call(pick_kernel, (1, (2 * band + 1) * samp), spot, *tiles, name="pick")


def solution(mesh):
    in_specs = (P("pair", None, "blk"),)
    out_specs = P(("blk", "pair"), None)
    return jax.shard_map(body, mesh=mesh, in_specs=in_specs, out_specs=out_specs, check_vma=False)
```

```python
import functools

import jax
import jax.numpy as jnp
from jax import lax
from jax.experimental import pallas as pl
from jax.experimental.pallas import tpu as pltpu
from jax.sharding import PartitionSpec as P

REACH = 6
EDGE = 6
SHARE = 0.63
BF16, F32 = jnp.bfloat16, jnp.float32
VMEM = pl.BlockSpec(memory_space=pltpu.VMEM)
SMEM = pl.BlockSpec(memory_space=pltpu.SMEM)


def move(array, source):
    peers = lax.axis_size("blk")
    chips = peers // 2
    pairs = []
    for d in range(peers):
        chip, core = source(d // 2, d % 2)
        pairs.append(((chip % chips) * 2 + core, d))
    return lax.ppermute(array, "blk", pairs)


def split(x):
    high = x.astype(BF16)
    return high, (x - high.astype(F32)).astype(BF16)


def product(left, right):
    return jnp.dot(left, right, preferred_element_type=F32)


def lane_slot(shape):
    return lax.broadcasted_iota(jnp.int32, shape, 1) // 32


def interleave(first, second):
    even = lane_slot(first.shape) % 2 == 0
    return (
        jnp.where(even, first, pltpu.roll(second, 32, 1)),
        jnp.where(even, pltpu.roll(first, 96, 1), second),
    )


def far_weights(tiles, flip):
    if flip:
        tiles = [jnp.concatenate([t] * 4, 0).T for t in tiles]
        blocks = [[t[32 * k : 32 * k + 32] for t in tiles] for k in range(4)]
    else:
        blocks = [tiles] * 4
    slot = lane_slot((32, 128))
    rows = [jnp.concatenate([jnp.where(slot == k, t, 0.0) for t in blocks[k]], 1) for k in range(4)]
    high, low = split(jnp.concatenate(rows, 0))
    return jnp.concatenate([high, high], 0), low


def near_turned(tiles):
    stack = jnp.concatenate([tiles[0], tiles[1], tiles[0], tiles[1]], 0).T
    return [stack[32 * k : 32 * k + 32] for k in (0, 2, 1, 3)]


def near_plain(tile):
    twice = pltpu.roll(tile, 64, 1)
    lower = lane_slot(tile.shape) < 2
    return [jnp.where(lower, tile, twice), jnp.where(lower, twice, tile)]


def spread(state, far):
    double, low = far
    high, rest = split(state)
    inner = product(jnp.concatenate([high, rest], 1), double) + product(high, low)
    return (*split(inner[:, :128]), *split(inner[:, 128:]))


def gather(inner, near):
    h0, l0, h1, l1 = inner
    results = []
    for k, tile in enumerate(near):
        rows = slice(32 * k, 32 * k + 32)
        weights = jnp.concatenate([h0[rows], h1[rows], l0[rows], l1[rows]], 0)
        both = product(jnp.concatenate(split(tile), 0), weights)
        results.append(both[:32] + both[32:])
    return jnp.concatenate(results, 0)


def identities(rows):
    row = lax.broadcasted_iota(jnp.int32, (rows, 128), 0) % 32
    lane = lax.broadcasted_iota(jnp.int32, (rows, 128), 1) % 32
    return jnp.where(row == lane, 1.0, 0.0)


def on_each_side(side_ref, run):
    for side in range(2):
        pl.when(side_ref[0] == side)(functools.partial(run, side == 1))


def turned(tile):
    stack = jnp.concatenate([tile] * 4, 0).T
    slot = lane_slot(tile.shape)
    result = stack[:32]
    for k in range(1, 4):
        result = jnp.where(slot == k, stack[32 * k : 32 * k + 32], result)
    return result


def edge_tile(tiles):
    slot = lane_slot((32, 128))
    row = lax.broadcasted_iota(jnp.int32, (32, 128), 0)
    current = jnp.broadcast_to(tiles[0][:1], (32, 128))
    for k, tile in enumerate(tiles[1:]):
        chosen = jnp.where(slot % 2 == (row >> k) % 2, current, 0.0)
        weights = [jnp.where(slot // 2 == n, tile, 0.0) for n in (0, 0, 1, 1)]
        current = jnp.dot(
            chosen,
            jnp.concatenate(weights, 0),
            precision=lax.Precision.HIGHEST,
            preferred_element_type=F32,
        )
    return current


def order_kernel(side_ref, sites_ref, whole, *pieces):
    sites = sites_ref.shape[0]

    def run(flip):
        def tile(k):
            return sites_ref[sites - 1 - k if flip else k]

        edge = edge_tile([turned(tile(k)) if flip else tile(k) for k in range(EDGE)])
        if flip:
            edge = turned(edge)
        at = 0
        for piece in pieces:
            for k in range(piece.shape[0]):
                value = edge if at == 0 else tile(at + EDGE - 1)
                piece[k] = value
                whole[at] = value
                at += 1

    on_each_side(side_ref, run)


def norms_only(state):
    slot = lane_slot((32, 128))
    first = jnp.where(slot == 0, state[192:224], state[224:256])
    second = jnp.where(slot == 1, state[256:288], state[288:320])
    kept = jnp.where(slot % 2 == 0, first, second)
    return jnp.concatenate([state[:192], kept], 0)


def home_kernel(side_ref, own, sibling, out):
    def run(flip):
        state = identities(64)
        for site in range(own.shape[0]):
            home = interleave(own[site], sibling[site])
            near = near_plain(own[site]) if flip else near_turned(home)[:2]
            state = gather(spread(state, far_weights(home, flip)), near)
        out[...] = state

    on_each_side(side_ref, run)


def chain_kernel(start, side_ref, own, sibling, first, second, other, home, *rest):
    out = rest[-1]
    count = first.shape[0]

    def run(flip):
        state = rest[0][...] if start else identities(320)
        cuts = (0, 4, 7, 10)
        groups = [state[32 * a : 32 * b] for a, b in zip(cuts, cuts[1:])]
        for index in range(count):
            whole = start + index
            far = interleave(first[index], second[index])
            if flip:
                near = [n for t in (own[whole], sibling[whole], other[index], first[index], second[index])
                        for n in near_plain(t)]
            else:
                extra = other[index]
                near = (
                    near_turned(interleave(own[whole], sibling[whole]))
                    + near_turned(interleave(extra, extra))[:2]
                    + near_turned(far)
                )
            weights = far_weights(far, flip)
            inner = [spread(g, weights) for g in groups]
            groups = [gather(i, near[a:b]) for i, a, b in zip(inner, cuts, cuts[1:])]
        state = jnp.concatenate(groups, 0)
        last = start + count == own.shape[0]
        out[...] = jnp.concatenate([norms_only(state), home[...]], 0) if last else state

    on_each_side(side_ref, run)


def meet_kernel(mine, theirs, out):
    units = jnp.sum((mine[...] * theirs[...]).reshape(-1, 32, 128), 1)
    units = jnp.concatenate([units, jnp.zeros((16 - units.shape[0], 128), F32)], 0)
    row = lax.broadcasted_iota(jnp.int32, (8, 128), 0)
    chosen = jnp.where(row == lane_slot((8, 128)), 1.0, 0.0)
    found = lax.dot_general(
        chosen, units, (((1,), (1,)), ((), ())), precision=lax.Precision.HIGHEST, preferred_element_type=F32
    )
    out[...] = jnp.concatenate([found, jnp.zeros((8, 112), F32)], 1)


def join_kernel(mine, theirs, out):
    out[...] = mine[...] + pltpu.roll(theirs[...], 16, 1)


def pick_kernel(spot_ref, here, after, before, out):
    joined = here[...] + pltpu.roll(after[...], 32, 1) + pltpu.roll(before[...], 64, 1)
    unit = lax.broadcasted_iota(jnp.int32, (128, 128), 0)
    slot = lax.broadcasted_iota(jnp.int32, (8, 128), 0)
    values = []
    for k in range(3):
        spot = spot_ref[pl.ds(k, 1), :]
        chosen = jnp.where(unit == spot // 8, 1.0, 0.0)
        found = jnp.dot(joined, chosen, precision=lax.Precision.HIGHEST, preferred_element_type=F32)
        values.append(jnp.sum(jnp.where(slot == spot % 8, found, 0.0), 0, keepdims=True))
    tile, remote, own = values
    width = out.shape[1]
    out[...] = (tile * tile / (own * remote))[:, :width]


def find(core, near, far):
    mine, theirs = ("A0", "A1"), ("Z1", "Z0")
    if core == 1:
        mine, theirs = theirs, mine
    own, sibling = f"O{core}", f"O{1 - core}"
    if near == far and near in mine:
        return lambda n, m: (6, mine.index(near) + 2 * m)
    for base, rows, lanes in ((0, (own, sibling, theirs[1]), mine), (7, (own,), (own, sibling))):
        if near in rows and far in lanes:
            return lambda n, m: (base + 2 * rows.index(near) + n, lanes.index(far) + 2 * m)
        if far in rows and near in lanes:
            return lambda n, m: (base + 2 * rows.index(far) + m, lanes.index(near) + 2 * n)
    return None


def spot_table(core, samp, band):
    views = [(role, (k, k + 1) if core == 0 else (k + 1, k)) for k, role in ((0, "O"), (2, "A"), (4, "Z"))]
    shift = {"O": 0, "A": -1, "Z": 2}

    def place(offset, alone=False):
        chip, lane = (core + offset) // 2, (core + offset) % 2
        for role, messages in views:
            for name, gap in shift.items():
                if gap - shift[role] == chip:
                    goal = f"{name}{lane}"
                    for k, message in enumerate(messages):
                        got = find(k, goal if alone else f"{role}{core}", goal)
                        if got:
                            return message, got
        raise ValueError(offset)

    def code(where, n, m):
        message, got = where
        unit, slot = got(n, m)
        return 8 * (16 * message + unit) + slot

    offsets = range(-band, band + 1)
    table = []
    for n in range(samp):
        tile = [code(place(o), n, m) for o in offsets for m in range(samp)]
        remote = [code(place(o, True), m, m) for o in offsets for m in range(samp)]
        own = [code(place(0, True), n, n)] * len(tile)
        rows = [r + r[:1] * (128 - len(r)) for r in (tile, remote, own)]
        table.append(rows + rows[:1] * 5)
    return table


def call(kernel, shapes, *args, name):
    many = isinstance(shapes, list)
    shapes = [jax.ShapeDtypeStruct(shape, F32) for shape in (shapes if many else [shapes])]
    return pl.pallas_call(
        kernel,
        out_shape=shapes if many else shapes[0],
        in_specs=[SMEM if a.ndim == 1 else VMEM for a in args],
        out_specs=[VMEM] * len(shapes) if many else VMEM,
        compiler_params=pltpu.CompilerParams(vmem_limit_bytes=40 * 2**20),
        name=name,
    )(*args)


def body(mps):
    sites, chi = mps.shape[:2]
    samp = mps.shape[2] // (2 * chi)
    blocks = lax.axis_size("blk")
    band = min(REACH, (blocks - 1) // 2)
    side = lax.axis_index("pair")
    flag = side[None].astype(jnp.int32)

    steps = sites - EDGE + 1
    starts = [0, round(SHARE * steps)]
    counts = [starts[1], steps - starts[1]]
    tile = mps.shape[1:]
    mps, *pieces = call(order_kernel, [(n, *tile) for n in (steps, *counts)], flag, mps, name="order")
    seconds = [move(p, lambda chip, core: (chip - 1, 1) if core == 0 else (chip + 2, 0)) for p in pieces]
    firsts = [move(p, lambda chip, core: (chip - 1, 0) if core == 0 else (chip + 2, 1)) for p in pieces]
    across = lambda chip, core: (chip, 1 - core)
    sibling = move(mps, across)
    inner = call(home_kernel, (64, 128), flag, mps, sibling, name="own_chains")
    spots = jnp.asarray([spot_table(core, samp, band) for core in range(2)], jnp.int32)
    spot = spots[lax.axis_index("blk") % 2, side]
    inner, spot = lax.optimization_barrier((inner, spot))
    carried = (inner,)
    for start, first, second in zip(starts, firsts, seconds):
        second, *carried = lax.optimization_barrier((second, *carried))
        other = move(second, across)
        rows = 288 if start == starts[-1] else 320
        state = call(functools.partial(chain_kernel, start), (rows, 128), flag, mps, sibling, first, second, other,
                     *carried, name="half_chains")
        carried = (carried[0], state)
    partner = lax.ppermute(state, "pair", [(0, 1), (1, 0)])
    tile = call(meet_kernel, (8, 128), state, partner, name="meet")
    tile = call(join_kernel, (8, 128), tile, move(tile, across), name="join")
    tiles = [tile] + [move(tile, lambda chip, core: (chip + gap, core)) for gap in (1, -2)]
    return call(pick_kernel, (1, (2 * band + 1) * samp), spot, *tiles, name="pick")


def solution(mesh):
    in_specs = (P("pair", None, "blk"),)
    out_specs = P(("blk", "pair"), None)
    return jax.shard_map(body, mesh=mesh, in_specs=in_specs, out_specs=out_specs, check_vma=False)
```

```python
import functools

import jax
import jax.numpy as jnp
from jax import lax
from jax.experimental import pallas as pl
from jax.experimental.pallas import tpu as pltpu
from jax.sharding import PartitionSpec as P

REACH = 6
EDGE = 6
SHARE = 0.63
BF16, F32 = jnp.bfloat16, jnp.float32
VMEM = pl.BlockSpec(memory_space=pltpu.VMEM)
SMEM = pl.BlockSpec(memory_space=pltpu.SMEM)


def move(array, source):
    peers = lax.axis_size("blk")
    chips = peers // 2
    pairs = []
    for d in range(peers):
        chip, core = source(d // 2, d % 2)
        pairs.append(((chip % chips) * 2 + core, d))
    return lax.ppermute(array, "blk", pairs)


def split(x):
    high = x.astype(BF16)
    return high, (x - high.astype(F32)).astype(BF16)


def product(left, right):
    return jnp.dot(left, right, preferred_element_type=F32)


def lane_slot(shape):
    return lax.broadcasted_iota(jnp.int32, shape, 1) // 32


def interleave(first, second):
    even = lane_slot(first.shape) % 2 == 0
    return (
        jnp.where(even, first, pltpu.roll(second, 32, 1)),
        jnp.where(even, pltpu.roll(first, 96, 1), second),
    )


def far_weights(tiles, flip):
    if flip:
        tiles = [jnp.concatenate([t] * 4, 0).T for t in tiles]
        blocks = [[t[32 * k : 32 * k + 32] for t in tiles] for k in range(4)]
    else:
        blocks = [tiles] * 4
    slot = lane_slot((32, 128))
    rows = [jnp.concatenate([jnp.where(slot == k, t, 0.0) for t in blocks[k]], 1) for k in range(4)]
    high, low = split(jnp.concatenate(rows, 0))
    return jnp.concatenate([high, high], 0), low


def near_turned(tiles):
    stack = jnp.concatenate([tiles[0], tiles[1], tiles[0], tiles[1]], 0).T
    return [stack[32 * k : 32 * k + 32] for k in (0, 2, 1, 3)]


def near_plain(tile):
    twice = pltpu.roll(tile, 64, 1)
    lower = lane_slot(tile.shape) < 2
    return [jnp.where(lower, tile, twice), jnp.where(lower, twice, tile)]


def spread(state, far):
    double, low = far
    high, rest = split(state)
    inner = product(jnp.concatenate([high, rest], 1), double) + product(high, low)
    return (*split(inner[:, :128]), *split(inner[:, 128:]))


def gather(inner, near):
    h0, l0, h1, l1 = inner
    results = []
    for k, tile in enumerate(near):
        rows = slice(32 * k, 32 * k + 32)
        weights = jnp.concatenate([h0[rows], h1[rows], l0[rows], l1[rows]], 0)
        both = product(jnp.concatenate(split(tile), 0), weights)
        results.append(both[:32] + both[32:])
    return jnp.concatenate(results, 0)


def identities(rows):
    row = lax.broadcasted_iota(jnp.int32, (rows, 128), 0) % 32
    lane = lax.broadcasted_iota(jnp.int32, (rows, 128), 1) % 32
    return jnp.where(row == lane, 1.0, 0.0)


def on_each_side(side_ref, run):
    for side in range(2):
        pl.when(side_ref[0] == side)(functools.partial(run, side == 1))


def turned(tile):
    stack = jnp.concatenate([tile] * 4, 0).T
    slot = lane_slot(tile.shape)
    result = stack[:32]
    for k in range(1, 4):
        result = jnp.where(slot == k, stack[32 * k : 32 * k + 32], result)
    return result


def edge_tile(tiles):
    slot = lane_slot((32, 128))
    row = lax.broadcasted_iota(jnp.int32, (32, 128), 0)
    current = jnp.broadcast_to(tiles[0][:1], (32, 128))
    for k, tile in enumerate(tiles[1:]):
        chosen = jnp.where(slot % 2 == (row >> k) % 2, current, 0.0)
        weights = [jnp.where(slot // 2 == n, tile, 0.0) for n in (0, 0, 1, 1)]
        current = jnp.dot(
            chosen,
            jnp.concatenate(weights, 0),
            precision=lax.Precision.HIGHEST,
            preferred_element_type=F32,
        )
    return current


def order_kernel(side_ref, sites_ref, whole, *pieces):
    sites = sites_ref.shape[0]

    def run(flip):
        def tile(k):
            return sites_ref[sites - 1 - k if flip else k]

        edge = edge_tile([turned(tile(k)) if flip else tile(k) for k in range(EDGE)])
        if flip:
            edge = turned(edge)
        at = 0
        for piece in pieces:
            for k in range(piece.shape[0]):
                value = edge if at == 0 else tile(at + EDGE - 1)
                piece[k] = value
                whole[at] = value
                at += 1

    on_each_side(side_ref, run)


def norms_only(state):
    slot = lane_slot((32, 128))
    first = jnp.where(slot == 0, state[192:224], state[224:256])
    second = jnp.where(slot == 1, state[256:288], state[288:320])
    kept = jnp.where(slot % 2 == 0, first, second)
    return jnp.concatenate([state[:192], kept], 0)


def home_kernel(side_ref, own, sibling, out):
    def run(flip):
        state = identities(64)
        for site in range(own.shape[0]):
            home = interleave(own[site], sibling[site])
            near = near_plain(own[site]) if flip else near_turned(home)[:2]
            state = gather(spread(state, far_weights(home, flip)), near)
        out[...] = state

    on_each_side(side_ref, run)


def chain_kernel(start, side_ref, own, sibling, first, second, other, home, *rest):
    out = rest[-1]
    count = first.shape[0]

    def run(flip):
        state = rest[0][...] if start else identities(320)
        cuts = (0, 10)
        groups = [state[32 * a : 32 * b] for a, b in zip(cuts, cuts[1:])]
        for index in range(count):
            whole = start + index
            far = interleave(first[index], second[index])
            if flip:
                near = [n for t in (own[whole], sibling[whole], other[index], first[index], second[index])
                        for n in near_plain(t)]
            else:
                extra = other[index]
                near = (
                    near_turned(interleave(own[whole], sibling[whole]))
                    + near_turned(interleave(extra, extra))[:2]
                    + near_turned(far)
                )
            weights = far_weights(far, flip)
            inner = [spread(g, weights) for g in groups]
            groups = [gather(i, near[a:b]) for i, a, b in zip(inner, cuts, cuts[1:])]
        state = jnp.concatenate(groups, 0)
        last = start + count == own.shape[0]
        out[...] = jnp.concatenate([norms_only(state), home[...]], 0) if last else state

    on_each_side(side_ref, run)


def meet_kernel(mine, theirs, out):
    units = jnp.sum((mine[...] * theirs[...]).reshape(-1, 32, 128), 1)
    units = jnp.concatenate([units, jnp.zeros((16 - units.shape[0], 128), F32)], 0)
    row = lax.broadcasted_iota(jnp.int32, (8, 128), 0)
    chosen = jnp.where(row == lane_slot((8, 128)), 1.0, 0.0)
    found = lax.dot_general(
        chosen, units, (((1,), (1,)), ((), ())), precision=lax.Precision.HIGHEST, preferred_element_type=F32
    )
    out[...] = jnp.concatenate([found, jnp.zeros((8, 112), F32)], 1)


def join_kernel(mine, theirs, out):
    out[...] = mine[...] + pltpu.roll(theirs[...], 16, 1)


def pick_kernel(spot_ref, here, after, before, out):
    joined = here[...] + pltpu.roll(after[...], 32, 1) + pltpu.roll(before[...], 64, 1)
    unit = lax.broadcasted_iota(jnp.int32, (128, 128), 0)
    slot = lax.broadcasted_iota(jnp.int32, (8, 128), 0)
    values = []
    for k in range(3):
        spot = spot_ref[pl.ds(k, 1), :]
        chosen = jnp.where(unit == spot // 8, 1.0, 0.0)
        found = jnp.dot(joined, chosen, precision=lax.Precision.HIGHEST, preferred_element_type=F32)
        values.append(jnp.sum(jnp.where(slot == spot % 8, found, 0.0), 0, keepdims=True))
    tile, remote, own = values
    width = out.shape[1]
    out[...] = (tile * tile / (own * remote))[:, :width]


def find(core, near, far):
    mine, theirs = ("A0", "A1"), ("Z1", "Z0")
    if core == 1:
        mine, theirs = theirs, mine
    own, sibling = f"O{core}", f"O{1 - core}"
    if near == far and near in mine:
        return lambda n, m: (6, mine.index(near) + 2 * m)
    for base, rows, lanes in ((0, (own, sibling, theirs[1]), mine), (7, (own,), (own, sibling))):
        if near in rows and far in lanes:
            return lambda n, m: (base + 2 * rows.index(near) + n, lanes.index(far) + 2 * m)
        if far in rows and near in lanes:
            return lambda n, m: (base + 2 * rows.index(far) + m, lanes.index(near) + 2 * n)
    return None


def spot_table(core, samp, band):
    views = [(role, (k, k + 1) if core == 0 else (k + 1, k)) for k, role in ((0, "O"), (2, "A"), (4, "Z"))]
    shift = {"O": 0, "A": -1, "Z": 2}

    def place(offset, alone=False):
        chip, lane = (core + offset) // 2, (core + offset) % 2
        for role, messages in views:
            for name, gap in shift.items():
                if gap - shift[role] == chip:
                    goal = f"{name}{lane}"
                    for k, message in enumerate(messages):
                        got = find(k, goal if alone else f"{role}{core}", goal)
                        if got:
                            return message, got
        raise ValueError(offset)

    def code(where, n, m):
        message, got = where
        unit, slot = got(n, m)
        return 8 * (16 * message + unit) + slot

    offsets = range(-band, band + 1)
    table = []
    for n in range(samp):
        tile = [code(place(o), n, m) for o in offsets for m in range(samp)]
        remote = [code(place(o, True), m, m) for o in offsets for m in range(samp)]
        own = [code(place(0, True), n, n)] * len(tile)
        rows = [r + r[:1] * (128 - len(r)) for r in (tile, remote, own)]
        table.append(rows + rows[:1] * 5)
    return table


def call(kernel, shapes, *args, name):
    many = isinstance(shapes, list)
    shapes = [jax.ShapeDtypeStruct(shape, F32) for shape in (shapes if many else [shapes])]
    return pl.pallas_call(
        kernel,
        out_shape=shapes if many else shapes[0],
        in_specs=[SMEM if a.ndim == 1 else VMEM for a in args],
        out_specs=[VMEM] * len(shapes) if many else VMEM,
        compiler_params=pltpu.CompilerParams(vmem_limit_bytes=40 * 2**20),
        name=name,
    )(*args)


def body(mps):
    sites, chi = mps.shape[:2]
    samp = mps.shape[2] // (2 * chi)
    blocks = lax.axis_size("blk")
    band = min(REACH, (blocks - 1) // 2)
    side = lax.axis_index("pair")
    flag = side[None].astype(jnp.int32)

    steps = sites - EDGE + 1
    starts = [0, round(SHARE * steps)]
    counts = [starts[1], steps - starts[1]]
    tile = mps.shape[1:]
    mps, *pieces = call(order_kernel, [(n, *tile) for n in (steps, *counts)], flag, mps, name="order")
    seconds = [move(p, lambda chip, core: (chip - 1, 1) if core == 0 else (chip + 2, 0)) for p in pieces]
    firsts = [move(p, lambda chip, core: (chip - 1, 0) if core == 0 else (chip + 2, 1)) for p in pieces]
    across = lambda chip, core: (chip, 1 - core)
    sibling = move(mps, across)
    inner = call(home_kernel, (64, 128), flag, mps, sibling, name="own_chains")
    spots = jnp.asarray([spot_table(core, samp, band) for core in range(2)], jnp.int32)
    spot = spots[lax.axis_index("blk") % 2, side]
    inner, spot = lax.optimization_barrier((inner, spot))
    carried = (inner,)
    for start, first, second in zip(starts, firsts, seconds):
        second, *carried = lax.optimization_barrier((second, *carried))
        other = move(second, across)
        rows = 288 if start == starts[-1] else 320
        state = call(functools.partial(chain_kernel, start), (rows, 128), flag, mps, sibling, first, second, other,
                     *carried, name="half_chains")
        carried = (carried[0], state)
    partner = lax.ppermute(state, "pair", [(0, 1), (1, 0)])
    tile = call(meet_kernel, (8, 128), state, partner, name="meet")
    tile = call(join_kernel, (8, 128), tile, move(tile, across), name="join")
    tiles = [tile] + [move(tile, lambda chip, core: (chip + gap, core)) for gap in (1, -2)]
    return call(pick_kernel, (1, (2 * band + 1) * samp), spot, *tiles, name="pick")


def solution(mesh):
    in_specs = (P("pair", None, "blk"),)
    out_specs = P(("blk", "pair"), None)
    return jax.shard_map(body, mesh=mesh, in_specs=in_specs, out_specs=out_specs, check_vma=False)
```

```python
import functools

import jax
import jax.numpy as jnp
from jax import lax
from jax.experimental import pallas as pl
from jax.experimental.pallas import tpu as pltpu
from jax.sharding import PartitionSpec as P

REACH = 6
EDGE = 6
SHARE = 0.63
BF16, F32 = jnp.bfloat16, jnp.float32
VMEM = pl.BlockSpec(memory_space=pltpu.VMEM)
SMEM = pl.BlockSpec(memory_space=pltpu.SMEM)


def move(array, source):
    peers = lax.axis_size("blk")
    chips = peers // 2
    pairs = []
    for d in range(peers):
        chip, core = source(d // 2, d % 2)
        pairs.append(((chip % chips) * 2 + core, d))
    return lax.ppermute(array, "blk", pairs)


def split(x):
    high = x.astype(BF16)
    return high, (x - high.astype(F32)).astype(BF16)


def product(left, right):
    return jnp.dot(left, right, preferred_element_type=F32)


def lane_slot(shape):
    return lax.broadcasted_iota(jnp.int32, shape, 1) // 32


def interleave(first, second):
    even = lane_slot(first.shape) % 2 == 0
    return (
        jnp.where(even, first, pltpu.roll(second, 32, 1)),
        jnp.where(even, pltpu.roll(first, 96, 1), second),
    )


def far_weights(tiles, flip):
    if flip:
        tiles = [jnp.concatenate([t] * 4, 0).T for t in tiles]
        blocks = [[t[32 * k : 32 * k + 32] for t in tiles] for k in range(4)]
    else:
        blocks = [tiles] * 4
    slot = lane_slot((32, 128))
    rows = [jnp.concatenate([jnp.where(slot == k, t, 0.0) for t in blocks[k]], 1) for k in range(4)]
    high, low = split(jnp.concatenate(rows, 0))
    return jnp.concatenate([high, high], 0), low


def near_turned(tiles):
    stack = jnp.concatenate([tiles[0], tiles[1], tiles[0], tiles[1]], 0).T
    return [stack[32 * k : 32 * k + 32] for k in (0, 2, 1, 3)]


def near_plain(tile):
    twice = pltpu.roll(tile, 64, 1)
    lower = lane_slot(tile.shape) < 2
    return [jnp.where(lower, tile, twice), jnp.where(lower, twice, tile)]


def spread(state, far):
    double, low = far
    high, rest = split(state)
    inner = product(jnp.concatenate([high, rest], 1), double) + product(high, low)
    return (*split(inner[:, :128]), *split(inner[:, 128:]))


def gather(inner, near):
    h0, l0, h1, l1 = inner
    results = []
    for k, tile in enumerate(near):
        rows = slice(32 * k, 32 * k + 32)
        weights = jnp.concatenate([h0[rows], h1[rows], l0[rows], l1[rows]], 0)
        both = product(jnp.concatenate(split(tile), 0), weights)
        results.append(both[:32] + both[32:])
    return jnp.concatenate(results, 0)


def identities(rows):
    row = lax.broadcasted_iota(jnp.int32, (rows, 128), 0) % 32
    lane = lax.broadcasted_iota(jnp.int32, (rows, 128), 1) % 32
    return jnp.where(row == lane, 1.0, 0.0)


def on_each_side(side_ref, run):
    for side in range(2):
        pl.when(side_ref[0] == side)(functools.partial(run, side == 1))


def turned(tile):
    stack = jnp.concatenate([tile] * 4, 0).T
    slot = lane_slot(tile.shape)
    result = stack[:32]
    for k in range(1, 4):
        result = jnp.where(slot == k, stack[32 * k : 32 * k + 32], result)
    return result


def edge_tile(tiles):
    slot = lane_slot((32, 128))
    row = lax.broadcasted_iota(jnp.int32, (32, 128), 0)
    current = jnp.broadcast_to(tiles[0][:1], (32, 128))
    for k, tile in enumerate(tiles[1:]):
        chosen = jnp.where(slot % 2 == (row >> k) % 2, current, 0.0)
        weights = [jnp.where(slot // 2 == n, tile, 0.0) for n in (0, 0, 1, 1)]
        current = jnp.dot(
            chosen,
            jnp.concatenate(weights, 0),
            precision=lax.Precision.HIGHEST,
            preferred_element_type=F32,
        )
    return current


def order_kernel(side_ref, sites_ref, whole, *pieces):
    sites = sites_ref.shape[0]

    def run(flip):
        def tile(k):
            return sites_ref[sites - 1 - k if flip else k]

        edge = edge_tile([turned(tile(k)) if flip else tile(k) for k in range(EDGE)])
        if flip:
            edge = turned(edge)
        at = 0
        for piece in pieces:
            for k in range(piece.shape[0]):
                value = edge if at == 0 else tile(at + EDGE - 1)
                piece[k] = value
                whole[at] = value
                at += 1

    on_each_side(side_ref, run)


def gather_alone(inner, near):
    h0, l0, h1, l1 = inner
    slot = lane_slot(h0.shape)
    zero = jnp.zeros_like(h0)
    high_weights, low_weights = [
        jnp.concatenate([jnp.where(slot == k, half, zero) for k in range(4) for half in halves], 0)
        for halves in ((h0, h1), (l0, l1))
    ]
    lower = lane_slot(near[0].shape) < 2
    tensors = [jnp.where(lower, near[a], near[b]) for a, b in ((0, 2), (1, 3))]
    high, low = split(jnp.concatenate(tensors, 1))
    both = product(jnp.concatenate([high, low], 0), high_weights)
    return both[:32] + both[32:] + product(high, low_weights)


def home_kernel(side_ref, own, sibling, out):
    def run(flip):
        state = identities(64)
        for site in range(own.shape[0]):
            home = interleave(own[site], sibling[site])
            near = near_plain(own[site]) if flip else near_turned(home)[:2]
            state = gather(spread(state, far_weights(home, flip)), near)
        out[...] = state

    on_each_side(side_ref, run)


def chain_kernel(start, side_ref, own, sibling, first, second, other, home, *rest):
    out = rest[-1]
    count = first.shape[0]

    def run(flip):
        state = rest[0][...] if start else identities(224)
        groups = [state[:128], state[128:]]
        for index in range(count):
            whole = start + index
            far = interleave(first[index], second[index])
            if flip:
                near = [n for t in (own[whole], sibling[whole], other[index], first[index], second[index])
                        for n in near_plain(t)]
            else:
                extra = other[index]
                near = (
                    near_turned(interleave(own[whole], sibling[whole]))
                    + near_turned(interleave(extra, extra))[:2]
                    + near_turned(far)
                )
            weights = far_weights(far, flip)
            pairs, rest_pairs = [spread(g, weights) for g in groups]
            pairs = gather(pairs, near[:4])
            others = gather([part[:64] for part in rest_pairs], near[4:6])
            alone = gather_alone([part[64:] for part in rest_pairs], near[6:])
            groups = [pairs, jnp.concatenate([others, alone], 0)]
        last = start + count == own.shape[0]
        out[...] = jnp.concatenate(groups + [home[...]] if last else groups, 0)

    on_each_side(side_ref, run)


def meet_kernel(mine, theirs, out):
    units = jnp.sum((mine[...] * theirs[...]).reshape(-1, 32, 128), 1)
    units = jnp.concatenate([units, jnp.zeros((16 - units.shape[0], 128), F32)], 0)
    row = lax.broadcasted_iota(jnp.int32, (8, 128), 0)
    chosen = jnp.where(row == lane_slot((8, 128)), 1.0, 0.0)
    found = lax.dot_general(
        chosen, units, (((1,), (1,)), ((), ())), precision=lax.Precision.HIGHEST, preferred_element_type=F32
    )
    out[...] = jnp.concatenate([found, jnp.zeros((8, 112), F32)], 1)


def join_kernel(mine, theirs, out):
    out[...] = mine[...] + pltpu.roll(theirs[...], 16, 1)


def pick_kernel(spot_ref, here, after, before, out):
    joined = here[...] + pltpu.roll(after[...], 32, 1) + pltpu.roll(before[...], 64, 1)
    unit = lax.broadcasted_iota(jnp.int32, (128, 128), 0)
    slot = lax.broadcasted_iota(jnp.int32, (8, 128), 0)
    values = []
    for k in range(3):
        spot = spot_ref[pl.ds(k, 1), :]
        chosen = jnp.where(unit == spot // 8, 1.0, 0.0)
        found = jnp.dot(joined, chosen, precision=lax.Precision.HIGHEST, preferred_element_type=F32)
        values.append(jnp.sum(jnp.where(slot == spot % 8, found, 0.0), 0, keepdims=True))
    tile, remote, own = values
    width = out.shape[1]
    out[...] = (tile * tile / (own * remote))[:, :width]


def find(core, near, far):
    mine, theirs = ("A0", "A1"), ("Z1", "Z0")
    if core == 1:
        mine, theirs = theirs, mine
    own, sibling = f"O{core}", f"O{1 - core}"
    if near == far and near in mine:
        return lambda n, m: (6, mine.index(near) + 2 * m)
    for base, rows, lanes in ((0, (own, sibling, theirs[1]), mine), (7, (own,), (own, sibling))):
        if near in rows and far in lanes:
            return lambda n, m: (base + 2 * rows.index(near) + n, lanes.index(far) + 2 * m)
        if far in rows and near in lanes:
            return lambda n, m: (base + 2 * rows.index(far) + m, lanes.index(near) + 2 * n)
    return None


def spot_table(core, samp, band):
    views = [(role, (k, k + 1) if core == 0 else (k + 1, k)) for k, role in ((0, "O"), (2, "A"), (4, "Z"))]
    shift = {"O": 0, "A": -1, "Z": 2}

    def place(offset, alone=False):
        chip, lane = (core + offset) // 2, (core + offset) % 2
        for role, messages in views:
            for name, gap in shift.items():
                if gap - shift[role] == chip:
                    goal = f"{name}{lane}"
                    for k, message in enumerate(messages):
                        got = find(k, goal if alone else f"{role}{core}", goal)
                        if got:
                            return message, got
        raise ValueError(offset)

    def code(where, n, m):
        message, got = where
        unit, slot = got(n, m)
        return 8 * (16 * message + unit) + slot

    offsets = range(-band, band + 1)
    table = []
    for n in range(samp):
        tile = [code(place(o), n, m) for o in offsets for m in range(samp)]
        remote = [code(place(o, True), m, m) for o in offsets for m in range(samp)]
        own = [code(place(0, True), n, n)] * len(tile)
        rows = [r + r[:1] * (128 - len(r)) for r in (tile, remote, own)]
        table.append(rows + rows[:1] * 5)
    return table


def call(kernel, shapes, *args, name):
    many = isinstance(shapes, list)
    shapes = [jax.ShapeDtypeStruct(shape, F32) for shape in (shapes if many else [shapes])]
    return pl.pallas_call(
        kernel,
        out_shape=shapes if many else shapes[0],
        in_specs=[SMEM if a.ndim == 1 else VMEM for a in args],
        out_specs=[VMEM] * len(shapes) if many else VMEM,
        compiler_params=pltpu.CompilerParams(vmem_limit_bytes=40 * 2**20),
        name=name,
    )(*args)


def body(mps):
    sites, chi = mps.shape[:2]
    samp = mps.shape[2] // (2 * chi)
    blocks = lax.axis_size("blk")
    band = min(REACH, (blocks - 1) // 2)
    side = lax.axis_index("pair")
    flag = side[None].astype(jnp.int32)

    steps = sites - EDGE + 1
    starts = [0, round(SHARE * steps)]
    counts = [starts[1], steps - starts[1]]
    tile = mps.shape[1:]
    mps, *pieces = call(order_kernel, [(n, *tile) for n in (steps, *counts)], flag, mps, name="order")
    seconds = [move(p, lambda chip, core: (chip - 1, 1) if core == 0 else (chip + 2, 0)) for p in pieces]
    firsts = [move(p, lambda chip, core: (chip - 1, 0) if core == 0 else (chip + 2, 1)) for p in pieces]
    across = lambda chip, core: (chip, 1 - core)
    sibling = move(mps, across)
    inner = call(home_kernel, (64, 128), flag, mps, sibling, name="own_chains")
    spots = jnp.asarray([spot_table(core, samp, band) for core in range(2)], jnp.int32)
    spot = spots[lax.axis_index("blk") % 2, side]
    inner, spot = lax.optimization_barrier((inner, spot))
    carried = (inner,)
    for start, first, second in zip(starts, firsts, seconds):
        second, *carried = lax.optimization_barrier((second, *carried))
        other = move(second, across)
        rows = 288 if start == starts[-1] else 224
        state = call(functools.partial(chain_kernel, start), (rows, 128), flag, mps, sibling, first, second, other,
                     *carried, name="half_chains")
        carried = (carried[0], state)
    partner = lax.ppermute(state, "pair", [(0, 1), (1, 0)])
    tile = call(meet_kernel, (8, 128), state, partner, name="meet")
    tile = call(join_kernel, (8, 128), tile, move(tile, across), name="join")
    tiles = [tile] + [move(tile, lambda chip, core: (chip + gap, core)) for gap in (1, -2)]
    return call(pick_kernel, (1, (2 * band + 1) * samp), spot, *tiles, name="pick")


def solution(mesh):
    in_specs = (P("pair", None, "blk"),)
    out_specs = P(("blk", "pair"), None)
    return jax.shard_map(body, mesh=mesh, in_specs=in_specs, out_specs=out_specs, check_vma=False)
```

```python
import functools

import jax
import jax.numpy as jnp
from jax import lax
from jax.experimental import pallas as pl
from jax.experimental.pallas import tpu as pltpu
from jax.sharding import PartitionSpec as P

REACH = 6
EDGE = 6
SHARE = 0.66
BF16, F32 = jnp.bfloat16, jnp.float32
VMEM = pl.BlockSpec(memory_space=pltpu.VMEM)
SMEM = pl.BlockSpec(memory_space=pltpu.SMEM)


def move(array, source):
    peers = lax.axis_size("blk")
    chips = peers // 2
    pairs = []
    for d in range(peers):
        chip, core = source(d // 2, d % 2)
        pairs.append(((chip % chips) * 2 + core, d))
    return lax.ppermute(array, "blk", pairs)


def split(x):
    high = x.astype(BF16)
    return high, (x - high.astype(F32)).astype(BF16)


def product(left, right):
    return jnp.dot(left, right, preferred_element_type=F32)


def lane_slot(shape):
    return lax.broadcasted_iota(jnp.int32, shape, 1) // 32


def interleave(first, second):
    even = lane_slot(first.shape) % 2 == 0
    return (
        jnp.where(even, first, pltpu.roll(second, 32, 1)),
        jnp.where(even, pltpu.roll(first, 96, 1), second),
    )


def far_weights(tiles, flip):
    if flip:
        tiles = [jnp.concatenate([t] * 4, 0).T for t in tiles]
        blocks = [[t[32 * k : 32 * k + 32] for t in tiles] for k in range(4)]
    else:
        blocks = [tiles] * 4
    slot = lane_slot((32, 128))
    rows = [jnp.concatenate([jnp.where(slot == k, t, 0.0) for t in blocks[k]], 1) for k in range(4)]
    high, low = split(jnp.concatenate(rows, 0))
    return jnp.concatenate([high, high], 0), low


def near_turned(tiles):
    stack = jnp.concatenate([tiles[0], tiles[1], tiles[0], tiles[1]], 0).T
    return [stack[32 * k : 32 * k + 32] for k in (0, 2, 1, 3)]


def near_plain(tile):
    twice = pltpu.roll(tile, 64, 1)
    lower = lane_slot(tile.shape) < 2
    return [jnp.where(lower, tile, twice), jnp.where(lower, twice, tile)]


def spread(state, far):
    double, low = far
    high, rest = split(state)
    inner = product(jnp.concatenate([high, rest], 1), double) + product(high, low)
    return (*split(inner[:, :128]), *split(inner[:, 128:]))


def gather(inner, near):
    h0, l0, h1, l1 = inner
    results = []
    for k, tile in enumerate(near):
        rows = slice(32 * k, 32 * k + 32)
        weights = jnp.concatenate([h0[rows], h1[rows], l0[rows], l1[rows]], 0)
        both = product(jnp.concatenate(split(tile), 0), weights)
        results.append(both[:32] + both[32:])
    return jnp.concatenate(results, 0)


def identities(rows):
    row = lax.broadcasted_iota(jnp.int32, (rows, 128), 0) % 32
    lane = lax.broadcasted_iota(jnp.int32, (rows, 128), 1) % 32
    return jnp.where(row == lane, 1.0, 0.0)


def on_each_side(side_ref, run):
    for side in range(2):
        pl.when(side_ref[0] == side)(functools.partial(run, side == 1))


def turned(tile):
    stack = jnp.concatenate([tile] * 4, 0).T
    slot = lane_slot(tile.shape)
    result = stack[:32]
    for k in range(1, 4):
        result = jnp.where(slot == k, stack[32 * k : 32 * k + 32], result)
    return result


def edge_tile(tiles):
    slot = lane_slot((32, 128))
    row = lax.broadcasted_iota(jnp.int32, (32, 128), 0)
    current = jnp.broadcast_to(tiles[0][:1], (32, 128))
    for k, tile in enumerate(tiles[1:]):
        chosen = jnp.where(slot % 2 == (row >> k) % 2, current, 0.0)
        high, low = split(jnp.concatenate([jnp.where(slot // 2 == n, tile, 0.0) for n in (0, 0, 1, 1)], 0))
        upper, lower = split(chosen)
        current = product(jnp.concatenate([upper, lower], 1), jnp.concatenate([high, high], 0)) + product(upper, low)
    return current


def order_kernel(side_ref, sites_ref, whole, *pieces):
    sites = sites_ref.shape[0]

    def run(flip):
        def tile(k):
            return sites_ref[sites - 1 - k if flip else k]

        edge = edge_tile([turned(tile(k)) if flip else tile(k) for k in range(EDGE)])
        if flip:
            edge = turned(edge)
        at = 0
        for piece in pieces:
            for k in range(piece.shape[0]):
                value = edge if at == 0 else tile(at + EDGE - 1)
                piece[k] = value
                whole[at] = value
                at += 1

    on_each_side(side_ref, run)


def gather_alone(inner, near):
    h0, l0, h1, l1 = inner
    slot = lane_slot(h0.shape)
    zero = jnp.zeros_like(h0)
    high_weights, low_weights = [
        jnp.concatenate([jnp.where(slot == k, half, zero) for k in range(4) for half in halves], 0)
        for halves in ((h0, h1), (l0, l1))
    ]
    lower = lane_slot(near[0].shape) < 2
    tensors = [jnp.where(lower, near[a], near[b]) for a, b in ((0, 2), (1, 3))]
    high, low = split(jnp.concatenate(tensors, 1))
    both = product(jnp.concatenate([high, low], 0), high_weights)
    return both[:32] + both[32:] + product(high, low_weights)


def home_kernel(side_ref, own, sibling, out):
    def run(flip):
        state = identities(64)
        for site in range(own.shape[0]):
            home = interleave(own[site], sibling[site])
            near = near_plain(own[site]) if flip else near_turned(home)[:2]
            state = gather(spread(state, far_weights(home, flip)), near)
        out[...] = state

    on_each_side(side_ref, run)


def chain_kernel(start, side_ref, own, sibling, first, second, other, home, *rest):
    out = rest[-1]
    count = first.shape[0]

    def run(flip):
        state = rest[0][...] if start else identities(224)
        groups = [state[:128], state[128:]]
        for index in range(count):
            whole = start + index
            far = interleave(first[index], second[index])
            if flip:
                near = [n for t in (own[whole], sibling[whole], other[index], first[index], second[index])
                        for n in near_plain(t)]
            else:
                extra = other[index]
                near = (
                    near_turned(interleave(own[whole], sibling[whole]))
                    + near_turned(interleave(extra, extra))[:2]
                    + near_turned(far)
                )
            weights = far_weights(far, flip)
            pairs, rest_pairs = [spread(g, weights) for g in groups]
            pairs = gather(pairs, near[:4])
            others = gather([part[:64] for part in rest_pairs], near[4:6])
            alone = gather_alone([part[64:] for part in rest_pairs], near[6:])
            groups = [pairs, jnp.concatenate([others, alone], 0)]
        last = start + count == own.shape[0]
        out[...] = jnp.concatenate(groups + [home[...]] if last else groups, 0)

    on_each_side(side_ref, run)


def meet_kernel(mine, theirs, out):
    units = jnp.sum((mine[...] * theirs[...]).reshape(-1, 32, 128), 1)
    units = jnp.concatenate([units, jnp.zeros((16 - units.shape[0], 128), F32)], 0)
    row = lax.broadcasted_iota(jnp.int32, (8, 128), 0)
    chosen = jnp.where(row == lane_slot((8, 128)), 1.0, 0.0)
    found = lax.dot_general(
        chosen, units, (((1,), (1,)), ((), ())), precision=lax.Precision.HIGHEST, preferred_element_type=F32
    )
    out[...] = jnp.concatenate([found, jnp.zeros((8, 112), F32)], 1)


def join_kernel(mine, theirs, out):
    out[...] = mine[...] + pltpu.roll(theirs[...], 16, 1)


def pick_kernel(spot_ref, here, after, before, out):
    joined = here[...] + pltpu.roll(after[...], 32, 1) + pltpu.roll(before[...], 64, 1)
    unit = lax.broadcasted_iota(jnp.int32, (128, 128), 0)
    slot = lax.broadcasted_iota(jnp.int32, (8, 128), 0)
    values = []
    for k in range(3):
        spot = spot_ref[pl.ds(k, 1), :]
        chosen = jnp.where(unit == spot // 8, 1.0, 0.0)
        found = jnp.dot(joined, chosen, precision=lax.Precision.HIGHEST, preferred_element_type=F32)
        values.append(jnp.sum(jnp.where(slot == spot % 8, found, 0.0), 0, keepdims=True))
    tile, remote, own = values
    width = out.shape[1]
    out[...] = (tile * tile / (own * remote))[:, :width]


def find(core, near, far):
    mine, theirs = ("A0", "A1"), ("Z1", "Z0")
    if core == 1:
        mine, theirs = theirs, mine
    own, sibling = f"O{core}", f"O{1 - core}"
    if near == far and near in mine:
        return lambda n, m: (6, mine.index(near) + 2 * m)
    for base, rows, lanes in ((0, (own, sibling, theirs[1]), mine), (7, (own,), (own, sibling))):
        if near in rows and far in lanes:
            return lambda n, m: (base + 2 * rows.index(near) + n, lanes.index(far) + 2 * m)
        if far in rows and near in lanes:
            return lambda n, m: (base + 2 * rows.index(far) + m, lanes.index(near) + 2 * n)
    return None


def spot_table(core, samp, band):
    views = [(role, (k, k + 1) if core == 0 else (k + 1, k)) for k, role in ((0, "O"), (2, "A"), (4, "Z"))]
    shift = {"O": 0, "A": -1, "Z": 2}

    def place(offset, alone=False):
        chip, lane = (core + offset) // 2, (core + offset) % 2
        for role, messages in views:
            for name, gap in shift.items():
                if gap - shift[role] == chip:
                    goal = f"{name}{lane}"
                    for k, message in enumerate(messages):
                        got = find(k, goal if alone else f"{role}{core}", goal)
                        if got:
                            return message, got
        raise ValueError(offset)

    def code(where, n, m):
        message, got = where
        unit, slot = got(n, m)
        return 8 * (16 * message + unit) + slot

    offsets = range(-band, band + 1)
    table = []
    for n in range(samp):
        tile = [code(place(o), n, m) for o in offsets for m in range(samp)]
        remote = [code(place(o, True), m, m) for o in offsets for m in range(samp)]
        own = [code(place(0, True), n, n)] * len(tile)
        rows = [r + r[:1] * (128 - len(r)) for r in (tile, remote, own)]
        table.append(rows + rows[:1] * 5)
    return table


def call(kernel, shapes, *args, name):
    many = isinstance(shapes, list)
    shapes = [jax.ShapeDtypeStruct(shape, F32) for shape in (shapes if many else [shapes])]
    return pl.pallas_call(
        kernel,
        out_shape=shapes if many else shapes[0],
        in_specs=[SMEM if a.ndim == 1 else VMEM for a in args],
        out_specs=[VMEM] * len(shapes) if many else VMEM,
        compiler_params=pltpu.CompilerParams(vmem_limit_bytes=40 * 2**20),
        name=name,
    )(*args)


def body(mps):
    sites, chi = mps.shape[:2]
    samp = mps.shape[2] // (2 * chi)
    blocks = lax.axis_size("blk")
    band = min(REACH, (blocks - 1) // 2)
    side = lax.axis_index("pair")
    flag = side[None].astype(jnp.int32)

    steps = sites - EDGE + 1
    starts = [0, round(SHARE * steps)]
    counts = [starts[1], steps - starts[1]]
    tile = mps.shape[1:]
    mps, *pieces = call(order_kernel, [(n, *tile) for n in (steps, *counts)], flag, mps, name="order")
    seconds = [move(p, lambda chip, core: (chip - 1, 1) if core == 0 else (chip + 2, 0)) for p in pieces]
    firsts = [move(p, lambda chip, core: (chip - 1, 0) if core == 0 else (chip + 2, 1)) for p in pieces]
    across = lambda chip, core: (chip, 1 - core)
    sibling = move(mps, across)
    inner = call(home_kernel, (64, 128), flag, mps, sibling, name="own_chains")
    spots = jnp.asarray([spot_table(core, samp, band) for core in range(2)], jnp.int32)
    spot = spots[lax.axis_index("blk") % 2, side]
    inner, spot = lax.optimization_barrier((inner, spot))
    carried = (inner,)
    for start, first, second in zip(starts, firsts, seconds):
        second, *carried = lax.optimization_barrier((second, *carried))
        other = move(second, across)
        rows = 288 if start == starts[-1] else 224
        state = call(functools.partial(chain_kernel, start), (rows, 128), flag, mps, sibling, first, second, other,
                     *carried, name="half_chains")
        carried = (carried[0], state)
    partner = lax.ppermute(state, "pair", [(0, 1), (1, 0)])
    tile = call(meet_kernel, (8, 128), state, partner, name="meet")
    tile = call(join_kernel, (8, 128), tile, move(tile, across), name="join")
    tiles = [tile] + [move(tile, lambda chip, core: (chip + gap, core)) for gap in (1, -2)]
    return call(pick_kernel, (1, (2 * band + 1) * samp), spot, *tiles, name="pick")


def solution(mesh):
    in_specs = (P("pair", None, "blk"),)
    out_specs = P(("blk", "pair"), None)
    return jax.shard_map(body, mesh=mesh, in_specs=in_specs, out_specs=out_specs, check_vma=False)
```

```python
import functools

import jax
import jax.numpy as jnp
from jax import lax
from jax.experimental import pallas as pl
from jax.experimental.pallas import tpu as pltpu
from jax.sharding import PartitionSpec as P

REACH = 6
EDGE = 6
SHARE = 0.63
BF16, F32 = jnp.bfloat16, jnp.float32
VMEM = pl.BlockSpec(memory_space=pltpu.VMEM)
SMEM = pl.BlockSpec(memory_space=pltpu.SMEM)


def move(array, source):
    peers = lax.axis_size("blk")
    chips = peers // 2
    pairs = []
    for d in range(peers):
        chip, core = source(d // 2, d % 2)
        pairs.append(((chip % chips) * 2 + core, d))
    return lax.ppermute(array, "blk", pairs)


def split(x):
    high = x.astype(BF16)
    return high, (x - high.astype(F32)).astype(BF16)


def product(left, right):
    return jnp.dot(left, right, preferred_element_type=F32)


def lane_slot(shape):
    return lax.broadcasted_iota(jnp.int32, shape, 1) // 32


def interleave(first, second):
    even = lane_slot(first.shape) % 2 == 0
    return (
        jnp.where(even, first, pltpu.roll(second, 32, 1)),
        jnp.where(even, pltpu.roll(first, 96, 1), second),
    )


def far_weights(tiles, flip):
    if flip:
        tiles = [jnp.concatenate([t] * 4, 0).T for t in tiles]
        blocks = [[t[32 * k : 32 * k + 32] for t in tiles] for k in range(4)]
    else:
        blocks = [tiles] * 4
    slot = lane_slot((32, 128))
    rows = [jnp.concatenate([jnp.where(slot == k, t, 0.0) for t in blocks[k]], 1) for k in range(4)]
    high, low = split(jnp.concatenate(rows, 0))
    return jnp.concatenate([high, high], 0), low


def near_turned(tiles):
    stack = jnp.concatenate([tiles[0], tiles[1], tiles[0], tiles[1]], 0).T
    return [stack[32 * k : 32 * k + 32] for k in (0, 2, 1, 3)]


def near_plain(tile):
    twice = pltpu.roll(tile, 64, 1)
    lower = lane_slot(tile.shape) < 2
    return [jnp.where(lower, tile, twice), jnp.where(lower, twice, tile)]


def spread(state, far):
    double, low = far
    high, rest = split(state)
    inner = product(jnp.concatenate([high, rest], 1), double) + product(high, low)
    return (*split(inner[:, :128]), *split(inner[:, 128:]))


def gather(inner, near):
    h0, l0, h1, l1 = inner
    results = []
    for k, tile in enumerate(near):
        rows = slice(32 * k, 32 * k + 32)
        weights = jnp.concatenate([h0[rows], h1[rows], l0[rows], l1[rows]], 0)
        both = product(jnp.concatenate(split(tile), 0), weights)
        results.append(both[:32] + both[32:])
    return jnp.concatenate(results, 0)


def identities(rows):
    row = lax.broadcasted_iota(jnp.int32, (rows, 128), 0) % 32
    lane = lax.broadcasted_iota(jnp.int32, (rows, 128), 1) % 32
    return jnp.where(row == lane, 1.0, 0.0)


def on_each_side(side_ref, run):
    for side in range(2):
        pl.when(side_ref[0] == side)(functools.partial(run, side == 1))


def turned(tile):
    stack = jnp.concatenate([tile] * 4, 0).T
    slot = lane_slot(tile.shape)
    result = stack[:32]
    for k in range(1, 4):
        result = jnp.where(slot == k, stack[32 * k : 32 * k + 32], result)
    return result


def edge_tile(tiles):
    slot = lane_slot((32, 128))
    row = lax.broadcasted_iota(jnp.int32, (32, 128), 0)
    current = jnp.broadcast_to(tiles[0][:1], (32, 128))
    for k, tile in enumerate(tiles[1:]):
        chosen = jnp.where(slot % 2 == (row >> k) % 2, current, 0.0)
        high, low = split(jnp.concatenate([jnp.where(slot // 2 == n, tile, 0.0) for n in (0, 0, 1, 1)], 0))
        upper, lower = split(chosen)
        current = product(jnp.concatenate([upper, lower], 1), jnp.concatenate([high, high], 0)) + product(upper, low)
    return current


def order_kernel(side_ref, sites_ref, whole, *pieces):
    sites = sites_ref.shape[0]

    def run(flip):
        def tile(k):
            return sites_ref[sites - 1 - k if flip else k]

        edge = edge_tile([turned(tile(k)) if flip else tile(k) for k in range(EDGE)])
        if flip:
            edge = turned(edge)
        at = 0
        for piece in pieces:
            for k in range(piece.shape[0]):
                value = edge if at == 0 else tile(at + EDGE - 1)
                piece[k] = value
                whole[at] = value
                at += 1

    on_each_side(side_ref, run)


def gather_alone(inner, near):
    h0, l0, h1, l1 = inner
    slot = lane_slot(h0.shape)
    zero = jnp.zeros_like(h0)
    high_weights, low_weights = [
        jnp.concatenate([jnp.where(slot == k, half, zero) for k in range(4) for half in halves], 0)
        for halves in ((h0, h1), (l0, l1))
    ]
    lower = lane_slot(near[0].shape) < 2
    tensors = [jnp.where(lower, near[a], near[b]) for a, b in ((0, 2), (1, 3))]
    high, low = split(jnp.concatenate(tensors, 1))
    both = product(jnp.concatenate([high, low], 0), high_weights)
    return both[:32] + both[32:] + product(high, low_weights)


def home_kernel(side_ref, own, sibling, out):
    def run(flip):
        state = identities(64)
        for site in range(own.shape[0]):
            home = interleave(own[site], sibling[site])
            near = near_plain(own[site]) if flip else near_turned(home)[:2]
            state = gather(spread(state, far_weights(home, flip)), near)
        out[...] = state

    on_each_side(side_ref, run)


def chain_kernel(start, side_ref, own, sibling, first, second, other, home, *rest):
    out = rest[-1]
    count = first.shape[0]

    def run(flip):
        state = rest[0][...] if start else identities(224)
        groups = [state[:128], state[128:]]
        for index in range(count):
            whole = start + index
            far = interleave(first[index], second[index])
            if flip:
                near = [n for t in (own[whole], sibling[whole], other[index], first[index], second[index])
                        for n in near_plain(t)]
            else:
                extra = other[index]
                near = (
                    near_turned(interleave(own[whole], sibling[whole]))
                    + near_turned(interleave(extra, extra))[:2]
                    + near_turned(far)
                )
            weights = far_weights(far, flip)
            pairs, rest_pairs = [spread(g, weights) for g in groups]
            pairs = gather(pairs, near[:4])
            others = gather([part[:64] for part in rest_pairs], near[4:6])
            alone = gather_alone([part[64:] for part in rest_pairs], near[6:])
            groups = [pairs, jnp.concatenate([others, alone], 0)]
        last = start + count == own.shape[0]
        out[...] = jnp.concatenate(groups + [home[...]] if last else groups, 0)

    on_each_side(side_ref, run)


def meet_kernel(mine, theirs, out):
    units = jnp.sum((mine[...] * theirs[...]).reshape(-1, 32, 128), 1)
    units = jnp.concatenate([units, jnp.zeros((16 - units.shape[0], 128), F32)], 0)
    row = lax.broadcasted_iota(jnp.int32, (8, 128), 0)
    chosen = jnp.where(row == lane_slot((8, 128)), 1.0, 0.0)
    found = lax.dot_general(
        chosen, units, (((1,), (1,)), ((), ())), precision=lax.Precision.HIGHEST, preferred_element_type=F32
    )
    out[...] = jnp.concatenate([found, jnp.zeros((8, 112), F32)], 1)


def join_kernel(mine, theirs, out):
    out[...] = mine[...] + pltpu.roll(theirs[...], 16, 1)


def pick_kernel(spot_ref, here, after, before, out):
    joined = here[...] + pltpu.roll(after[...], 32, 1) + pltpu.roll(before[...], 64, 1)
    unit = lax.broadcasted_iota(jnp.int32, (128, 128), 0)
    slot = lax.broadcasted_iota(jnp.int32, (8, 128), 0)
    values = []
    for k in range(3):
        spot = spot_ref[pl.ds(k, 1), :]
        chosen = jnp.where(unit == spot // 8, 1.0, 0.0)
        found = jnp.dot(joined, chosen, precision=lax.Precision.HIGHEST, preferred_element_type=F32)
        values.append(jnp.sum(jnp.where(slot == spot % 8, found, 0.0), 0, keepdims=True))
    tile, remote, own = values
    width = out.shape[1]
    out[...] = (tile * tile / (own * remote))[:, :width]


def find(core, near, far):
    mine, theirs = ("A0", "A1"), ("Z1", "Z0")
    if core == 1:
        mine, theirs = theirs, mine
    own, sibling = f"O{core}", f"O{1 - core}"
    if near == far and near in mine:
        return lambda n, m: (6, mine.index(near) + 2 * m)
    for base, rows, lanes in ((0, (own, sibling, theirs[1]), mine), (7, (own,), (own, sibling))):
        if near in rows and far in lanes:
            return lambda n, m: (base + 2 * rows.index(near) + n, lanes.index(far) + 2 * m)
        if far in rows and near in lanes:
            return lambda n, m: (base + 2 * rows.index(far) + m, lanes.index(near) + 2 * n)
    return None


def spot_table(core, samp, band):
    views = [(role, (k, k + 1) if core == 0 else (k + 1, k)) for k, role in ((0, "O"), (2, "A"), (4, "Z"))]
    shift = {"O": 0, "A": -1, "Z": 2}

    def place(offset, alone=False):
        chip, lane = (core + offset) // 2, (core + offset) % 2
        for role, messages in views:
            for name, gap in shift.items():
                if gap - shift[role] == chip:
                    goal = f"{name}{lane}"
                    for k, message in enumerate(messages):
                        got = find(k, goal if alone else f"{role}{core}", goal)
                        if got:
                            return message, got
        raise ValueError(offset)

    def code(where, n, m):
        message, got = where
        unit, slot = got(n, m)
        return 8 * (16 * message + unit) + slot

    offsets = range(-band, band + 1)
    table = []
    for n in range(samp):
        tile = [code(place(o), n, m) for o in offsets for m in range(samp)]
        remote = [code(place(o, True), m, m) for o in offsets for m in range(samp)]
        own = [code(place(0, True), n, n)] * len(tile)
        rows = [r + r[:1] * (128 - len(r)) for r in (tile, remote, own)]
        table.append(rows + rows[:1] * 5)
    return table


def call(kernel, shapes, *args, name):
    many = isinstance(shapes, list)
    shapes = [jax.ShapeDtypeStruct(shape, F32) for shape in (shapes if many else [shapes])]
    return pl.pallas_call(
        kernel,
        out_shape=shapes if many else shapes[0],
        in_specs=[SMEM if a.ndim == 1 else VMEM for a in args],
        out_specs=[VMEM] * len(shapes) if many else VMEM,
        compiler_params=pltpu.CompilerParams(vmem_limit_bytes=40 * 2**20),
        name=name,
    )(*args)


def body(mps):
    sites, chi = mps.shape[:2]
    samp = mps.shape[2] // (2 * chi)
    blocks = lax.axis_size("blk")
    band = min(REACH, (blocks - 1) // 2)
    side = lax.axis_index("pair")
    flag = side[None].astype(jnp.int32)

    steps = sites - EDGE + 1
    starts = [0, round(SHARE * steps)]
    counts = [starts[1], steps - starts[1]]
    tile = mps.shape[1:]
    mps, *pieces = call(order_kernel, [(n, *tile) for n in (steps, *counts)], flag, mps, name="order")
    seconds = [move(p, lambda chip, core: (chip - 1, 1) if core == 0 else (chip + 2, 0)) for p in pieces]
    firsts = [move(p, lambda chip, core: (chip - 1, 0) if core == 0 else (chip + 2, 1)) for p in pieces]
    across = lambda chip, core: (chip, 1 - core)
    sibling = move(mps, across)
    inner = call(home_kernel, (64, 128), flag, mps, sibling, name="own_chains")
    spots = jnp.asarray([spot_table(core, samp, band) for core in range(2)], jnp.int32)
    spot = spots[lax.axis_index("blk") % 2, side]
    inner, spot = lax.optimization_barrier((inner, spot))
    carried = (inner,)
    for start, first, second in zip(starts, firsts, seconds):
        second, *carried = lax.optimization_barrier((second, *carried))
        other = move(second, across)
        rows = 288 if start == starts[-1] else 224
        state = call(functools.partial(chain_kernel, start), (rows, 128), flag, mps, sibling, first, second, other,
                     *carried, name="half_chains")
        carried = (carried[0], state)
    partner = lax.ppermute(state, "pair", [(0, 1), (1, 0)])
    tile = call(meet_kernel, (8, 128), state, partner, name="meet")
    tile = call(join_kernel, (8, 128), tile, move(tile, across), name="join")
    tiles = [tile] + [move(tile, lambda chip, core: (chip + gap, core)) for gap in (1, -2)]
    return call(pick_kernel, (1, (2 * band + 1) * samp), spot, *tiles, name="pick")


def solution(mesh):
    in_specs = (P("pair", None, "blk"),)
    out_specs = P(("blk", "pair"), None)
    return jax.shard_map(body, mesh=mesh, in_specs=in_specs, out_specs=out_specs, check_vma=False)
```

```python
import functools

import jax
import jax.numpy as jnp
from jax import lax
from jax.experimental import pallas as pl
from jax.experimental.pallas import tpu as pltpu
from jax.sharding import PartitionSpec as P

REACH = 6
EDGE = 6
SHARE = 0.6
BF16, F32 = jnp.bfloat16, jnp.float32
VMEM = pl.BlockSpec(memory_space=pltpu.VMEM)
SMEM = pl.BlockSpec(memory_space=pltpu.SMEM)


def move(array, source):
    peers = lax.axis_size("blk")
    chips = peers // 2
    pairs = []
    for d in range(peers):
        chip, core = source(d // 2, d % 2)
        pairs.append(((chip % chips) * 2 + core, d))
    return lax.ppermute(array, "blk", pairs)


def split(x):
    high = x.astype(BF16)
    return high, (x - high.astype(F32)).astype(BF16)


def product(left, right):
    return jnp.dot(left, right, preferred_element_type=F32)


def lane_slot(shape):
    return lax.broadcasted_iota(jnp.int32, shape, 1) // 32


def interleave(first, second):
    even = lane_slot(first.shape) % 2 == 0
    return (
        jnp.where(even, first, pltpu.roll(second, 32, 1)),
        jnp.where(even, pltpu.roll(first, 96, 1), second),
    )


def far_weights(tiles, flip):
    if flip:
        tiles = [jnp.concatenate([t] * 4, 0).T for t in tiles]
        blocks = [[t[32 * k : 32 * k + 32] for t in tiles] for k in range(4)]
    else:
        blocks = [tiles] * 4
    slot = lane_slot((32, 128))
    rows = [jnp.concatenate([jnp.where(slot == k, t, 0.0) for t in blocks[k]], 1) for k in range(4)]
    high, low = split(jnp.concatenate(rows, 0))
    return jnp.concatenate([high, high], 0), low


def near_turned(tiles):
    stack = jnp.concatenate([tiles[0], tiles[1], tiles[0], tiles[1]], 0).T
    return [stack[32 * k : 32 * k + 32] for k in (0, 2, 1, 3)]


def near_plain(tile):
    twice = pltpu.roll(tile, 64, 1)
    lower = lane_slot(tile.shape) < 2
    return [jnp.where(lower, tile, twice), jnp.where(lower, twice, tile)]


def spread(state, far):
    double, low = far
    high, rest = split(state)
    inner = product(jnp.concatenate([high, rest], 1), double) + product(high, low)
    return (*split(inner[:, :128]), *split(inner[:, 128:]))


def gather(inner, near):
    h0, l0, h1, l1 = inner
    results = []
    for k, tile in enumerate(near):
        rows = slice(32 * k, 32 * k + 32)
        weights = jnp.concatenate([h0[rows], h1[rows], l0[rows], l1[rows]], 0)
        both = product(jnp.concatenate(split(tile), 0), weights)
        results.append(both[:32] + both[32:])
    return jnp.concatenate(results, 0)


def identities(rows):
    row = lax.broadcasted_iota(jnp.int32, (rows, 128), 0) % 32
    lane = lax.broadcasted_iota(jnp.int32, (rows, 128), 1) % 32
    return jnp.where(row == lane, 1.0, 0.0)


def on_each_side(side_ref, run):
    for side in range(2):
        pl.when(side_ref[0] == side)(functools.partial(run, side == 1))


def turned(tile):
    stack = jnp.concatenate([tile] * 4, 0).T
    slot = lane_slot(tile.shape)
    result = stack[:32]
    for k in range(1, 4):
        result = jnp.where(slot == k, stack[32 * k : 32 * k + 32], result)
    return result


def edge_tile(tiles):
    slot = lane_slot((32, 128))
    row = lax.broadcasted_iota(jnp.int32, (32, 128), 0)
    current = jnp.broadcast_to(tiles[0][:1], (32, 128))
    for k, tile in enumerate(tiles[1:]):
        chosen = jnp.where(slot % 2 == (row >> k) % 2, current, 0.0)
        high, low = split(jnp.concatenate([jnp.where(slot // 2 == n, tile, 0.0) for n in (0, 0, 1, 1)], 0))
        upper, lower = split(chosen)
        current = product(jnp.concatenate([upper, lower], 1), jnp.concatenate([high, high], 0)) + product(upper, low)
    return current


def order_kernel(side_ref, sites_ref, whole, *pieces):
    sites = sites_ref.shape[0]

    def run(flip):
        def tile(k):
            return sites_ref[sites - 1 - k if flip else k]

        edge = edge_tile([turned(tile(k)) if flip else tile(k) for k in range(EDGE)])
        if flip:
            edge = turned(edge)
        at = 0
        for piece in pieces:
            for k in range(piece.shape[0]):
                value = edge if at == 0 else tile(at + EDGE - 1)
                piece[k] = value
                whole[at] = value
                at += 1

    on_each_side(side_ref, run)


def gather_alone(inner, near):
    h0, l0, h1, l1 = inner
    slot = lane_slot(h0.shape)
    zero = jnp.zeros_like(h0)
    high_weights, low_weights = [
        jnp.concatenate([jnp.where(slot == k, half, zero) for k in range(4) for half in halves], 0)
        for halves in ((h0, h1), (l0, l1))
    ]
    lower = lane_slot(near[0].shape) < 2
    tensors = [jnp.where(lower, near[a], near[b]) for a, b in ((0, 2), (1, 3))]
    high, low = split(jnp.concatenate(tensors, 1))
    both = product(jnp.concatenate([high, low], 0), high_weights)
    return both[:32] + both[32:] + product(high, low_weights)


def home_kernel(side_ref, own, sibling, out):
    def run(flip):
        state = identities(64)
        for site in range(own.shape[0]):
            home = interleave(own[site], sibling[site])
            near = near_plain(own[site]) if flip else near_turned(home)[:2]
            state = gather(spread(state, far_weights(home, flip)), near)
        out[...] = state

    on_each_side(side_ref, run)


def chain_kernel(start, side_ref, own, sibling, first, second, other, home, *rest):
    out = rest[-1]
    count = first.shape[0]

    def run(flip):
        state = rest[0][...] if start else identities(224)
        groups = [state[:128], state[128:]]
        for index in range(count):
            whole = start + index
            far = interleave(first[index], second[index])
            if flip:
                near = [n for t in (own[whole], sibling[whole], other[index], first[index], second[index])
                        for n in near_plain(t)]
            else:
                extra = other[index]
                near = (
                    near_turned(interleave(own[whole], sibling[whole]))
                    + near_turned(interleave(extra, extra))[:2]
                    + near_turned(far)
                )
            weights = far_weights(far, flip)
            pairs, rest_pairs = [spread(g, weights) for g in groups]
            pairs = gather(pairs, near[:4])
            others = gather([part[:64] for part in rest_pairs], near[4:6])
            alone = gather_alone([part[64:] for part in rest_pairs], near[6:])
            groups = [pairs, jnp.concatenate([others, alone], 0)]
        last = start + count == own.shape[0]
        out[...] = jnp.concatenate(groups + [home[...]] if last else groups, 0)

    on_each_side(side_ref, run)


def meet_kernel(mine, theirs, out):
    units = jnp.sum((mine[...] * theirs[...]).reshape(-1, 32, 128), 1)
    units = jnp.concatenate([units, jnp.zeros((16 - units.shape[0], 128), F32)], 0)
    row = lax.broadcasted_iota(jnp.int32, (8, 128), 0)
    chosen = jnp.where(row == lane_slot((8, 128)), 1.0, 0.0)
    found = lax.dot_general(
        chosen, units, (((1,), (1,)), ((), ())), precision=lax.Precision.HIGHEST, preferred_element_type=F32
    )
    out[...] = jnp.concatenate([found, jnp.zeros((8, 112), F32)], 1)


def join_kernel(mine, theirs, out):
    out[...] = mine[...] + pltpu.roll(theirs[...], 16, 1)


def pick_kernel(spot_ref, here, after, before, out):
    joined = here[...] + pltpu.roll(after[...], 32, 1) + pltpu.roll(before[...], 64, 1)
    unit = lax.broadcasted_iota(jnp.int32, (128, 128), 0)
    slot = lax.broadcasted_iota(jnp.int32, (8, 128), 0)
    values = []
    for k in range(3):
        spot = spot_ref[pl.ds(k, 1), :]
        chosen = jnp.where(unit == spot // 8, 1.0, 0.0)
        found = jnp.dot(joined, chosen, precision=lax.Precision.HIGHEST, preferred_element_type=F32)
        values.append(jnp.sum(jnp.where(slot == spot % 8, found, 0.0), 0, keepdims=True))
    tile, remote, own = values
    width = out.shape[1]
    out[...] = (tile * tile / (own * remote))[:, :width]


def find(core, near, far):
    mine, theirs = ("A0", "A1"), ("Z1", "Z0")
    if core == 1:
        mine, theirs = theirs, mine
    own, sibling = f"O{core}", f"O{1 - core}"
    if near == far and near in mine:
        return lambda n, m: (6, mine.index(near) + 2 * m)
    for base, rows, lanes in ((0, (own, sibling, theirs[1]), mine), (7, (own,), (own, sibling))):
        if near in rows and far in lanes:
            return lambda n, m: (base + 2 * rows.index(near) + n, lanes.index(far) + 2 * m)
        if far in rows and near in lanes:
            return lambda n, m: (base + 2 * rows.index(far) + m, lanes.index(near) + 2 * n)
    return None


def spot_table(core, samp, band):
    views = [(role, (k, k + 1) if core == 0 else (k + 1, k)) for k, role in ((0, "O"), (2, "A"), (4, "Z"))]
    shift = {"O": 0, "A": -1, "Z": 2}

    def place(offset, alone=False):
        chip, lane = (core + offset) // 2, (core + offset) % 2
        for role, messages in views:
            for name, gap in shift.items():
                if gap - shift[role] == chip:
                    goal = f"{name}{lane}"
                    for k, message in enumerate(messages):
                        got = find(k, goal if alone else f"{role}{core}", goal)
                        if got:
                            return message, got
        raise ValueError(offset)

    def code(where, n, m):
        message, got = where
        unit, slot = got(n, m)
        return 8 * (16 * message + unit) + slot

    offsets = range(-band, band + 1)
    table = []
    for n in range(samp):
        tile = [code(place(o), n, m) for o in offsets for m in range(samp)]
        remote = [code(place(o, True), m, m) for o in offsets for m in range(samp)]
        own = [code(place(0, True), n, n)] * len(tile)
        rows = [r + r[:1] * (128 - len(r)) for r in (tile, remote, own)]
        table.append(rows + rows[:1] * 5)
    return table


def call(kernel, shapes, *args, name):
    many = isinstance(shapes, list)
    shapes = [jax.ShapeDtypeStruct(shape, F32) for shape in (shapes if many else [shapes])]
    return pl.pallas_call(
        kernel,
        out_shape=shapes if many else shapes[0],
        in_specs=[SMEM if a.ndim == 1 else VMEM for a in args],
        out_specs=[VMEM] * len(shapes) if many else VMEM,
        compiler_params=pltpu.CompilerParams(vmem_limit_bytes=40 * 2**20),
        name=name,
    )(*args)


def body(mps):
    sites, chi = mps.shape[:2]
    samp = mps.shape[2] // (2 * chi)
    blocks = lax.axis_size("blk")
    band = min(REACH, (blocks - 1) // 2)
    side = lax.axis_index("pair")
    flag = side[None].astype(jnp.int32)

    steps = sites - EDGE + 1
    starts = [0, round(SHARE * steps)]
    counts = [starts[1], steps - starts[1]]
    tile = mps.shape[1:]
    mps, *pieces = call(order_kernel, [(n, *tile) for n in (steps, *counts)], flag, mps, name="order")
    seconds = [move(p, lambda chip, core: (chip - 1, 1) if core == 0 else (chip + 2, 0)) for p in pieces]
    firsts = [move(p, lambda chip, core: (chip - 1, 0) if core == 0 else (chip + 2, 1)) for p in pieces]
    across = lambda chip, core: (chip, 1 - core)
    sibling = move(mps, across)
    inner = call(home_kernel, (64, 128), flag, mps, sibling, name="own_chains")
    spots = jnp.asarray([spot_table(core, samp, band) for core in range(2)], jnp.int32)
    spot = spots[lax.axis_index("blk") % 2, side]
    inner, spot = lax.optimization_barrier((inner, spot))
    carried = (inner,)
    for start, first, second in zip(starts, firsts, seconds):
        second, *carried = lax.optimization_barrier((second, *carried))
        other = move(second, across)
        rows = 288 if start == starts[-1] else 224
        state = call(functools.partial(chain_kernel, start), (rows, 128), flag, mps, sibling, first, second, other,
                     *carried, name="half_chains")
        carried = (carried[0], state)
    partner = lax.ppermute(state, "pair", [(0, 1), (1, 0)])
    tile = call(meet_kernel, (8, 128), state, partner, name="meet")
    tile = call(join_kernel, (8, 128), tile, move(tile, across), name="join")
    tiles = [tile] + [move(tile, lambda chip, core: (chip + gap, core)) for gap in (1, -2)]
    return call(pick_kernel, (1, (2 * band + 1) * samp), spot, *tiles, name="pick")


def solution(mesh):
    in_specs = (P("pair", None, "blk"),)
    out_specs = P(("blk", "pair"), None)
    return jax.shard_map(body, mesh=mesh, in_specs=in_specs, out_specs=out_specs, check_vma=False)
```

```python
import functools

import jax
import jax.numpy as jnp
from jax import lax
from jax.experimental import pallas as pl
from jax.experimental.pallas import tpu as pltpu
from jax.sharding import PartitionSpec as P

REACH = 6
EDGE = 6
SHARE = 0.63
BF16, F32 = jnp.bfloat16, jnp.float32
VMEM = pl.BlockSpec(memory_space=pltpu.VMEM)
SMEM = pl.BlockSpec(memory_space=pltpu.SMEM)


def move(array, source):
    peers = lax.axis_size("blk")
    chips = peers // 2
    pairs = []
    for d in range(peers):
        chip, core = source(d // 2, d % 2)
        pairs.append(((chip % chips) * 2 + core, d))
    return lax.ppermute(array, "blk", pairs)


def split(x):
    high = x.astype(BF16)
    return high, (x - high.astype(F32)).astype(BF16)


def product(left, right):
    return jnp.dot(left, right, preferred_element_type=F32)


def lane_slot(shape):
    return lax.broadcasted_iota(jnp.int32, shape, 1) // 32


def interleave(first, second):
    even = lane_slot(first.shape) % 2 == 0
    return (
        jnp.where(even, first, pltpu.roll(second, 32, 1)),
        jnp.where(even, pltpu.roll(first, 96, 1), second),
    )


def far_weights(tiles, flip):
    if flip:
        tiles = [jnp.concatenate([t] * 4, 0).T for t in tiles]
        blocks = [[t[32 * k : 32 * k + 32] for t in tiles] for k in range(4)]
    else:
        blocks = [tiles] * 4
    slot = lane_slot((32, 128))
    rows = [jnp.concatenate([jnp.where(slot == k, t, 0.0) for t in blocks[k]], 1) for k in range(4)]
    high, low = split(jnp.concatenate(rows, 0))
    return jnp.concatenate([high, high], 0), low


def near_turned(tiles):
    stack = jnp.concatenate([tiles[0], tiles[1], tiles[0], tiles[1]], 0).T
    return [stack[32 * k : 32 * k + 32] for k in (0, 2, 1, 3)]


def near_plain(tile):
    twice = pltpu.roll(tile, 64, 1)
    lower = lane_slot(tile.shape) < 2
    return [jnp.where(lower, tile, twice), jnp.where(lower, twice, tile)]


def spread(state, far):
    double, low = far
    high, rest = split(state)
    inner = product(jnp.concatenate([high, rest], 1), double) + product(high, low)
    return (*split(inner[:, :128]), *split(inner[:, 128:]))


def gather(inner, near):
    h0, l0, h1, l1 = inner
    results = []
    for k, tile in enumerate(near):
        rows = slice(32 * k, 32 * k + 32)
        weights = jnp.concatenate([h0[rows], h1[rows], l0[rows], l1[rows]], 0)
        both = product(jnp.concatenate(split(tile), 0), weights)
        results.append(both[:32] + both[32:])
    return jnp.concatenate(results, 0)


def identities(rows):
    row = lax.broadcasted_iota(jnp.int32, (rows, 128), 0) % 32
    lane = lax.broadcasted_iota(jnp.int32, (rows, 128), 1) % 32
    return jnp.where(row == lane, 1.0, 0.0)


def on_each_side(side_ref, run):
    for side in range(2):
        pl.when(side_ref[0] == side)(functools.partial(run, side == 1))


def turned(tile):
    stack = jnp.concatenate([tile] * 4, 0).T
    slot = lane_slot(tile.shape)
    result = stack[:32]
    for k in range(1, 4):
        result = jnp.where(slot == k, stack[32 * k : 32 * k + 32], result)
    return result


def edge_tile(tiles):
    slot = lane_slot((32, 128))
    row = lax.broadcasted_iota(jnp.int32, (32, 128), 0)
    current = jnp.broadcast_to(tiles[0][:1], (32, 128))
    for k, tile in enumerate(tiles[1:]):
        chosen = jnp.where(slot % 2 == (row >> k) % 2, current, 0.0)
        high, low = split(jnp.concatenate([jnp.where(slot // 2 == n, tile, 0.0) for n in (0, 0, 1, 1)], 0))
        upper, lower = split(chosen)
        current = product(jnp.concatenate([upper, lower], 1), jnp.concatenate([high, high], 0)) + product(upper, low)
    return current


def order_kernel(side_ref, sites_ref, whole, *pieces):
    sites = sites_ref.shape[0]

    def run(flip):
        def tile(k):
            return sites_ref[sites - 1 - k if flip else k]

        edge = edge_tile([turned(tile(k)) if flip else tile(k) for k in range(EDGE)])
        if flip:
            edge = turned(edge)
        at = 0
        for piece in pieces:
            for k in range(piece.shape[0]):
                value = edge if at == 0 else tile(at + EDGE - 1)
                piece[k] = value
                whole[at] = value
                at += 1

    on_each_side(side_ref, run)


def gather_alone(inner, near):
    h0, l0, h1, l1 = inner
    slot = lane_slot(h0.shape)
    zero = jnp.zeros_like(h0)
    high_weights, low_weights = [
        jnp.concatenate([jnp.where(slot == k, half, zero) for k in range(4) for half in halves], 0)
        for halves in ((h0, h1), (l0, l1))
    ]
    lower = lane_slot(near[0].shape) < 2
    tensors = [jnp.where(lower, near[a], near[b]) for a, b in ((0, 2), (1, 3))]
    high, low = split(jnp.concatenate(tensors, 1))
    both = product(jnp.concatenate([high, low], 0), high_weights)
    return both[:32] + both[32:] + product(high, low_weights)


def home_kernel(side_ref, own, sibling, out):
    def run(flip):
        state = identities(64)
        for site in range(own.shape[0]):
            home = interleave(own[site], sibling[site])
            near = near_plain(own[site]) if flip else near_turned(home)[:2]
            state = gather(spread(state, far_weights(home, flip)), near)
        out[...] = state

    on_each_side(side_ref, run)


def chain_kernel(start, side_ref, own, sibling, first, second, other, home, *rest):
    out = rest[-1]
    count = first.shape[0]

    def run(flip):
        state = rest[0][...] if start else identities(224)
        groups = [state[:128], state[128:]]
        for index in range(count):
            whole = start + index
            far = interleave(first[index], second[index])
            if flip:
                near = [n for t in (own[whole], sibling[whole], other[index], first[index], second[index])
                        for n in near_plain(t)]
            else:
                extra = other[index]
                near = (
                    near_turned(interleave(own[whole], sibling[whole]))
                    + near_turned(interleave(extra, extra))[:2]
                    + near_turned(far)
                )
            weights = far_weights(far, flip)
            pairs, rest_pairs = [spread(g, weights) for g in groups]
            pairs = gather(pairs, near[:4])
            others = gather([part[:64] for part in rest_pairs], near[4:6])
            alone = gather_alone([part[64:] for part in rest_pairs], near[6:])
            groups = [pairs, jnp.concatenate([others, alone], 0)]
        last = start + count == own.shape[0]
        out[...] = jnp.concatenate(groups + [home[...]] if last else groups, 0)

    on_each_side(side_ref, run)


def meet_kernel(mine, theirs, out):
    units = jnp.sum((mine[...] * theirs[...]).reshape(-1, 32, 128), 1)
    units = jnp.concatenate([units, jnp.zeros((16 - units.shape[0], 128), F32)], 0)
    row = lax.broadcasted_iota(jnp.int32, (8, 128), 0)
    chosen = jnp.where(row == lane_slot((8, 128)), 1.0, 0.0)
    found = lax.dot_general(
        chosen, units, (((1,), (1,)), ((), ())), precision=lax.Precision.HIGHEST, preferred_element_type=F32
    )
    out[...] = jnp.concatenate([found, jnp.zeros((8, 112), F32)], 1)


def join_kernel(mine, theirs, out):
    out[...] = mine[...] + pltpu.roll(theirs[...], 16, 1)


def pick_kernel(spot_ref, here, after, before, out):
    joined = here[...] + pltpu.roll(after[...], 32, 1) + pltpu.roll(before[...], 64, 1)
    unit = lax.broadcasted_iota(jnp.int32, (128, 128), 0)
    slot = lax.broadcasted_iota(jnp.int32, (8, 128), 0)
    values = []
    for k in range(3):
        spot = spot_ref[pl.ds(k, 1), :]
        chosen = jnp.where(unit == spot // 8, 1.0, 0.0)
        found = jnp.dot(joined, chosen, precision=lax.Precision.HIGHEST, preferred_element_type=F32)
        values.append(jnp.sum(jnp.where(slot == spot % 8, found, 0.0), 0, keepdims=True))
    tile, remote, own = values
    width = out.shape[1]
    out[...] = (tile * tile / (own * remote))[:, :width]


def find(core, near, far):
    mine, theirs = ("A0", "A1"), ("Z1", "Z0")
    if core == 1:
        mine, theirs = theirs, mine
    own, sibling = f"O{core}", f"O{1 - core}"
    if near == far and near in mine:
        return lambda n, m: (6, mine.index(near) + 2 * m)
    for base, rows, lanes in ((0, (own, sibling, theirs[1]), mine), (7, (own,), (own, sibling))):
        if near in rows and far in lanes:
            return lambda n, m: (base + 2 * rows.index(near) + n, lanes.index(far) + 2 * m)
        if far in rows and near in lanes:
            return lambda n, m: (base + 2 * rows.index(far) + m, lanes.index(near) + 2 * n)
    return None


def spot_table(core, samp, band):
    views = [(role, (k, k + 1) if core == 0 else (k + 1, k)) for k, role in ((0, "O"), (2, "A"), (4, "Z"))]
    shift = {"O": 0, "A": -1, "Z": 2}

    def place(offset, alone=False):
        chip, lane = (core + offset) // 2, (core + offset) % 2
        for role, messages in views:
            for name, gap in shift.items():
                if gap - shift[role] == chip:
                    goal = f"{name}{lane}"
                    for k, message in enumerate(messages):
                        got = find(k, goal if alone else f"{role}{core}", goal)
                        if got:
                            return message, got
        raise ValueError(offset)

    def code(where, n, m):
        message, got = where
        unit, slot = got(n, m)
        return 8 * (16 * message + unit) + slot

    offsets = range(-band, band + 1)
    table = []
    for n in range(samp):
        tile = [code(place(o), n, m) for o in offsets for m in range(samp)]
        remote = [code(place(o, True), m, m) for o in offsets for m in range(samp)]
        own = [code(place(0, True), n, n)] * len(tile)
        rows = [r + r[:1] * (128 - len(r)) for r in (tile, remote, own)]
        table.append(rows + rows[:1] * 5)
    return table


def call(kernel, shapes, *args, name):
    many = isinstance(shapes, list)
    shapes = [jax.ShapeDtypeStruct(shape, F32) for shape in (shapes if many else [shapes])]
    return pl.pallas_call(
        kernel,
        out_shape=shapes if many else shapes[0],
        in_specs=[SMEM if a.ndim == 1 else VMEM for a in args],
        out_specs=[VMEM] * len(shapes) if many else VMEM,
        compiler_params=pltpu.CompilerParams(vmem_limit_bytes=40 * 2**20),
        name=name,
    )(*args)


def body(mps):
    sites, chi = mps.shape[:2]
    samp = mps.shape[2] // (2 * chi)
    blocks = lax.axis_size("blk")
    band = min(REACH, (blocks - 1) // 2)
    side = lax.axis_index("pair")
    flag = side[None].astype(jnp.int32)

    steps = sites - EDGE + 1
    starts = [0, round(SHARE * steps)]
    counts = [starts[1], steps - starts[1]]
    tile = mps.shape[1:]
    mps, *pieces = call(order_kernel, [(n, *tile) for n in (steps, *counts)], flag, mps, name="order")
    seconds = [move(p, lambda chip, core: (chip - 1, 1) if core == 0 else (chip + 2, 0)) for p in pieces]
    firsts = [move(p, lambda chip, core: (chip - 1, 0) if core == 0 else (chip + 2, 1)) for p in pieces]
    across = lambda chip, core: (chip, 1 - core)
    sibling = move(mps, across)
    inner = call(home_kernel, (64, 128), flag, mps, sibling, name="own_chains")
    spots = jnp.asarray([spot_table(core, samp, band) for core in range(2)], jnp.int32)
    spot = spots[lax.axis_index("blk") % 2, side]
    carried = (inner,)
    for start, first, second in zip(starts, firsts, seconds):
        second, *carried = lax.optimization_barrier((second, *carried))
        if start:
            spot, state = lax.optimization_barrier((spot, carried[-1]))
            carried = (carried[0], state)
        other = move(second, across)
        rows = 288 if start == starts[-1] else 224
        state = call(functools.partial(chain_kernel, start), (rows, 128), flag, mps, sibling, first, second, other,
                     *carried, name="half_chains")
        carried = (carried[0], state)
    partner = lax.ppermute(state, "pair", [(0, 1), (1, 0)])
    tile = call(meet_kernel, (8, 128), state, partner, name="meet")
    tile = call(join_kernel, (8, 128), tile, move(tile, across), name="join")
    tiles = [tile] + [move(tile, lambda chip, core: (chip + gap, core)) for gap in (1, -2)]
    return call(pick_kernel, (1, (2 * band + 1) * samp), spot, *tiles, name="pick")


def solution(mesh):
    in_specs = (P("pair", None, "blk"),)
    out_specs = P(("blk", "pair"), None)
    return jax.shard_map(body, mesh=mesh, in_specs=in_specs, out_specs=out_specs, check_vma=False)
```
